256 devices in a mesh: blk: 64 (over x, z, y_lo), lat: 4 (over y_hi, core).
Axes of the slice: x: 4, y: 4 (y_hi: 2, y_lo: 2; y = y_hi * 2 + y_lo), z: 8, core: 2. Of those that a mesh axis runs over, the one named last changes fastest.
Arguments:
- displacement: float32 [3, 5, 5, 5, 64, 8, 128], P(None, None, None, None, 'blk', 'lat'), may hold values from -6 to 6
- velocity: float32 [3, 5, 5, 5, 64, 8, 128], P(None, None, None, None, 'blk', 'lat'), may hold values from -6 to 6
- rigidity: float32 [5, 5, 5, 64, 8, 128], P(None, None, None, 'blk', 'lat'), may hold values from 0.5 to 2
- density: float32 [5, 5, 5, 64, 8, 128], P(None, None, None, 'blk', 'lat'), may hold values from 0.5 to 2
- history: float32 [256, 63, 3, 128], P(('blk', 'lat')), may hold values from -0.12 to 0.12
- kernel: float32 [64, 3, 3, 128], replicated, may hold values from -0.4375 to 0.4375
- owner_order: int32 [256], replicated, may hold values from 0 to 255, each once
- rigid_offset: float32 [3], replicated, may hold values from -1.8 to 1.8
- rigid_velocity: float32 [3], replicated, may hold values from -6 to 6
Outputs:
- new_displacement: float32 [3, 5, 5, 5, 64, 8, 128], P(None, None, None, None, 'blk', 'lat')
- new_velocity: float32 [3, 5, 5, 5, 64, 8, 128], P(None, None, None, None, 'blk', 'lat')
- new_history: float32 [256, 63, 3, 128], P(('blk', 'lat'))
- new_offset: float32 [3], replicated
- new_rigid_velocity: float32 [3], replicated
The draws below stay inside these ranges and needn't reach their ends.
Inputs may be any that keep to these rules, and one draw needn't show every extreme that they name: owner_order names every column 0 to 255 once; row j of history belongs to column owner_order[j].
All inputs are finite; a program needn't handle non-finite values.
Results may differ from the reference program's by a relative error of at most 0.0003.
Values sent between devices are 32-bit elements; how exact they have to be, the bound alone decides.
A program may use at most 64 MiB of HBM per device.

```python
import math
import jax
import jax.numpy as jnp
import numpy as np
from jax import lax

L = 128
LAGS = 64
STEPS = 3
EZ = 128
NXE = 64
NYE = 8
COLS = 256


def level_of(key, dims, cuts, smallest, high):
    level, own = 1.0, jax.random.fold_in(key, 6)
    for dim, blocks in cuts:
        draws = jnp.exp(jax.random.uniform(jax.random.fold_in(own, dim), (blocks,), jnp.float32, smallest / len(cuts), high / len(cuts)))
        level = level * jnp.repeat(draws, dims[dim] // blocks).reshape([-1 if axis == dim else 1 for axis in range(len(dims))])
    return level


def normal_values(key, dims, width, most, cuts=(), kind=jnp.bfloat16):
    entries = jax.random.normal(key, dims, jnp.float32) * width
    if len(cuts) > 0:
        entries = level_of(key, dims, cuts, -0.22, 0.18) * entries
    return jnp.clip(entries, min=-most, max=most).astype(kind)


def setup_inputs(seed: int = 0) -> dict:
    key_of = jax.random.split(jax.random.key(seed), 10)
    displacement = normal_values(key_of[0], (3, 5, 5, 5, NXE, NYE, EZ), 1.0, 6.0, ((4, 64), (5, 4)), jnp.float32)
    velocity = normal_values(key_of[1], (3, 5, 5, 5, NXE, NYE, EZ), 1.0, 6.0, ((4, 64), (5, 4)), jnp.float32)
    rigidity = jnp.clip(jnp.exp(math.log(2.0) - 1.3862944 * jax.random.uniform(key_of[2], (5, 5, 5, NXE, NYE, EZ), jnp.float32) ** level_of(key_of[2], (5, 5, 5, NXE, NYE, EZ), ((3, 64), (4, 4)), -0.2, 0.2)), 0.5, 2.0)
    density = jnp.clip(jnp.exp(math.log(2.0) - 1.3862944 * jax.random.uniform(key_of[3], (5, 5, 5, NXE, NYE, EZ), jnp.float32) ** level_of(key_of[3], (5, 5, 5, NXE, NYE, EZ), ((3, 64), (4, 4)), -0.2, 0.2)), 0.5, 2.0)
    history = normal_values(key_of[4], (COLS, LAGS - 1, 3, L), 0.02, 0.12, ((0, 256),), jnp.float32)
    kernel = normal_values(key_of[5], (LAGS, 3, 3, L), (3 * LAGS) ** -0.5, 0.4375, (), jnp.float32)
    owner_order = jax.random.permutation(key_of[6], COLS).astype(jnp.int32)
    rigid_offset = normal_values(key_of[7], (3,), 0.3, 1.8, (), jnp.float32)
    rigid_velocity = normal_values(key_of[8], (3,), 1.0, 6.0, (), jnp.float32)
    return {"displacement": displacement, "velocity": velocity, "rigidity": rigidity, "density": density, "history": history, "kernel": kernel, "owner_order": owner_order, "rigid_offset": rigid_offset, "rigid_velocity": rigid_velocity}


pole_gap = 0.1
time_step = 0.03
rigid_gain = 20.0
coupling = 1.0
highest = lax.Precision.HIGHEST

def node_tables():
    points = np.array([-1.0, -math.sqrt(3.0 / 7.0), 0.0, math.sqrt(3.0 / 7.0), 1.0])
    weights = np.array([0.1, 49.0 / 90.0, 32.0 / 45.0, 49.0 / 90.0, 0.1])
    products = np.array([np.prod([points[row_at] - points[others] for others in range(5) if others != row_at]) for row_at in range(5)])
    slopes = np.zeros((5, 5))
    for row_at in range(5):
        for col_at in range(5):
            if row_at == col_at:
                slopes[row_at, col_at] = sum((1.0 / (points[row_at] - points[others]) for others in range(5) if others != row_at))
            else:
                slopes[row_at, col_at] = products[row_at] / products[col_at] / (points[row_at] - points[col_at])
    return (points, weights, slopes)

def node_volume():
    points, weights, slopes = node_tables()
    node_weight = jnp.asarray(weights, dtype=jnp.float32)
    volume = node_weight[:, None, None] * node_weight[None, :, None] * node_weight[None, None, :]
    return volume[:, :, :, None, None, None]

def stiffness(values, rigidity):
    points, weights, slopes = node_tables()
    deriv = jnp.asarray(slopes, dtype=jnp.float32)
    scaled = (node_volume() * rigidity)[None]
    first_dir = jnp.einsum('ia,kabcxyz->kibcxyz', deriv, values, precision=highest) * scaled
    second_dir = jnp.einsum('jb,kabcxyz->kajcxyz', deriv, values, precision=highest) * scaled
    third_dir = jnp.einsum('lc,kabcxyz->kablxyz', deriv, values, precision=highest) * scaled
    result = jnp.einsum('ia,kibcxyz->kabcxyz', deriv, first_dir, precision=highest)
    result = result + jnp.einsum('jb,kajcxyz->kabcxyz', deriv, second_dir, precision=highest)
    return result + jnp.einsum('lc,kablxyz->kabcxyz', deriv, third_dir, precision=highest)

def join_faces(lower, upper, before_first, after_last, axis):
    count = lower.shape[axis]
    earlier = jnp.concatenate((before_first, lax.slice_in_dim(upper, 0, count - 1, axis=axis)), axis=axis)
    later = jnp.concatenate((lax.slice_in_dim(lower, 1, count, axis=axis), after_last), axis=axis)
    return (lower + earlier, upper + later)

def assemble_whole(forces):
    lower, upper = (forces[:, 0], forces[:, 4])
    count = lower.shape[3]
    lower, upper = join_faces(lower, upper, lax.slice_in_dim(upper, count - 1, count, axis=3), lax.slice_in_dim(lower, 0, 1, axis=3), 3)
    forces = forces.at[:, 0].set(lower).at[:, 4].set(upper)
    lower, upper = (forces[:, :, 0], forces[:, :, 4])
    empty = jnp.zeros_like(lax.slice_in_dim(lower, 0, 1, axis=4))
    lower, upper = join_faces(lower, upper, empty, empty, 4)
    forces = forces.at[:, :, 0].set(lower).at[:, :, 4].set(upper)
    lower, upper = (forces[:, :, :, 0], forces[:, :, :, 4])
    empty = jnp.zeros_like(lax.slice_in_dim(lower, 0, 1, axis=5))
    lower, upper = join_faces(lower, upper, empty, empty, 5)
    return forces.at[:, :, :, 0].set(lower).at[:, :, :, 4].set(upper)

def interface_grid(row_first, row_count, col_first, col_count, lat_elems, lon_elems):
    points, weights, slopes = node_tables()
    nodes = jnp.asarray(points, dtype=jnp.float32)
    node_weight = jnp.asarray(weights, dtype=jnp.float32)
    theta_step = (math.pi - 2.0 * pole_gap) / lat_elems
    phi_step = 2.0 * math.pi / lon_elems
    row_elem = (row_first + jnp.arange(5 * row_count, dtype=jnp.int32) // 5).astype(jnp.float32)
    col_elem = (col_first + jnp.arange(5 * col_count, dtype=jnp.int32) // 5).astype(jnp.float32)
    colatitude = pole_gap + (row_elem + 0.5 * (1.0 + jnp.tile(nodes, row_count))) * theta_step
    longitude = (col_elem + 0.5 * (1.0 + jnp.tile(nodes, col_count))) * phi_step
    row_weight = jnp.tile(node_weight, row_count)
    col_weight = jnp.tile(node_weight, col_count)
    area_weight = 0.25 * theta_step * phi_step * (row_weight * jnp.sin(colatitude))[:, None] * col_weight[None, :]
    face_weight = row_weight[:, None] * col_weight[None, :]
    return (colatitude, longitude, area_weight, face_weight)

def rotation(colatitude, longitude):
    sin_theta = jnp.sin(colatitude)[:, None]
    cos_theta = jnp.cos(colatitude)[:, None]
    sin_phi = jnp.sin(longitude)[None, :]
    cos_phi = jnp.cos(longitude)[None, :]
    filled = jnp.ones((colatitude.shape[0], longitude.shape[0]), jnp.float32)
    radial = (sin_theta * cos_phi, sin_theta * sin_phi, cos_theta * filled)
    polar_dir = (cos_theta * cos_phi, cos_theta * sin_phi, -sin_theta * filled)
    azimuth = (-sin_phi * filled, cos_phi * filled, 0.0 * filled)
    return jnp.stack([jnp.stack([radial[axis_at], polar_dir[axis_at], azimuth[axis_at]]) for axis_at in range(3)])

def legendre(colatitude, degrees):
    cosine = jnp.cos(colatitude)[:, None]
    sine = jnp.sin(colatitude)[:, None]
    orders = jnp.arange(degrees, dtype=jnp.float32)[None, :]
    factor = jnp.where(orders == 0, math.sqrt(0.5), -jnp.sqrt((2.0 * orders + 1.0) / jnp.maximum(2.0 * orders, 1.0)) * sine)
    diagonal = jnp.cumprod(factor, axis=1)

    def advance(state_pair, degree):
        previous, before = state_pair
        level = degree.astype(jnp.float32)
        upward = jnp.sqrt(jnp.maximum(4.0 * level * level - 1.0, 0.0) / jnp.maximum(level * level - orders * orders, 1.0))
        lowered = (level - 1.0) * (level - 1.0)
        downward = jnp.sqrt(jnp.maximum(lowered - orders * orders, 0.0) / jnp.maximum(4.0 * lowered - 1.0, 1.0))
        recurred = upward * (cosine * previous - downward * before)
        values = jnp.where(orders == level, diagonal, jnp.where(orders + 1.0 == level, jnp.sqrt(2.0 * orders + 3.0) * cosine * diagonal, jnp.where(orders + 1.0 < level, recurred, 0.0)))
        return ((values, previous), values)
    zeroed = jnp.zeros((colatitude.shape[0], degrees), jnp.float32)
    finals, levels = lax.scan(advance, (zeroed, zeroed), jnp.arange(degrees, dtype=jnp.int32))
    return levels

def doubled(colatitude, degrees):
    levels = legendre(colatitude, degrees)
    return jnp.concatenate((levels, levels), axis=2)

def circle_table(longitude, degrees):
    orders = jnp.arange(degrees, dtype=jnp.float32)[None, :]
    angles = longitude[:, None] * orders
    cosines = jnp.where(orders == 0, 1.0 / math.sqrt(2.0 * math.pi), jnp.cos(angles) / math.sqrt(math.pi))
    sines = jnp.where(orders == 0, 0.0, jnp.sin(angles) / math.sqrt(math.pi))
    return jnp.concatenate((cosines, sines), axis=1)

def project(relative, area_weight, circle, levels):
    fourier = jnp.einsum('ktf,fc->ktc', relative * area_weight, circle, precision=highest)
    return jnp.einsum('ktc,ltc->ckl', fourier, levels, precision=highest)

def synthesize(coeffs, circle, levels):
    partial_value = jnp.einsum('ckl,ltc->ktc', coeffs, levels, precision=highest)
    return jnp.einsum('ktc,fc->ktf', partial_value, circle, precision=highest)

def respond(owned_rows, history, kernel):
    stacked = jnp.concatenate((owned_rows[:, None], history), axis=1)
    replies = jnp.einsum('jabl,cjbl->cal', kernel, stacked, precision=highest)
    return (replies, stacked[:, :-1])

def to_grid(values):
    bottom = values[:, :, :, 0, :, :, 0]
    lon_count, lat_count = (bottom.shape[3], bottom.shape[4])
    return bottom.transpose(0, 4, 2, 3, 1).reshape(3, 5 * lat_count, 5 * lon_count)

def from_grid(grid, lon_count, lat_count):
    return grid.reshape(3, lat_count, 5, lon_count, 5).transpose(0, 4, 2, 3, 1)

def reference(displacement, velocity, rigidity, density, history, kernel, owner_order, rigid_offset, rigid_velocity):
    lon_elems, lat_elems = (displacement.shape[4], displacement.shape[5])
    degrees = kernel.shape[3]
    colatitude, longitude, area_weight, face_weight = interface_grid(0, lat_elems, 0, lon_elems, lat_elems, lon_elems)
    rotated = rotation(colatitude, longitude)
    levels = doubled(colatitude, degrees)
    circle = circle_table(longitude, degrees)
    inverse = 1.0 / assemble_whole((density * node_volume())[None])
    for step_index in range(STEPS):
        relative = to_grid(displacement) - jnp.einsum('jktf,j->ktf', rotated, rigid_offset, precision=highest)
        partial_value = project(relative, area_weight, circle, levels)
        ordered = jnp.take(partial_value, owner_order, axis=0)
        replies, history = respond(ordered, history, kernel)
        coeffs = jnp.zeros_like(replies).at[owner_order].set(replies)
        traction = synthesize(coeffs, circle, levels)
        pull_sum = jnp.einsum('jktf,ktf->j', rotated * area_weight, traction, precision=highest)
        rigid_velocity = rigid_velocity + time_step * rigid_gain * pull_sum
        rigid_offset = rigid_offset + time_step * rigid_velocity
        forces = -stiffness(displacement, rigidity)
        forces = forces.at[:, :, :, 0, :, :, 0].add(from_grid(-coupling * face_weight * traction, lon_elems, lat_elems))
        velocity = velocity + time_step * assemble_whole(forces) * inverse
        displacement = displacement + time_step * velocity
    return (displacement, velocity, history, rigid_offset, rigid_velocity)
```

```python
import functools
import math

import jax
import jax.numpy as jnp
import numpy as np
from jax import lax
from jax.experimental import pallas as pl
from jax.experimental.pallas import tpu as pltpu
from jax.sharding import Mesh
from jax.sharding import PartitionSpec as P

STEPS = 3
AXES = ("x", "z", "ylo", "yhi", "core")
SIZES = {"x": 4, "z": 8, "ylo": 2, "yhi": 2, "core": 2}
BLK = ("x", "z", "ylo")
LAT = ("yhi", "core")
MESH_ID = pl.DeviceIdType.MESH
FIRST = ("core", "z")
SECOND = ("x", "ylo", "yhi")
GROUP = 16

pole_gap = 0.1
time_step = 0.03
rigid_gain = 20.0
coupling = 1.0


def node_tables():
    points = np.array([-1.0, -math.sqrt(3.0 / 7.0), 0.0, math.sqrt(3.0 / 7.0), 1.0])
    weights = np.array([0.1, 49.0 / 90.0, 32.0 / 45.0, 49.0 / 90.0, 0.1])
    products = np.array(
        [np.prod([points[i] - points[j] for j in range(5) if j != i]) for i in range(5)]
    )
    slopes = np.zeros((5, 5))
    for i in range(5):
        for j in range(5):
            if i == j:
                slopes[i, j] = sum(1.0 / (points[i] - points[o]) for o in range(5) if o != i)
            else:
                slopes[i, j] = products[i] / products[j] / (points[i] - points[j])
    return points, weights, slopes


POINTS, WEIGHTS, SLOPES = node_tables()
THETA_STEP = (math.pi - 2.0 * pole_gap) / 8
PHI_STEP = 2.0 * math.pi / 64
THETA = pole_gap + (np.arange(8)[:, None] + 0.5 * (1.0 + POINTS)) * THETA_STEP
PHI = (np.arange(64)[:, None] + 0.5 * (1.0 + POINTS)) * PHI_STEP


def legendre_table():
    cosine, sine = np.cos(THETA).reshape(-1), np.sin(THETA).reshape(-1)
    table = np.zeros((128, 128, 40))
    diagonal = np.full(40, math.sqrt(0.5))
    for m in range(128):
        if m > 0:
            diagonal = diagonal * -math.sqrt((2 * m + 1) / (2 * m)) * sine
        table[m, m] = diagonal
        if m + 1 < 128:
            table[m, m + 1] = math.sqrt(2 * m + 3) * cosine * diagonal
        for l in range(m + 2, 128):
            up = math.sqrt((4.0 * l * l - 1) / (l * l - m * m))
            low = math.sqrt(((l - 1.0) ** 2 - m * m) / (4.0 * (l - 1.0) ** 2 - 1))
            table[m, l] = up * (cosine * table[m, l - 1] - low * table[m, l - 2])
    padded = np.zeros((128, 8, 8, 128), np.float32)
    padded[:, :, :5] = table.transpose(0, 2, 1).reshape(128, 8, 5, 128)
    return padded.reshape(128, 64, 128)


def circle_values():
    m = np.arange(128)
    angle = m[:, None, None] * PHI[None]
    cosines = np.cos(angle) / math.sqrt(math.pi)
    cosines[0] = 1.0 / math.sqrt(2.0 * math.pi)
    sines = np.sin(angle) / math.sqrt(math.pi)
    sines[0] = 0.0
    return np.concatenate((cosines, sines))


def rotations():
    st, ct = np.sin(THETA)[:, :, None, None], np.cos(THETA)[:, :, None, None]
    sp, cp = np.sin(PHI)[None, None], np.cos(PHI)[None, None]
    one, zero = np.ones((8, 5, 64, 5)), np.zeros((8, 5, 64, 5))
    return np.stack(
        [
            np.stack([st * cp, ct * cp, -sp * one]),
            np.stack([st * sp, ct * sp, cp * one]),
            np.stack([ct * one, -st * one, zero]),
        ]
    )


def areas():
    scale = 0.25 * THETA_STEP * PHI_STEP
    return scale * (WEIGHTS * np.sin(THETA))[:, :, None] * WEIGHTS


def pull_table():
    weighted = np.einsum("yba,jkybea,cea->cjkyb", areas(), rotations(), circle_values())
    table = np.zeros((256, 8, 4, 32))
    for k in range(3):
        for lat in range(4):
            for ey in range(2):
                at = (2 * k + ey) * 5
                table[:, :3, lat, at : at + 5] = weighted[:, :, k, 2 * lat + ey]
    return table.reshape(256, 8, 128).astype(np.float32)


def packed_tables():
    theta_part = np.zeros((4, 3, 8, 128))
    phi_part = np.zeros((64, 2, 8, 128))
    area = areas()
    for r in range(6):
        k, ey = r // 2, r % 2
        for a in range(5):
            for b in range(5):
                lane = 32 * (r % 4) + 5 * a + b
                for lat in range(4):
                    theta = THETA[2 * lat + ey, b]
                    weight = area[2 * lat + ey, b, a]
                    theta_part[lat, 0, r, lane] = weight
                    theta_part[lat, 1, r, lane] = weight * (math.sin(theta), math.cos(theta), 1.0)[k]
                    theta_part[lat, 2, r, lane] = weight * (math.cos(theta), -math.sin(theta), 0.0)[k]
                cp, sp = np.cos(PHI[:, a]), np.sin(PHI[:, a])
                phi_part[:, 0, r, lane] = (cp, cp, -sp)[k]
                phi_part[:, 1, r, lane] = (sp, sp, cp)[k]
    return theta_part.astype(np.float32), phi_part.astype(np.float32)


def circle_at(column, elem, node_shift):
    order = column % 128
    turns = ((order * elem) % 64).astype(jnp.float32) * PHI_STEP
    angle = turns + order.astype(jnp.float32) * node_shift
    cosine = jnp.where(order == 0, 1.0 / math.sqrt(2.0 * math.pi), jnp.cos(angle) / math.sqrt(math.pi))
    sine = jnp.where(order == 0, 0.0, jnp.sin(angle) / math.sqrt(math.pi))
    return jnp.where(column < 128, cosine, sine)


def flat(axes, index):
    at = 0
    for axis in axes:
        at = at * SIZES[axis] + index[axis]
    return at


def unflat(axes, at):
    index = {}
    for axis in reversed(axes):
        index[axis] = at % SIZES[axis]
        at = at // SIZES[axis]
    return index


def partners(axes, me, shifts):
    count = math.prod(SIZES[axis] for axis in axes)
    mine = flat(axes, me)
    found = []
    for shift in shifts:
        other = {**me, **unflat(axes, lax.rem(mine + (shift + count), count))}
        found.append(tuple(other[axis] for axis in AXES))
    return found


def on_sphere(
    u_in, v_in, wr, hist, kern, leg, pull_tab, gt, gs, theta_part, phi_part, x_in, xv_in,
    u, v, hist_out, rigid_out,
    force, inv, gsb, past, coefs, g1, g2, lon_lo, lon_hi, lat_lo, lat_hi,
    send1, recv1, send2, recv2, send_h, recv_h,
):
    me = {axis: lax.axis_index(axis) for axis in AXES}
    lat = flat(LAT, me)
    elem = flat(BLK, me)
    near = partners(FIRST, me, range(1, GROUP))
    far = partners(SECOND, me, range(1, GROUP))
    lon_next, lon_prev = partners(BLK, me, (1, -1))
    lat_next, lat_prev = partners(LAT, me, (1, -1))
    everyone = near + far + [lon_next, lon_prev, lat_next, lat_prev]
    barrier = pltpu.get_barrier_semaphore()
    for other in everyone:
        pl.semaphore_signal(barrier, inc=1, device_id=other, device_id_type=MESH_ID)
    pl.semaphore_wait(barrier, len(everyone))

    lanes = lax.broadcasted_iota(jnp.int32, (8, 128), 1)
    subs = lax.broadcasted_iota(jnp.int32, (8, 128), 0)
    lane_row = lax.broadcasted_iota(jnp.int32, (1, 128), 1)
    even = subs % 2 == 0
    in_field = subs < 6
    slot_near = flat(FIRST, me)
    slot_far = flat(SECOND, me)

    def send(src, dst, ssem, rsem, other):
        copy = pltpu.make_async_remote_copy(
            src_ref=src, dst_ref=dst, send_sem=ssem, recv_sem=rsem,
            device_id=other, device_id_type=MESH_ID,
        )
        copy.start()
        return copy

    def spread(buf, rows, ssem, rsem, step, stage):
        if stage == 0:
            start, count, others = (slot_far * GROUP + slot_near) * rows, rows, near
        else:
            start, count, others = slot_far * GROUP * rows, GROUP * rows, far
        block = buf.at[step, pl.ds(start, count), :]
        return [
            send(block, block, ssem.at[step, stage, d], rsem.at[step, stage, d], other)
            for d, other in enumerate(others)
        ]

    def arrived(copies):
        for copy in copies:
            copy.wait_recv()

    def left(copies):
        for copy in copies:
            copy.wait_send()

    def along(stride, base_of, first):
        def line(i, carry):
            base = base_of(i)
            values = [u[base + q * stride] for q in range(5)]
            weights = [wr[base + q * stride] for q in range(5)]
            grads = []
            for p in range(5):
                total = float(SLOPES[p, 0]) * values[0]
                for q in range(1, 5):
                    total = total + float(SLOPES[p, q]) * values[q]
                grads.append(total * weights[p])
            for q in range(5):
                total = float(SLOPES[0, q]) * grads[0]
                for p in range(1, 5):
                    total = total + float(SLOPES[p, q]) * grads[p]
                at = base + q * stride
                if first:
                    force[at] = jnp.where(in_field, -total, weights[q])
                else:
                    force[at] = force[at] - total
            return carry

        lax.fori_loop(0, 25, line, 0)

    u[...] = u_in[...]
    v[...] = v_in[...]
    coefs[...] = jnp.zeros_like(coefs)

    def prepare():
        for a in range(5):
            gsb[a] = jnp.broadcast_to(gs[:, a : a + 1], (256, 128))
        for step in range(STEPS):
            old = hist[0 : 63 - step]
            for k in range(3):
                rows = jnp.sum(kern[step + 1 : 64, k] * old, axis=0)
                past[step, k : k + 1] = jnp.sum(rows, axis=0, keepdims=True)
        hist_out[3:63] = hist[0:60]

    area = theta_part[lat, 0]
    rig_x = theta_part[lat, 1] * phi_part[elem, 0]
    rig_y = theta_part[lat, 1] * phi_part[elem, 1]
    rig_z = theta_part[lat, 2]

    def one_step(step, state):
        offset, speed = state
        packed = jnp.zeros((8, 128), jnp.float32)
        for i in range(25):
            first_lane = jnp.broadcast_to(u[i * 5][:, 0:1], (8, 128))
            packed = jnp.where(lanes == (subs % 4) * 32 + i, first_lane, packed)
        packed = packed * area - (offset[0] * rig_x + offset[1] * rig_y + offset[2] * rig_z)
        row0 = jnp.sum(packed[0:4], axis=0, keepdims=True)
        row1 = jnp.sum(packed[4:8], axis=0, keepdims=True)
        mine = slot_far * GROUP + slot_near
        g1[step, pl.ds(2 * mine, 2), :] = jnp.concatenate((row0, row1), axis=0)
        copies1 = spread(g1, 2, send1, recv1, step, 0)

        along(25, lambda i: i, True)
        along(5, lambda i: (i // 5) * 25 + i % 5, False)
        along(1, lambda i: i * 5, False)
        for i in range(25):
            low, high = force[i * 5], force[i * 5 + 4]
            force[i * 5] = low + jnp.where(lanes == 0, 0.0, pltpu.roll(high, 1, 1))
            force[i * 5 + 4] = high + jnp.where(lanes == 127, 0.0, pltpu.roll(low, 127, 1))
        up = send(force.at[pl.ds(100, 25)], lon_lo.at[step], send_h.at[step, 0], recv_h.at[step, 0], lon_next)
        down = send(force.at[pl.ds(0, 25)], lon_hi.at[step], send_h.at[step, 1], recv_h.at[step, 1], lon_prev)

        @pl.when(step == 0)
        def _():
            prepare()

        arrived(copies1)
        copies2 = spread(g1, 2, send1, recv1, step, 1)

        up.wait()
        down.wait()
        force[0:25] = force[0:25] + lon_lo[step]
        force[100:125] = force[100:125] + lon_hi[step]
        lat_send = []
        for a in range(5):
            lat_send.append(
                send(force.at[pl.ds(a * 25 + 20, 5)], lat_lo.at[step, pl.ds(a * 5, 5)],
                     send_h.at[step, 2 + a], recv_h.at[step, 2 + a], lat_next)
            )
            lat_send.append(
                send(force.at[pl.ds(a * 25, 5)], lat_hi.at[step, pl.ds(a * 5, 5)],
                     send_h.at[step, 7 + a], recv_h.at[step, 7 + a], lat_prev)
            )

        arrived(copies2)
        field = g1[step].reshape(8, 4, 16, 128)
        summed = jnp.sum(field * gt[...].reshape(8, 1, 16, 128), axis=0)
        summed = summed[:, 0:8] + summed[:, 8:16]
        summed = (summed[:, 0:2] + summed[:, 2:4]) + (summed[:, 4:6] + summed[:, 6:8])
        parts = [jnp.zeros((8, 128), jnp.float32) for k in range(3)]
        for at in range(4):
            for ey in range(2):
                block = leg[(2 * at + ey) * 8 : (2 * at + ey) * 8 + 8]
                for k in range(3):
                    r = 2 * k + ey
                    row = summed[at, r // 4 : r // 4 + 1]
                    local = lanes - 32 * (r % 4)
                    keep = (local >= 0) & (local < 25) & (local % 5 == subs)
                    column = jnp.sum(jnp.where(keep, row, 0.0), axis=1, keepdims=True)
                    parts[k] = parts[k] + column * block
        coef = jnp.concatenate([jnp.sum(part, axis=0, keepdims=True) for part in parts], axis=0)
        coefs[step + 2] = coef
        reply = past[step]
        for k in range(3):
            total = jnp.sum(kern[0, k] * coef, axis=0, keepdims=True)
            for back in (1, 2):
                total = total + jnp.sum(kern[back, k] * coefs[step + 2 - back], axis=0, keepdims=True)
            rep = past[step, k : k + 1] + total
            parts[k] = rep
        message = jnp.zeros((8, 128), jnp.float32)
        for at in range(4):
            for ey in range(2):
                block = leg[(2 * at + ey) * 8 : (2 * at + ey) * 8 + 8]
                for k in range(3):
                    column = jnp.sum(block * parts[k], axis=1, keepdims=True)
                    put = (lanes == 32 * at + (2 * k + ey) * 5 + subs) & (subs < 5)
                    message = jnp.where(put, column, message)
        message = jnp.sum(message, axis=0, keepdims=True)
        pulls = jnp.sum(pull_tab[...] * message, axis=1, keepdims=True)
        for j, lane in enumerate((30, 31, 62)):
            message = message + jnp.where(lane_row == lane, pulls[j : j + 1], 0.0)
        g2[step, pl.ds(mine, 1), :] = message
        copies3 = spread(g2, 1, send2, recv2, step, 0)

        for copy in lat_send:
            copy.wait()
        from_below = jnp.where((subs == 0) & (lat == 0), 0.0, 1.0)
        for a in range(5):
            for c in range(5):
                low, high = force[a * 25 + c], force[a * 25 + 20 + c]
                below, above = lat_lo[step, a * 5 + c], lat_hi[step, a * 5 + c]
                below = jnp.where(lat == 0, 0.0, pltpu.roll(below, 7, 0))
                above = jnp.where(lat == 3, 0.0, pltpu.roll(above, 1, 0))
                force[a * 25 + c] = low + jnp.where(even, below, pltpu.roll(high, 1, 0))
                force[a * 25 + 20 + c] = high + jnp.where(even, pltpu.roll(low, 7, 0), above)

        def advance(i, carry):
            total = force[i]
            inverse = 1.0 / jnp.where(even, total[6:7], total[7:8])
            inv[i] = inverse
            speed_now = v[i] + time_step * (total * inverse)
            speed_now = jnp.where(in_field, speed_now, 0.0)
            v[i] = speed_now
            u[i] = u[i] + time_step * speed_now
            return carry

        lax.fori_loop(0, 125, advance, 0)

        arrived(copies3)
        copies4 = spread(g2, 1, send2, recv2, step, 1)
        left(copies1)
        left(copies2)
        arrived(copies4)

        field = g2[step]
        whole = jnp.sum(field, axis=0, keepdims=True)
        new_offset, new_speed = [], []
        for j, lane in enumerate((30, 31, 62)):
            pull = jnp.sum(jnp.where(lane_row == lane, whole, 0.0), axis=1, keepdims=True)
            new_speed.append(speed[j] + time_step * rigid_gain * pull)
            new_offset.append(offset[j] + time_step * new_speed[j])
        edge = lanes == 0
        for a in range(5):
            row = jnp.sum(field * gsb[a], axis=0, keepdims=True)
            along_lon = float(WEIGHTS[a] * (2.0 if a in (0, 4) else 1.0))
            for b in range(5):
                local = lanes - 32 * lat
                here = (local == subs * 5 + b) & in_field
                traction = jnp.sum(jnp.where(here, row, 0.0), axis=1, keepdims=True)
                face = float(coupling * WEIGHTS[b]) * along_lon
                if b == 0:
                    face = face * jnp.where(even & (lat == 0), 1.0, 2.0)
                if b == 4:
                    face = face * jnp.where((~even) & (lat == 3), 1.0, 2.0)
                i = (a * 5 + b) * 5
                gain = jnp.where(edge, time_step * (traction * face) * inv[i], 0.0)
                v[i] = v[i] - gain
                u[i] = u[i] - time_step * gain
        left(copies3)
        left(copies4)
        return tuple(new_offset), tuple(new_speed)

    start = (
        tuple(jnp.full((1, 1), x_in[j], jnp.float32) for j in range(3)),
        tuple(jnp.full((1, 1), xv_in[j], jnp.float32) for j in range(3)),
    )
    offset, speed = lax.fori_loop(0, STEPS, one_step, start)
    for step in range(STEPS):
        hist_out[step] = coefs[STEPS + 1 - step]
    for j in range(3):
        rigid_out[j : j + 1] = jnp.broadcast_to(offset[j], (1, 128))
        rigid_out[3 + j : 4 + j] = jnp.broadcast_to(speed[j], (1, 128))


def to_rows(field):
    return field.transpose(1, 2, 3, 0, 4, 5, 6).reshape(125, -1, 128)


def from_rows(rows):
    return rows[:, :6].reshape(5, 5, 5, 3, 1, 2, 128).transpose(3, 0, 1, 2, 4, 5, 6)


def on_device(
    displacement, velocity, rigidity, density, history, kernel, owner_order, rigid_offset, rigid_velocity
):
    elem = lax.axis_index(BLK)
    column = lax.dynamic_index_in_dim(owner_order, lax.axis_index(AXES), 0, keepdims=False)
    legendre = lax.dynamic_index_in_dim(jnp.asarray(legendre_table()), column % 128, 0, keepdims=False)
    pull_tab = lax.dynamic_index_in_dim(jnp.asarray(pull_table()), column, 0, keepdims=False)
    shift = jnp.asarray(0.5 * (1.0 + POINTS) * PHI_STEP, dtype=jnp.float32)
    row = np.arange(128)
    x, ylo, z = row // 32, row // 16 % 2, row // 2 % 8
    lane = np.arange(128) % 32
    lane_shift = 0.5 * (1.0 + POINTS[np.minimum(lane // 5, 4)]) * PHI_STEP
    row_elem = jnp.asarray(((x * 8 + z) * 2 + ylo)[:, None], dtype=jnp.int32)
    own_circle = circle_at(column, row_elem, jnp.asarray(lane_shift[None], dtype=jnp.float32))
    own_circle = jnp.where(jnp.asarray(lane[None] < 25), own_circle, 0.0)
    slots = owner_order.reshape(4, 8, 2, 2, 2).transpose(0, 2, 3, 4, 1).reshape(256, 1)
    lane_circle = circle_at(slots, elem, jnp.pad(shift, (0, 3))[None])
    theta_part, phi_part = packed_tables()

    u8 = jnp.pad(to_rows(displacement), ((0, 0), (0, 2), (0, 0)))
    v8 = jnp.pad(to_rows(velocity), ((0, 0), (0, 2), (0, 0)))
    volume = (WEIGHTS[:, None, None] * WEIGHTS[:, None] * WEIGHTS).reshape(125, 1, 1).astype(np.float32)
    rig2, den2 = rigidity.reshape(125, 2, 128), density.reshape(125, 2, 128)
    wr = jnp.concatenate((rig2, rig2, rig2, den2), axis=1) * volume

    vmem = pl.BlockSpec(memory_space=pltpu.VMEM)
    smem = pl.BlockSpec(memory_space=pltpu.SMEM)
    sds = functools.partial(jax.ShapeDtypeStruct, dtype=jnp.float32)
    new_u, new_v, new_history, rigid = pl.pallas_call(
        on_sphere,
        out_shape=(sds((125, 8, 128)), sds((125, 8, 128)), sds((63, 3, 128)), sds((8, 128))),
        in_specs=[vmem] * 11 + [smem] * 2,
        out_specs=(vmem,) * 4,
        scratch_shapes=[
            pltpu.VMEM((125, 8, 128), jnp.float32),
            pltpu.VMEM((125, 8, 128), jnp.float32),
            pltpu.VMEM((5, 256, 128), jnp.float32),
            pltpu.VMEM((STEPS, 8, 128), jnp.float32),
            pltpu.VMEM((STEPS + 2, 3, 128), jnp.float32),
            pltpu.VMEM((STEPS, 512, 128), jnp.float32),
            pltpu.VMEM((STEPS, 256, 128), jnp.float32),
            pltpu.VMEM((STEPS, 25, 8, 128), jnp.float32),
            pltpu.VMEM((STEPS, 25, 8, 128), jnp.float32),
            pltpu.VMEM((STEPS, 25, 8, 128), jnp.float32),
            pltpu.VMEM((STEPS, 25, 8, 128), jnp.float32),
            pltpu.SemaphoreType.DMA((STEPS, 2, GROUP - 1)),
            pltpu.SemaphoreType.DMA((STEPS, 2, GROUP - 1)),
            pltpu.SemaphoreType.DMA((STEPS, 2, GROUP - 1)),
            pltpu.SemaphoreType.DMA((STEPS, 2, GROUP - 1)),
            pltpu.SemaphoreType.DMA((STEPS, 12)),
            pltpu.SemaphoreType.DMA((STEPS, 12)),
        ],
        compiler_params=pltpu.CompilerParams(
            collective_id=0, has_side_effects=True, vmem_limit_bytes=40 * 1024 * 1024
        ),
    )(
        u8, v8, wr, history[0], kernel, legendre, pull_tab, own_circle, lane_circle,
        jnp.asarray(theta_part), jnp.asarray(phi_part), rigid_offset, rigid_velocity,
    )
    return from_rows(new_u), from_rows(new_v), new_history[None], rigid[0:3, 0], rigid[3:6, 0]


def solution(mesh):
    split = Mesh(mesh.devices.reshape(4, 8, 2, 2, 2), AXES)
    field = P(None, None, None, None, BLK, LAT, None)
    scalar_field = P(None, None, None, BLK, LAT, None)
    owned = P(AXES, None, None, None)
    return jax.shard_map(
        on_device,
        mesh=split,
        in_specs=(field, field, scalar_field, scalar_field, owned, P(), P(), P(), P()),
        out_specs=(field, field, owned, P(), P()),
        check_vma=False,
    )
```

```python
import functools
import math

import jax
import jax.numpy as jnp
import numpy as np
from jax import lax
from jax.experimental import pallas as pl
from jax.experimental.pallas import tpu as pltpu
from jax.sharding import Mesh
from jax.sharding import PartitionSpec as P

STEPS = 3
AXES = ("x", "z", "ylo", "yhi", "core")
SIZES = {"x": 4, "z": 8, "ylo": 2, "yhi": 2, "core": 2}
BLK = ("x", "z", "ylo")
LAT = ("yhi", "core")
MESH_ID = pl.DeviceIdType.MESH
FIRST = ("core", "z")
SECOND = ("x", "ylo", "yhi")
GROUP = 16
PLANE = ("x", "ylo", "yhi", "core")

pole_gap = 0.1
time_step = 0.03
rigid_gain = 20.0
coupling = 1.0


def node_tables():
    points = np.array([-1.0, -math.sqrt(3.0 / 7.0), 0.0, math.sqrt(3.0 / 7.0), 1.0])
    weights = np.array([0.1, 49.0 / 90.0, 32.0 / 45.0, 49.0 / 90.0, 0.1])
    products = np.array(
        [np.prod([points[i] - points[j] for j in range(5) if j != i]) for i in range(5)]
    )
    slopes = np.zeros((5, 5))
    for i in range(5):
        for j in range(5):
            if i == j:
                slopes[i, j] = sum(1.0 / (points[i] - points[o]) for o in range(5) if o != i)
            else:
                slopes[i, j] = products[i] / products[j] / (points[i] - points[j])
    return points, weights, slopes


POINTS, WEIGHTS, SLOPES = node_tables()
THETA_STEP = (math.pi - 2.0 * pole_gap) / 8
PHI_STEP = 2.0 * math.pi / 64
THETA = pole_gap + (np.arange(8)[:, None] + 0.5 * (1.0 + POINTS)) * THETA_STEP
PHI = (np.arange(64)[:, None] + 0.5 * (1.0 + POINTS)) * PHI_STEP


def legendre_table():
    cosine, sine = np.cos(THETA).reshape(-1), np.sin(THETA).reshape(-1)
    table = np.zeros((128, 128, 40))
    diagonal = np.full(40, math.sqrt(0.5))
    for m in range(128):
        if m > 0:
            diagonal = diagonal * -math.sqrt((2 * m + 1) / (2 * m)) * sine
        table[m, m] = diagonal
        if m + 1 < 128:
            table[m, m + 1] = math.sqrt(2 * m + 3) * cosine * diagonal
        for l in range(m + 2, 128):
            up = math.sqrt((4.0 * l * l - 1) / (l * l - m * m))
            low = math.sqrt(((l - 1.0) ** 2 - m * m) / (4.0 * (l - 1.0) ** 2 - 1))
            table[m, l] = up * (cosine * table[m, l - 1] - low * table[m, l - 2])
    return table.transpose(0, 2, 1).astype(np.float32)


def circle_values():
    m = np.arange(128)
    angle = m[:, None, None] * PHI[None]
    cosines = np.cos(angle) / math.sqrt(math.pi)
    cosines[0] = 1.0 / math.sqrt(2.0 * math.pi)
    sines = np.sin(angle) / math.sqrt(math.pi)
    sines[0] = 0.0
    return np.concatenate((cosines, sines))


def rotations():
    st, ct = np.sin(THETA)[:, :, None, None], np.cos(THETA)[:, :, None, None]
    sp, cp = np.sin(PHI)[None, None], np.cos(PHI)[None, None]
    one, zero = np.ones((8, 5, 64, 5)), np.zeros((8, 5, 64, 5))
    return np.stack(
        [
            np.stack([st * cp, ct * cp, -sp * one]),
            np.stack([st * sp, ct * sp, cp * one]),
            np.stack([ct * one, -st * one, zero]),
        ]
    )


def areas():
    scale = 0.25 * THETA_STEP * PHI_STEP
    return scale * (WEIGHTS * np.sin(THETA))[:, :, None] * WEIGHTS


def pull_table():
    weighted = np.einsum("yba,jkybea,cea->cjkyb", areas(), rotations(), circle_values())
    table = np.zeros((256, 8, 4, 32))
    for k in range(3):
        for lat in range(4):
            for ey in range(2):
                at = (2 * k + ey) * 5
                table[:, :3, lat, at : at + 5] = weighted[:, :, k, 2 * lat + ey]
    return table.reshape(256, 8, 128).astype(np.float32)


def packed_tables():
    table = np.zeros((4, 3, 8, 128))
    area = areas()
    for lat in range(4):
        for r in range(6):
            for a in range(5):
                for b in range(5):
                    ey = r % 2
                    weight = area[2 * lat + ey, b, a]
                    table[lat, a // 4, r, 32 * (a % 4) + 5 * r + b] = weight
                    if r < 2:
                        copies = 2.0 if a in (0, 4) else 1.0
                        pole = (lat, ey, b) in ((0, 0, 0), (3, 1, 4))
                        copies *= 2.0 if b in (0, 4) and not pole else 1.0
                        face = coupling * WEIGHTS[a] * WEIGHTS[b] * copies
                        table[lat, 2, r, 32 + 10 * a + 5 * ey + b] = time_step**2 * weight * face
    return table.astype(np.float32)


def column_tables():
    table = np.zeros((256, 16, 128))
    e = np.arange(64)
    elem = ((e // 16) * 8 + e % 8) * 2 + e // 8 % 2
    m = np.arange(128)
    turn = m[:, None] * elem * PHI_STEP
    shift = m[:, None] * (0.5 * (1.0 + POINTS) * PHI_STEP)
    scale = np.full((128, 1), 1.0 / math.sqrt(math.pi))
    scale[0] = 1.0 / math.sqrt(2.0 * math.pi)
    real = np.ones((128, 1))
    real[0] = 0.0
    for kind in range(2):
        cols = slice(128 * kind, 128 * kind + 128)
        for pair in range(2):
            table[cols, 2 * pair, pair::2] = np.cos(turn)
            table[cols, 2 * pair + 1, pair::2] = np.sin(turn)
            for a in range(4) if pair == 0 else (4,):
                lanes = slice(32 * (a % 4), 32 * (a % 4) + 30)
                if kind == 0:
                    first, second = scale[:, 0] * np.cos(shift[:, a]), -scale[:, 0] * np.sin(shift[:, a])
                else:
                    first, second = (real * scale)[:, 0] * np.sin(shift[:, a]), (real * scale)[:, 0] * np.cos(shift[:, a])
                table[cols, 4 + 2 * pair, lanes] = first[:, None]
                table[cols, 5 + 2 * pair, lanes] = second[:, None]
    table[:, 8:11] = pull_table()[:, :3]
    circle = np.zeros((256, 384))
    circle[:, :320] = circle_values()[:, elem].transpose(0, 2, 1).reshape(256, 320)
    table[:, 11:14] = circle.reshape(256, 3, 128)
    return table.astype(np.float32)


def flat(axes, index):
    at = 0
    for axis in axes:
        at = at * SIZES[axis] + index[axis]
    return at


def unflat(axes, at):
    index = {}
    for axis in reversed(axes):
        index[axis] = at % SIZES[axis]
        at = at // SIZES[axis]
    return index


def partners(axes, me, shifts):
    count = math.prod(SIZES[axis] for axis in axes)
    mine = flat(axes, me)
    found = []
    for shift in shifts:
        other = {**me, **unflat(axes, lax.rem(mine + (shift + count), count))}
        found.append(tuple(other[axis] for axis in AXES))
    return found


def on_sphere(
    u_in, v_in, rig_in, den_in, volume, hist, kern, leg_in, cols_in, packing, order, x_in, xv_in,
    u_out, v_out, hist_out, rigid_out,
    u, v, wr, force, inv, face_force, leg, cols, lp, e32, d32, q8, gown, gtt, ga, gsb, wi, past, coefs, g1, g2,
    lon_lo, lon_hi, lat_lo, lat_hi,
    load_sem, store_sem, send1, recv1, send2, recv2, send_p, recv_p, send_h, recv_h,
):
    me = {axis: lax.axis_index(axis) for axis in AXES}
    lat, depth = flat(LAT, me), me["z"]
    near = partners(FIRST, me, range(1, GROUP))
    far = partners(SECOND, me, range(1, GROUP))
    plane = partners(PLANE, me, range(1, 32))
    column_mates = partners(("z",), me, range(1, 8))
    lon_next, lon_prev = partners(BLK, me, (1, -1))
    lat_next, lat_prev = partners(LAT, me, (1, -1))
    everyone = near + plane + [lon_next, lon_prev, lat_next, lat_prev]
    barrier = pltpu.get_barrier_semaphore()
    for other in everyone:
        pl.semaphore_signal(barrier, inc=1, device_id=other, device_id_type=MESH_ID)

    u[...] = jnp.zeros_like(u)
    v[...] = jnp.zeros_like(v)
    loads = []

    def load(src, dst):
        copy = pltpu.make_async_copy(src, dst, load_sem.at[len(loads)])
        copy.start()
        loads.append(copy)

    for k in range(3):
        load(u_in.at[k], u.at[:, pl.ds(2 * k, 2), :])
    for k in range(3):
        load(rig_in, wr.at[:, pl.ds(2 * k, 2), :])
    load(den_in, wr.at[:, pl.ds(6, 2), :])
    for k in range(3):
        load(v_in.at[k], v.at[:, pl.ds(2 * k, 2), :])
    load(cols_in, cols)
    load(leg_in, leg)

    lanes = lax.broadcasted_iota(jnp.int32, (8, 128), 1)
    subs = lax.broadcasted_iota(jnp.int32, (8, 128), 0)
    slant = lanes - 5 * subs
    even = subs % 2 == 0
    in_field = subs < 6
    slot_near, slot_far, slot_plane = flat(FIRST, me), flat(SECOND, me), flat(PLANE, me)
    mine = slot_far * GROUP + slot_near

    def send(src, dst, ssem, rsem, other):
        copy = pltpu.make_async_remote_copy(
            src_ref=src, dst_ref=dst, send_sem=ssem, recv_sem=rsem,
            device_id=other, device_id_type=MESH_ID,
        )
        copy.start()
        return copy

    def spread(at, stage):
        if stage == 0:
            start, count, others = mine * 2, 2, near
        else:
            start, count, others = slot_far * GROUP * 2, GROUP * 2, far
        block = g1.at[at, pl.ds(start, count), :]
        return [
            send(block, block, send1.at[at, stage, d], recv1.at[at, stage, d], other)
            for d, other in enumerate(others)
        ]

    def arrived(copies):
        for copy in copies:
            copy.wait_recv()

    unsent = []

    def copies_of(a, b):
        count = 2.0 if a in (0, 4) else 1.0
        if b == 0:
            return count * jnp.where(even & (lat == 0), 1.0, 2.0)
        if b == 4:
            return count * jnp.where((~even) & (lat == 3), 1.0, 2.0)
        return count

    def pack(value, first=None):
        packed = [jnp.zeros((8, 128), jnp.float32) for row in range(2)]
        for a in range(5):
            for b in range(5):
                node = jnp.broadcast_to(value(a, b)[:, 0:1], (8, 128))
                if first is None:
                    row, at = a // 4, 32 * (a % 4) + b
                else:
                    row, at = 0, first + 10 * a + b
                packed[row] = jnp.where(slant == at, node, packed[row])
        return packed

    def post(at, value, tail=None):
        packed = pack(value)
        rows = [packed[row] * packing[lat, row] for row in range(2)]
        if tail is not None:
            rows[1] = rows[1] + tail
        g1[at, pl.ds(2 * mine, 2), :] = jnp.concatenate(
            [jnp.sum(row, axis=0, keepdims=True) for row in rows], axis=0
        )
        copies = spread(at, 0)
        unsent.extend(copies)
        return copies

    def forward(at):
        copies = spread(at, 1)
        unsent.extend(copies)
        return copies

    def gradients(base, stride):
        values = [u[base + q * stride] for q in range(5)]
        weights = [wr[base + q * stride] for q in range(5)]
        grads = []
        for p in range(5):
            total = float(SLOPES[p, 0]) * values[0]
            for q in range(1, 5):
                total = total + float(SLOPES[p, q]) * values[q]
            grads.append(total * weights[p])
        return grads, weights

    def divergence(grads, q):
        total = float(SLOPES[0, q]) * grads[0]
        for p in range(1, 5):
            total = total + float(SLOPES[p, q]) * grads[p]
        return total

    def along(stride, base_of, first):
        def line(i, carry):
            base = base_of(i)
            grads, weights = gradients(base, stride)
            for q in range(5):
                total = divergence(grads, q)
                at = base + q * stride
                if first:
                    force[at] = jnp.where(in_field, -total, weights[q])
                else:
                    force[at] = force[at] - total
            return carry

        lax.fori_loop(0, 25, line, 0)

    def stiffness():
        along(25, lambda i: i, True)
        along(5, lambda i: (i // 5) * 25 + i % 5, False)
        along(1, lambda i: i * 5, False)

    def interface_stiffness():
        def radial(i, carry):
            grads, weights = gradients(i * 5, 1)
            face_force[i] = -divergence(grads, 0)
            return carry

        def flat_lines(i, carry):
            grads, weights = gradients(i * 5, 25)
            for q in range(5):
                face_force[q * 5 + i] = face_force[q * 5 + i] - divergence(grads, q)
            grads, weights = gradients(i * 25, 5)
            for q in range(5):
                face_force[i * 5 + q] = face_force[i * 5 + q] - divergence(grads, q)
            return carry

        lax.fori_loop(0, 25, radial, 0)
        lax.fori_loop(0, 5, flat_lines, 0)

    def join_radial():
        for i in range(25):
            low, high = force[i * 5], force[i * 5 + 4]
            force[i * 5] = low + jnp.where(lanes == 0, 0.0, pltpu.roll(high, 1, 1))
            force[i * 5 + 4] = high + jnp.where(lanes == 127, 0.0, pltpu.roll(low, 127, 1))

    def lon_out(step):
        return [
            send(force.at[pl.ds(100, 25)], lon_lo.at[step], send_h.at[step, 0], recv_h.at[step, 0], lon_next),
            send(force.at[pl.ds(0, 25)], lon_hi.at[step], send_h.at[step, 1], recv_h.at[step, 1], lon_prev),
        ]

    def lon_in_lat_out(step, copies):
        for copy in copies:
            copy.wait()
        force[0:25] = force[0:25] + lon_lo[step]
        force[100:125] = force[100:125] + lon_hi[step]
        out = []
        for a in range(5):
            out.append(
                send(force.at[pl.ds(a * 25 + 20, 5)], lat_lo.at[step, pl.ds(a * 5, 5)],
                     send_h.at[step, 2 + a], recv_h.at[step, 2 + a], lat_next)
            )
            out.append(
                send(force.at[pl.ds(a * 25, 5)], lat_hi.at[step, pl.ds(a * 5, 5)],
                     send_h.at[step, 7 + a], recv_h.at[step, 7 + a], lat_prev)
            )
        return out

    def lat_in(step, copies):
        for copy in copies:
            copy.wait()
        for a in range(5):
            for c in range(5):
                low, high = force[a * 25 + c], force[a * 25 + 20 + c]
                below, above = lat_lo[step, a * 5 + c], lat_hi[step, a * 5 + c]
                below = jnp.where(lat == 0, 0.0, pltpu.roll(below, 7, 0))
                above = jnp.where(lat == 3, 0.0, pltpu.roll(above, 1, 0))
                force[a * 25 + c] = low + jnp.where(even, below, pltpu.roll(high, 1, 0))
                force[a * 25 + 20 + c] = high + jnp.where(even, pltpu.roll(low, 7, 0), above)

    def advance():
        def node(i, carry):
            speed_now = jnp.where(in_field, v[i] + time_step * (force[i] * inv[i]), 0.0)
            v[i] = speed_now
            u[i] = u[i] + time_step * speed_now
            return carry

        lax.fori_loop(0, 125, node, 0)

    def predicted(a, b):
        i = a * 5 + b
        push = (time_step**2 * copies_of(a, b)) * (inv[i * 5] * face_force[i])
        return u[i * 5] + time_step * v[i * 5] + push

    def analysed(at):
        field = g1[at].reshape(8, 4, 16, 128)
        field = jnp.concatenate([field[:, i].reshape(128, 128) for i in range(4)], axis=1)
        sums = jnp.dot(e32[...], field, precision=lax.Precision.HIGHEST, preferred_element_type=jnp.float32)
        result = jnp.zeros((8, 128), jnp.float32)
        for i in range(4):
            part = d32[0:8] * sums[0:8, 128 * i : 128 * i + 128]
            for q in range(1, 4):
                part = part + d32[8 * q : 8 * q + 8] * sums[8 * q : 8 * q + 8, 128 * i : 128 * i + 128]
            part = part + pltpu.roll(part, 64, 1)
            part = part + pltpu.roll(part, 32, 1)
            result = jnp.where(lanes // 32 == i, part, result)
        return result

    def owners(step, sums, offset):
        for j in range(3):
            sums = sums - offset[j] * q8[j]
        found = [jnp.zeros((8, 128), jnp.float32) for k in range(3)]
        for t in range(40):
            block = lp[t]
            for k in range(3):
                lane = (t // 10) * 32 + (2 * k + t // 5 % 2) * 5 + t % 5
                found[k] = found[k] + sums[:, lane : lane + 1] * block
        replies = []
        for k in range(3):
            coefs[step + 2, k] = found[k]
            row = jnp.sum(jnp.where(subs == depth, found[k], 0.0), axis=0, keepdims=True)
            hist_out[STEPS - 1 - step, k : k + 1] = row
        for k in range(3):
            reply = past[3 * step + k]
            for i in range(3):
                reply = reply + kern[0, k, i : i + 1] * found[i]
                for back in range(1, step + 1):
                    reply = reply + kern[back, k, i : i + 1] * coefs[step + 2 - back, i]
            replies.append(reply)
        message = jnp.zeros((8, 128), jnp.float32)
        for t in range(40):
            block = lp[t]
            for k in range(3):
                lane = (t // 10) * 32 + (2 * k + t // 5 % 2) * 5 + t % 5
                value = jnp.sum(block * replies[k], axis=1, keepdims=True)
                message = jnp.where(lanes == lane, value, message)
        pulls = [jnp.sum(message * q8[j], axis=1, keepdims=True) for j in range(3)]
        for j, lane in enumerate((30, 31, 62)):
            message = jnp.where(lanes == lane, pulls[j], message)
        block = g2.at[step, pl.ds(8 * slot_plane, 8), :]
        g2[step, pl.ds(8 * slot_plane, 8), :] = message
        copies = [send(block, block, send2.at[step, d], recv2.at[step, d], other) for d, other in enumerate(plane)]
        unsent.extend(copies)
        return copies

    def rigid_step(step, offset, speed):
        whole = jnp.sum(g2[step], axis=0, keepdims=True)
        lane_row = lax.broadcasted_iota(jnp.int32, (1, 128), 1)
        new_offset, new_speed = [], []
        for j, lane in enumerate((30, 31, 62)):
            pull = jnp.sum(jnp.where(lane_row == lane, whole, 0.0), axis=1, keepdims=True)
            new_speed.append(speed[j] + time_step * rigid_gain * pull)
            new_offset.append(offset[j] + time_step * new_speed[j])
        return new_offset, new_speed

    def add_traction(step):
        field = g2[step]
        edge = lanes == 0
        for a in range(5):
            row = jnp.sum(field * gsb[a], axis=0, keepdims=True)
            for b in range(5):
                here = (slant == 32 * lat + b) & in_field
                traction = jnp.sum(jnp.where(here, row, 0.0), axis=1, keepdims=True)
                face = float(coupling * WEIGHTS[a] * WEIGHTS[b]) * copies_of(a, b)
                i = (a * 5 + b) * 5
                gain = jnp.where(edge, time_step * (traction * face) * inv[i], 0.0)
                v[i] = v[i] - gain
                u[i] = u[i] - time_step * gain

    def moved(step):
        total = jnp.zeros((8, 128), jnp.float32)
        for q, (start, count) in enumerate(((0, 128), (128, 128), (256, 64))):
            traction = jnp.dot(
                ga[start : start + count], g2[step], precision=lax.Precision.HIGHEST,
                preferred_element_type=jnp.float32,
            )
            total = total + jnp.dot(
                gown[q, :, 0:count], traction * wi[start : start + count], precision=lax.Precision.HIGHEST,
                preferred_element_type=jnp.float32,
            )
        return total

    def mine_of(position):
        return order[position]

    for copy in loads[0:3]:
        copy.wait()
    packed_start = pack(lambda a, b: u[(a * 5 + b) * 5])
    pl.semaphore_wait(barrier, len(everyone))
    rows = [packed_start[row] * packing[lat, row] for row in range(2)]
    g1[0, pl.ds(2 * mine, 2), :] = jnp.concatenate([jnp.sum(row, axis=0, keepdims=True) for row in rows], axis=0)
    wave0 = spread(0, 0)
    unsent.extend(wave0)

    for step in range(STEPS):
        old = hist[0 : 63 - step]
        for k in range(3):
            total = jnp.sum(kern[step + 1 : 64, k] * old, axis=0)
            past[3 * step + k, pl.ds(depth, 1), :] = jnp.sum(total, axis=0, keepdims=True)
    own_past = past.at[:, pl.ds(depth, 1), :]
    wave_past = [
        send(own_past, own_past, send_p.at[d], recv_p.at[d], other) for d, other in enumerate(column_mates)
    ]
    unsent.extend(wave_past)

    for copy in loads[3:10]:
        copy.wait()

    def weigh(i, carry):
        wr[i] = wr[i] * volume[i]
        return carry

    lax.fori_loop(0, 125, weigh, 0)
    stiffness()
    for i in range(25):
        face_force[i] = force[i * 5]
    join_radial()
    lon = lon_out(0)

    for copy in loads[10:]:
        copy.wait()
    base = (me["x"] * 16 + me["ylo"]) * 4 + lat
    own = [order[base + 8 * i] for i in range(8)]
    for i in range(8):
        for q in range(4):
            e32[8 * q + i : 8 * q + i + 1] = cols[own[i], q : q + 1]
            d32[8 * q + i : 8 * q + i + 1] = cols[own[i], 4 + q : 5 + q]
        for q in range(3):
            q8[q, i : i + 1] = cols[own[i], 8 + q : 9 + q]
            gown[q, i : i + 1] = cols[own[i], 11 + q : 12 + q]

    def take(t, carry):
        for i in range(8):
            lp[t, i : i + 1] = leg[lax.rem(own[i], 128), pl.ds(t, 1), :]
        return carry

    lax.fori_loop(0, 40, take, 0)
    arrived(wave0)
    wave0 = forward(0)

    lat_copies = lon_in_lat_out(0, lon)

    def circle_row(s, carry):
        i, rest = s % 8, s // 8
        column = order[((rest // 8) * 16 + i * 2 + rest // 4 % 2) * 4 + rest % 4]
        for q in range(3):
            gtt[q, pl.ds(s, 1), :] = cols[column, 11 + q : 12 + q]
        return carry

    lax.fori_loop(0, 256, circle_row, 0)
    many = lax.broadcasted_iota(jnp.int32, (256, 128), 1)
    elem = (me["x"] * 2 + me["ylo"]) * 8 + depth
    for a in range(5):
        picked = jnp.where(many == elem + 64 * (a % 2), gtt[a // 2], 0.0)
        gsb[a] = jnp.broadcast_to(jnp.sum(picked, axis=1, keepdims=True), (256, 128))
    for q in range(3):
        ga[128 * q : 128 * q + 128] = jnp.transpose(gtt[q])
    hist_out[3:63] = hist[0:60]
    arrived(wave_past)

    offset = [jnp.full((1, 1), x_in[j], jnp.float32) for j in range(3)]
    speed = [jnp.full((1, 1), xv_in[j], jnp.float32) for j in range(3)]

    arrived(wave0)
    replies0 = owners(0, analysed(0), offset)
    lat_in(0, lat_copies)

    def invert(i, carry):
        mass = force[i]
        inv[i] = 1.0 / jnp.where(even, mass[6:7], mass[7:8])
        return carry

    lax.fori_loop(0, 125, invert, 0)
    tail = pack(lambda a, b: inv[(a * 5 + b) * 5], 32)[0] * packing[lat, 2]
    wave1 = post(1, predicted, tail)
    advance()
    arrived(wave1)
    wave1 = forward(1)
    arrived(replies0)
    add_traction(0)
    offset, speed = rigid_step(0, offset, speed)

    interface_stiffness()
    wave2 = post(2, predicted)
    stiffness()
    join_radial()
    lon = lon_out(1)
    arrived(wave1)
    factors = g1[1, pl.ds(1, 256, 2), :].reshape(8, 4, 8, 128)
    wide = lax.broadcasted_iota(jnp.int32, (64, 128), 1)
    for a in range(5):
        total = jnp.zeros((64, 128), jnp.float32)
        for i in range(4):
            block = factors[:, i].reshape(64, 128)
            for k in range(3):
                start = 32 * i + 10 * k
                turned = pltpu.roll(block, (start - 32 - 10 * a) % 128, 1)
                total = jnp.where((wide >= start) & (wide < start + 10), turned, total)
        wi[64 * a : 64 * a + 64] = total
    replies1 = owners(1, analysed(1) - moved(0), offset)
    arrived(wave2)
    wave2 = forward(2)
    lat_copies = lon_in_lat_out(1, lon)
    lat_in(1, lat_copies)
    advance()
    arrived(replies1)
    add_traction(1)
    offset, speed = rigid_step(1, offset, speed)

    stiffness()
    join_radial()
    lon = lon_out(2)
    shift = moved(1)
    arrived(wave2)
    replies2 = owners(2, analysed(2) - shift, offset)
    lat_copies = lon_in_lat_out(2, lon)
    lat_in(2, lat_copies)
    advance()
    arrived(replies2)
    add_traction(2)
    offset, speed = rigid_step(2, offset, speed)

    stores = []
    for k in range(3):
        for n, (src, dst) in enumerate(((u, u_out), (v, v_out))):
            copy = pltpu.make_async_copy(src.at[:, pl.ds(2 * k, 2), :], dst.at[k], store_sem.at[2 * k + n])
            copy.start()
            stores.append(copy)
    for j in range(3):
        rigid_out[j : j + 1] = jnp.broadcast_to(offset[j], (1, 128))
        rigid_out[3 + j : 4 + j] = jnp.broadcast_to(speed[j], (1, 128))
    rigid_out[6:8] = jnp.zeros((2, 128), jnp.float32)
    for copy in unsent:
        copy.wait_send()
    for copy in stores:
        copy.wait()


def on_device(
    displacement, velocity, rigidity, density, history, kernel, owner_order, rigid_offset, rigid_velocity
):
    volume = (WEIGHTS[:, None, None] * WEIGHTS[:, None] * WEIGHTS).reshape(125).astype(np.float32)
    vmem = pl.BlockSpec(memory_space=pltpu.VMEM)
    smem = pl.BlockSpec(memory_space=pltpu.SMEM)
    hbm = pl.BlockSpec(memory_space=pl.ANY)
    sds = functools.partial(jax.ShapeDtypeStruct, dtype=jnp.float32)
    state = (125, 8, 128)
    sem = pltpu.SemaphoreType.DMA
    new_u, new_v, new_history, rigid = pl.pallas_call(
        on_sphere,
        out_shape=(sds((3, 125, 2, 128)), sds((3, 125, 2, 128)), sds((63, 3, 128)), sds((8, 128))),
        in_specs=[hbm] * 4 + [smem, vmem, vmem, hbm, hbm, vmem] + [smem] * 3,
        out_specs=(hbm, hbm, vmem, vmem),
        scratch_shapes=[
            pltpu.VMEM(shape, jnp.float32)
            for shape in (
                state, state, state, state, state, (25, 8, 128),
                (128, 40, 128), (256, 16, 128), (40, 8, 128), (32, 128), (32, 128), (3, 8, 128), (3, 8, 128),
                (3, 256, 128), (384, 256), (5, 256, 128), (320, 128), (9, 8, 128), (STEPS + 2, 3, 8, 128),
                (STEPS, 512, 128), (STEPS, 256, 128),
            )
            + ((STEPS, 25, 8, 128),) * 4
        ]
        + [
            sem((12,)), sem((6,)), sem((STEPS, 2, GROUP - 1)), sem((STEPS, 2, GROUP - 1)),
            sem((STEPS, 31)), sem((STEPS, 31)), sem((7,)), sem((7,)), sem((STEPS, 12)), sem((STEPS, 12)),
        ],
        compiler_params=pltpu.CompilerParams(
            collective_id=0, has_side_effects=True, vmem_limit_bytes=40 * 1024 * 1024
        ),
    )(
        displacement.reshape(3, 125, 2, 128), velocity.reshape(3, 125, 2, 128),
        rigidity.reshape(125, 2, 128), density.reshape(125, 2, 128), jnp.asarray(volume),
        history[0], kernel, jnp.asarray(legendre_table()), jnp.asarray(column_tables()),
        jnp.asarray(packed_tables()), owner_order, rigid_offset, rigid_velocity,
    )
    shape = displacement.shape
    return new_u.reshape(shape), new_v.reshape(shape), new_history[None], rigid[0:3, 0], rigid[3:6, 0]


def solution(mesh):
    split = Mesh(mesh.devices.reshape(4, 8, 2, 2, 2), AXES)
    field = P(None, None, None, None, BLK, LAT, None)
    scalar_field = P(None, None, None, BLK, LAT, None)
    owned = P(AXES, None, None, None)
    return jax.shard_map(
        on_device,
        mesh=split,
        in_specs=(field, field, scalar_field, scalar_field, owned, P(), P(), P(), P()),
        out_specs=(field, field, owned, P(), P()),
        check_vma=False,
    )
```

```python
import functools
import math

import jax
import jax.numpy as jnp
import numpy as np
from jax import lax
from jax.experimental import pallas as pl
from jax.experimental.pallas import tpu as pltpu
from jax.sharding import Mesh
from jax.sharding import PartitionSpec as P

STEPS = 3
VMEM_BYTES = 60 * 1024 * 1024
AXES = ("x", "z", "ylo", "yhi", "core")
SIZES = {"x": 4, "z": 8, "ylo": 2, "yhi": 2, "core": 2}
BLK = ("x", "z", "ylo")
LAT = ("yhi", "core")
MESH_ID = pl.DeviceIdType.MESH
FIRST = ("core", "z")
SECOND = ("x", "ylo", "yhi")
GROUP = 16
PLANE = ("x", "ylo", "yhi", "core")

pole_gap = 0.1
time_step = 0.03
rigid_gain = 20.0
coupling = 1.0


def node_tables():
    points = np.array([-1.0, -math.sqrt(3.0 / 7.0), 0.0, math.sqrt(3.0 / 7.0), 1.0])
    weights = np.array([0.1, 49.0 / 90.0, 32.0 / 45.0, 49.0 / 90.0, 0.1])
    products = np.array(
        [np.prod([points[i] - points[j] for j in range(5) if j != i]) for i in range(5)]
    )
    slopes = np.zeros((5, 5))
    for i in range(5):
        for j in range(5):
            if i == j:
                slopes[i, j] = sum(1.0 / (points[i] - points[o]) for o in range(5) if o != i)
            else:
                slopes[i, j] = products[i] / products[j] / (points[i] - points[j])
    return points, weights, slopes


POINTS, WEIGHTS, SLOPES = node_tables()
THETA_STEP = (math.pi - 2.0 * pole_gap) / 8
PHI_STEP = 2.0 * math.pi / 64
THETA = pole_gap + (np.arange(8)[:, None] + 0.5 * (1.0 + POINTS)) * THETA_STEP
PHI = (np.arange(64)[:, None] + 0.5 * (1.0 + POINTS)) * PHI_STEP


def legendre_table():
    cosine, sine = np.cos(THETA).reshape(-1), np.sin(THETA).reshape(-1)
    table = np.zeros((128, 128, 40))
    diagonal = np.full(40, math.sqrt(0.5))
    for m in range(128):
        if m > 0:
            diagonal = diagonal * -math.sqrt((2 * m + 1) / (2 * m)) * sine
        table[m, m] = diagonal
        if m + 1 < 128:
            table[m, m + 1] = math.sqrt(2 * m + 3) * cosine * diagonal
        for l in range(m + 2, 128):
            up = math.sqrt((4.0 * l * l - 1) / (l * l - m * m))
            low = math.sqrt(((l - 1.0) ** 2 - m * m) / (4.0 * (l - 1.0) ** 2 - 1))
            table[m, l] = up * (cosine * table[m, l - 1] - low * table[m, l - 2])
    return table.transpose(0, 2, 1).astype(np.float32)


def circle_values():
    m = np.arange(128)
    angle = m[:, None, None] * PHI[None]
    cosines = np.cos(angle) / math.sqrt(math.pi)
    cosines[0] = 1.0 / math.sqrt(2.0 * math.pi)
    sines = np.sin(angle) / math.sqrt(math.pi)
    sines[0] = 0.0
    return np.concatenate((cosines, sines))


def rotations():
    st, ct = np.sin(THETA)[:, :, None, None], np.cos(THETA)[:, :, None, None]
    sp, cp = np.sin(PHI)[None, None], np.cos(PHI)[None, None]
    one, zero = np.ones((8, 5, 64, 5)), np.zeros((8, 5, 64, 5))
    return np.stack(
        [
            np.stack([st * cp, ct * cp, -sp * one]),
            np.stack([st * sp, ct * sp, cp * one]),
            np.stack([ct * one, -st * one, zero]),
        ]
    )


def areas():
    scale = 0.25 * THETA_STEP * PHI_STEP
    return scale * (WEIGHTS * np.sin(THETA))[:, :, None] * WEIGHTS


def pull_table():
    weighted = np.einsum("yba,jkybea,cea->cjkyb", areas(), rotations(), circle_values())
    table = np.zeros((256, 8, 4, 32))
    for k in range(3):
        for lat in range(4):
            for ey in range(2):
                at = (2 * k + ey) * 5
                table[:, :3, lat, at : at + 5] = weighted[:, :, k, 2 * lat + ey]
    return table.reshape(256, 8, 128).astype(np.float32)


def packed_tables():
    table = np.zeros((4, 3, 8, 128))
    area = areas()
    for lat in range(4):
        for r in range(6):
            for a in range(5):
                for b in range(5):
                    ey = r % 2
                    weight = area[2 * lat + ey, b, a]
                    table[lat, a // 4, r, 32 * (a % 4) + 5 * r + b] = weight
                    if r < 2:
                        copies = 2.0 if a in (0, 4) else 1.0
                        pole = (lat, ey, b) in ((0, 0, 0), (3, 1, 4))
                        copies *= 2.0 if b in (0, 4) and not pole else 1.0
                        face = coupling * WEIGHTS[a] * WEIGHTS[b] * copies
                        table[lat, 2, r, 32 + 10 * a + 5 * ey + b] = time_step**2 * weight * face
    return table.astype(np.float32)


def column_tables():
    table = np.zeros((256, 16, 128))
    e = np.arange(64)
    elem = ((e // 16) * 8 + e % 8) * 2 + e // 8 % 2
    m = np.arange(128)
    turn = m[:, None] * elem * PHI_STEP
    shift = m[:, None] * (0.5 * (1.0 + POINTS) * PHI_STEP)
    scale = np.full((128, 1), 1.0 / math.sqrt(math.pi))
    scale[0] = 1.0 / math.sqrt(2.0 * math.pi)
    real = np.ones((128, 1))
    real[0] = 0.0
    for kind in range(2):
        cols = slice(128 * kind, 128 * kind + 128)
        for pair in range(2):
            table[cols, 2 * pair, pair::2] = np.cos(turn)
            table[cols, 2 * pair + 1, pair::2] = np.sin(turn)
            for a in range(4) if pair == 0 else (4,):
                lanes = slice(32 * (a % 4), 32 * (a % 4) + 30)
                if kind == 0:
                    first, second = scale[:, 0] * np.cos(shift[:, a]), -scale[:, 0] * np.sin(shift[:, a])
                else:
                    first, second = (real * scale)[:, 0] * np.sin(shift[:, a]), (real * scale)[:, 0] * np.cos(shift[:, a])
                table[cols, 4 + 2 * pair, lanes] = first[:, None]
                table[cols, 5 + 2 * pair, lanes] = second[:, None]
    table[:, 8:11] = pull_table()[:, :3]
    circle = np.zeros((256, 384))
    circle[:, :320] = circle_values()[:, elem].transpose(0, 2, 1).reshape(256, 320)
    table[:, 11:14] = circle.reshape(256, 3, 128)
    return table.astype(np.float32)


def flat(axes, index):
    at = 0
    for axis in axes:
        at = at * SIZES[axis] + index[axis]
    return at


def unflat(axes, at):
    index = {}
    for axis in reversed(axes):
        index[axis] = at % SIZES[axis]
        at = at // SIZES[axis]
    return index


def partners(axes, me, shifts):
    count = math.prod(SIZES[axis] for axis in axes)
    mine = flat(axes, me)
    found = []
    for shift in shifts:
        other = {**me, **unflat(axes, lax.rem(mine + (shift + count), count))}
        found.append(tuple(other[axis] for axis in AXES))
    return found


def on_sphere(
    u_in, v_in, rig_in, den_in, volume, hist_in, kern, leg_in, cols_in, packing, order, x_in, xv_in,
    u_out, v_out, hist_out, rigid_out,
    un, vn, rn, dn, u, v, wr, force, inv, face_force, hist, leg, cols, lp, e32, d32, q8, gown, gtt, ga, gsb, wi, past, coefs, g1, g2,
    lon_lo, lon_hi, lat_lo, lat_hi, edges,
    load_sem, store_sem, send1, recv1, send2, recv2, send_p, recv_p, send_h, recv_h,
):
    me = {axis: lax.axis_index(axis) for axis in AXES}
    lat, depth = flat(LAT, me), me["z"]
    near = partners(FIRST, me, range(1, GROUP))
    far = partners(SECOND, me, range(1, GROUP))
    plane = partners(PLANE, me, range(1, 32))
    column_mates = partners(("z",), me, range(1, 8))
    lon_next, lon_prev = partners(BLK, me, (1, -1))
    lat_next, lat_prev = partners(LAT, me, (1, -1))
    corners = [lon[:3] + colat[3:] for lon in (lon_next, lon_prev) for colat in (lat_next, lat_prev)]
    everyone = near + plane + [lon_next, lon_prev, lat_next, lat_prev] + corners
    barrier = pltpu.get_barrier_semaphore()
    for other in everyone:
        pl.semaphore_signal(barrier, inc=1, device_id=other, device_id_type=MESH_ID)

    loads = []

    def load(src, dst):
        copy = pltpu.make_async_copy(src, dst, load_sem.at[len(loads)])
        copy.start()
        loads.append(copy)

    load(u_in, un)
    load(rig_in, rn)
    load(den_in, dn)
    load(v_in, vn)
    hist[0:16] = jnp.zeros((16, 128), jnp.float32)
    load(hist_in.at[:, 0, :], hist.at[pl.ds(9, 189), :])
    load(cols_in, cols)
    load(leg_in, leg)

    lanes = lax.broadcasted_iota(jnp.int32, (8, 128), 1)
    subs = lax.broadcasted_iota(jnp.int32, (8, 128), 0)
    slant = lanes - 5 * subs
    even = subs % 2 == 0
    in_field = subs < 6
    slot_near, slot_far, slot_plane = flat(FIRST, me), flat(SECOND, me), flat(PLANE, me)
    mine = slot_far * GROUP + slot_near

    def send(src, dst, ssem, rsem, other):
        copy = pltpu.make_async_remote_copy(
            src_ref=src, dst_ref=dst, send_sem=ssem, recv_sem=rsem,
            device_id=other, device_id_type=MESH_ID,
        )
        copy.start()
        return copy

    def spread(at, stage):
        if stage == 0:
            start, count, others = mine * 2, 2, near
        else:
            start, count, others = slot_far * GROUP * 2, GROUP * 2, far
        block = g1.at[at, pl.ds(start, count), :]
        return [
            send(block, block, send1.at[at, stage, d], recv1.at[at, stage, d], other)
            for d, other in enumerate(others)
        ]

    def arrived(copies):
        for copy in copies:
            copy.wait_recv()

    unsent = []

    def copies_of(a, b):
        count = 2.0 if a in (0, 4) else 1.0
        if b == 0:
            return count * jnp.where(even & (lat == 0), 1.0, 2.0)
        if b == 4:
            return count * jnp.where((~even) & (lat == 3), 1.0, 2.0)
        return count

    def pack(value, first=None):
        packed = [jnp.zeros((8, 128), jnp.float32) for row in range(2)]
        for a in range(5):
            for b in range(5):
                node = jnp.broadcast_to(value(a, b)[:, 0:1], (8, 128))
                if first is None:
                    row, at = a // 4, 32 * (a % 4) + b
                else:
                    row, at = 0, first + 10 * a + b
                packed[row] = jnp.where(slant == at, node, packed[row])
        return packed

    def post(at, value, tail=None):
        packed = pack(value)
        rows = [packed[row] * packing[lat, row] for row in range(2)]
        if tail is not None:
            rows[1] = rows[1] + tail
        g1[at, pl.ds(2 * mine, 2), :] = jnp.concatenate(
            [jnp.sum(row, axis=0, keepdims=True) for row in rows], axis=0
        )
        copies = spread(at, 0)
        unsent.extend(copies)
        return copies

    def forward(at):
        copies = spread(at, 1)
        unsent.extend(copies)
        return copies

    def gradients(base, stride):
        values = [u[base + q * stride] for q in range(5)]
        weights = [wr[base + q * stride] for q in range(5)]
        grads = []
        for p in range(5):
            total = float(SLOPES[p, 0]) * values[0]
            for q in range(1, 5):
                total = total + float(SLOPES[p, q]) * values[q]
            grads.append(total * weights[p])
        return grads, weights

    def divergence(grads, q):
        total = float(SLOPES[0, q]) * grads[0]
        for p in range(1, 5):
            total = total + float(SLOPES[p, q]) * grads[p]
        return total

    def along(stride, base_of, first):
        def line(i, carry):
            base = base_of(i)
            grads, weights = gradients(base, stride)
            for q in range(5):
                total = divergence(grads, q)
                at = base + q * stride
                if first:
                    force[at] = jnp.where(in_field, -total, weights[q])
                else:
                    force[at] = force[at] - total
            return carry

        lax.fori_loop(0, 25, line, 0)

    def stiffness():
        along(25, lambda i: i, True)
        along(5, lambda i: (i // 5) * 25 + i % 5, False)
        along(1, lambda i: i * 5, False)

    def interface_stiffness():
        def radial(i, carry):
            grads, weights = gradients(i * 5, 1)
            face_force[i] = -divergence(grads, 0)
            return carry

        def flat_lines(i, carry):
            grads, weights = gradients(i * 5, 25)
            for q in range(5):
                face_force[q * 5 + i] = face_force[q * 5 + i] - divergence(grads, q)
            grads, weights = gradients(i * 25, 5)
            for q in range(5):
                face_force[i * 5 + q] = face_force[i * 5 + q] - divergence(grads, q)
            return carry

        lax.fori_loop(0, 25, radial, 0)
        lax.fori_loop(0, 5, flat_lines, 0)

    def join_radial():
        for i in range(25):
            low, high = force[i * 5], force[i * 5 + 4]
            force[i * 5] = low + jnp.where(lanes == 0, 0.0, pltpu.roll(high, 1, 1))
            force[i * 5 + 4] = high + jnp.where(lanes == 127, 0.0, pltpu.roll(low, 127, 1))

    def halo_out(step):
        moves = [
            (pl.ds(100, 25), lon_lo.at[step], lon_next),
            (pl.ds(0, 25), lon_hi.at[step], lon_prev),
            (pl.ds(120, 5), edges.at[step, 0], corners[0]),
            (pl.ds(100, 5), edges.at[step, 1], corners[1]),
            (pl.ds(20, 5), edges.at[step, 2], corners[2]),
            (pl.ds(0, 5), edges.at[step, 3], corners[3]),
        ]
        for a in range(5):
            moves.append((pl.ds(25 * a + 20, 5), lat_lo.at[step, pl.ds(5 * a, 5)], lat_next))
            moves.append((pl.ds(25 * a, 5), lat_hi.at[step, pl.ds(5 * a, 5)], lat_prev))
        return [
            send(force.at[rows], dst, send_h.at[step, n], recv_h.at[step, n], other)
            for n, (rows, dst, other) in enumerate(moves)
        ]

    def halo_in(step, copies):
        for copy in copies:
            copy.wait()
        force[0:25] = force[0:25] + lon_lo[step]
        force[100:125] = force[100:125] + lon_hi[step]
        for a in range(5):
            for c in range(5):
                low, high = force[a * 25 + c], force[a * 25 + 20 + c]
                below, above = lat_lo[step, a * 5 + c], lat_hi[step, a * 5 + c]
                if a == 0:
                    below, above = below + edges[step, 0, c], above + edges[step, 1, c]
                if a == 4:
                    below, above = below + edges[step, 2, c], above + edges[step, 3, c]
                below = jnp.where(lat == 0, 0.0, pltpu.roll(below, 7, 0))
                above = jnp.where(lat == 3, 0.0, pltpu.roll(above, 1, 0))
                force[a * 25 + c] = low + jnp.where(even, below, pltpu.roll(high, 1, 0))
                force[a * 25 + 20 + c] = high + jnp.where(even, pltpu.roll(low, 7, 0), above)

    def node_step(i):
        speed_now = jnp.where(in_field, v[i] + time_step * (force[i] * inv[i]), 0.0)
        v[i] = speed_now
        u[i] = u[i] + time_step * speed_now

    def inside(body):
        def line(t, carry):
            for c in range(5):
                body(25 * (1 + t // 3) + 5 * (1 + t % 3) + c)
            return carry

        lax.fori_loop(0, 9, line, 0)

    def around(body):
        def ends(t, carry):
            for c in range(5):
                body(5 * t + c)
                body(100 + 5 * t + c)
            return carry

        def middle(t, carry):
            for c in range(5):
                body(25 * t + c)
                body(25 * t + 20 + c)
            return carry

        lax.fori_loop(0, 5, ends, 0)
        lax.fori_loop(1, 4, middle, 0)

    def predicted(a, b):
        i = a * 5 + b
        push = (time_step**2 * copies_of(a, b)) * (inv[i * 5] * face_force[i])
        return u[i * 5] + time_step * v[i * 5] + push

    def analysed(at):
        field = g1[at].reshape(8, 4, 16, 128)
        field = jnp.concatenate([field[:, i].reshape(128, 128) for i in range(4)], axis=1)
        sums = jnp.dot(e32[...], field, precision=lax.Precision.HIGHEST, preferred_element_type=jnp.float32)
        result = jnp.zeros((8, 128), jnp.float32)
        for i in range(4):
            part = d32[0:8] * sums[0:8, 128 * i : 128 * i + 128]
            for q in range(1, 4):
                part = part + d32[8 * q : 8 * q + 8] * sums[8 * q : 8 * q + 8, 128 * i : 128 * i + 128]
            part = part + pltpu.roll(part, 64, 1)
            part = part + pltpu.roll(part, 32, 1)
            result = jnp.where(lanes // 32 == i, part, result)
        return result

    def owners(step, sums, offset):
        for j in range(3):
            sums = sums - offset[j] * q8[j]
        found = [jnp.zeros((8, 128), jnp.float32) for k in range(3)]
        for t in range(40):
            block = lp[t]
            for k in range(3):
                lane = (t // 10) * 32 + (2 * k + t // 5 % 2) * 5 + t % 5
                found[k] = found[k] + sums[:, lane : lane + 1] * block
        replies = []
        for k in range(3):
            coefs[step + 2, k] = found[k]
            row = jnp.sum(jnp.where(subs == depth, found[k], 0.0), axis=0, keepdims=True)
            hist[3 * (STEPS - 1 - step) + k : 3 * (STEPS - 1 - step) + k + 1] = row
        for k in range(3):
            reply = past[3 * step + k]
            for i in range(3):
                reply = reply + kern[k, i, 0:1] * found[i]
                for back in range(1, step + 1):
                    reply = reply + kern[k, i, back : back + 1] * coefs[step + 2 - back, i]
            replies.append(reply)
        message = jnp.zeros((8, 128), jnp.float32)
        for t in range(40):
            block = lp[t]
            for k in range(3):
                lane = (t // 10) * 32 + (2 * k + t // 5 % 2) * 5 + t % 5
                value = jnp.sum(block * replies[k], axis=1, keepdims=True)
                message = jnp.where(lanes == lane, value, message)
        pulls = [jnp.sum(message * q8[j], axis=1, keepdims=True) for j in range(3)]
        for j, lane in enumerate((30, 31, 62)):
            message = jnp.where(lanes == lane, pulls[j], message)
        block = g2.at[step, pl.ds(8 * slot_plane, 8), :]
        g2[step, pl.ds(8 * slot_plane, 8), :] = message
        copies = [send(block, block, send2.at[step, d], recv2.at[step, d], other) for d, other in enumerate(plane)]
        unsent.extend(copies)
        return copies

    def rigid_step(step, offset, speed):
        whole = jnp.sum(g2[step], axis=0, keepdims=True)
        lane_row = lax.broadcasted_iota(jnp.int32, (1, 128), 1)
        new_offset, new_speed = [], []
        for j, lane in enumerate((30, 31, 62)):
            pull = jnp.sum(jnp.where(lane_row == lane, whole, 0.0), axis=1, keepdims=True)
            new_speed.append(speed[j] + time_step * rigid_gain * pull)
            new_offset.append(offset[j] + time_step * new_speed[j])
        return new_offset, new_speed

    def add_traction(step, shared_moved=True):
        field = g2[step]
        edge = lanes == 0
        for a in range(5):
            row = jnp.sum(field * gsb[a], axis=0, keepdims=True)
            for b in range(5):
                here = (slant == 32 * lat + b) & in_field
                traction = jnp.sum(jnp.where(here, row, 0.0), axis=1, keepdims=True)
                face = float(coupling * WEIGHTS[a] * WEIGHTS[b]) * copies_of(a, b)
                i = (a * 5 + b) * 5
                gain = jnp.where(edge, time_step * (traction * face) * inv[i], 0.0)
                v[i] = v[i] - gain
                if shared_moved or (0 < a < 4 and 0 < b < 4):
                    u[i] = u[i] - time_step * gain

    def moved(step):
        total = jnp.zeros((8, 128), jnp.float32)
        for q, (start, count) in enumerate(((0, 128), (128, 128), (256, 64))):
            traction = jnp.dot(
                ga[start : start + count], g2[step], precision=lax.Precision.HIGHEST,
                preferred_element_type=jnp.float32,
            )
            total = total + jnp.dot(
                gown[q, :, 0:count], traction * wi[start : start + count], precision=lax.Precision.HIGHEST,
                preferred_element_type=jnp.float32,
            )
        return total

    none = jnp.zeros((2, 128), jnp.float32)

    def stacked(field, i):
        return jnp.concatenate([field[0, i], field[1, i], field[2, i], none], axis=0)

    def by_fives(body):
        def five(t, carry):
            for i in range(5):
                body(5 * t + i)
            return carry

        lax.fori_loop(0, 25, five, 0)

    for copy in loads[0:3]:
        copy.wait()

    def stack_state(i):
        u[i] = stacked(un, i)
        wr[i] = jnp.concatenate([rn[i], rn[i], rn[i], dn[i]], axis=0) * volume[i]

    by_fives(stack_state)
    packed_start = pack(lambda a, b: u[(a * 5 + b) * 5])
    rows = [packed_start[row] * packing[lat, row] for row in range(2)]
    g1[0, pl.ds(2 * mine, 2), :] = jnp.concatenate([jnp.sum(row, axis=0, keepdims=True) for row in rows], axis=0)
    stiffness()
    for i in range(25):
        face_force[i] = force[i * 5]
    join_radial()

    loads[4].wait()
    for step in range(STEPS):
        old = [hist[pl.ds(6 - 3 * step + i, 64, 3), :] for i in range(3)]
        for k in range(3):
            total = sum(kern[k, i] * old[i] for i in range(3))
            past[3 * step + k, pl.ds(depth, 1), :] = jnp.sum(total, axis=0, keepdims=True)

    loads[5].wait()
    base = (me["x"] * 16 + me["ylo"]) * 4 + lat
    own = [order[base + 8 * i] for i in range(8)]
    for i in range(8):
        for q in range(4):
            e32[8 * q + i : 8 * q + i + 1] = cols[own[i], q : q + 1]
            d32[8 * q + i : 8 * q + i + 1] = cols[own[i], 4 + q : 5 + q]
        for q in range(3):
            q8[q, i : i + 1] = cols[own[i], 8 + q : 9 + q]
            gown[q, i : i + 1] = cols[own[i], 11 + q : 12 + q]

    def circle_rows(t, carry):
        for i in range(8):
            column = order[((t // 8) * 16 + i * 2 + t // 4 % 2) * 4 + t % 4]
            for q in range(3):
                gtt[q, pl.ds(8 * t + i, 1), :] = cols[column, 11 + q : 12 + q]
        return carry

    lax.fori_loop(0, 32, circle_rows, 0)
    loads[6].wait()

    def take(t, carry):
        for i in range(8):
            lp[t, i : i + 1] = leg[lax.rem(own[i], 128), pl.ds(t, 1), :]
        return carry

    lax.fori_loop(0, 40, take, 0)
    many = lax.broadcasted_iota(jnp.int32, (256, 128), 1)
    elem = (me["x"] * 2 + me["ylo"]) * 8 + depth
    for a in range(5):
        picked = jnp.where(many == elem + 64 * (a % 2), gtt[a // 2], 0.0)
        gsb[a] = jnp.broadcast_to(jnp.sum(picked, axis=1, keepdims=True), (256, 128))
    for q in range(3):
        ga[128 * q : 128 * q + 128] = jnp.transpose(gtt[q])
    loads[3].wait()

    def stack_speed(i):
        v[i] = stacked(vn, i)

    by_fives(stack_speed)
    offset = [jnp.full((1, 1), x_in[j], jnp.float32) for j in range(3)]
    speed = [jnp.full((1, 1), xv_in[j], jnp.float32) for j in range(3)]

    pl.semaphore_wait(barrier, len(everyone))
    wave0 = spread(0, 0)
    halo = halo_out(0)
    own_past = past.at[:, pl.ds(depth, 1), :]
    wave_past = [
        send(own_past, own_past, send_p.at[d], recv_p.at[d], other) for d, other in enumerate(column_mates)
    ]
    unsent.extend(wave0)
    unsent.extend(wave_past)
    stores = [pltpu.make_async_copy(hist.at[pl.ds(9, 180), :], hist_out.at[pl.ds(9, 180), 0, :], store_sem.at[2])]
    stores[0].start()

    arrived(wave0)
    wave0 = forward(0)
    halo_in(0, halo)

    def invert(i):
        mass = force[i]
        inv[i] = 1.0 / jnp.where(even, mass[6:7], mass[7:8])

    def invert_column(i, carry):
        for b in range(5):
            invert(25 * i + 5 * b)
        return carry

    lax.fori_loop(0, 5, invert_column, 0)
    tail = pack(lambda a, b: inv[(a * 5 + b) * 5], 32)[0] * packing[lat, 2]
    wave1 = post(1, predicted, tail)
    arrived(wave_past)
    by_fives(invert)
    arrived(wave0)
    replies0 = owners(0, analysed(0), offset)
    arrived(wave1)
    wave1 = forward(1)
    by_fives(node_step)
    arrived(replies0)
    add_traction(0)
    offset, speed = rigid_step(0, offset, speed)

    interface_stiffness()
    wave2 = post(2, predicted)
    stiffness()
    join_radial()
    halo = halo_out(1)
    arrived(wave1)
    factors = g1[1, pl.ds(1, 256, 2), :].reshape(8, 4, 8, 128)
    wide = lax.broadcasted_iota(jnp.int32, (64, 128), 1)
    for a in range(5):
        total = jnp.zeros((64, 128), jnp.float32)
        for i in range(4):
            block = factors[:, i].reshape(64, 128)
            for k in range(3):
                start = 32 * i + 10 * k
                turned = pltpu.roll(block, (start - 32 - 10 * a) % 128, 1)
                total = jnp.where((wide >= start) & (wide < start + 10), turned, total)
        wi[64 * a : 64 * a + 64] = total
    replies1 = owners(1, analysed(1) - moved(0), offset)
    arrived(wave2)
    wave2 = forward(2)
    inside(node_step)
    halo_in(1, halo)
    around(node_step)
    arrived(replies1)
    add_traction(1)
    offset, speed = rigid_step(1, offset, speed)

    stiffness()
    join_radial()
    halo = halo_out(2)
    shift = moved(1)
    arrived(wave2)
    replies2 = owners(2, analysed(2) - shift, offset)
    inside(node_step)
    arrived(replies2)
    add_traction(2, shared_moved=False)
    offset, speed = rigid_step(2, offset, speed)

    def unstack(i):
        place, speed_now = u[i], v[i]
        for k in range(3):
            un[k, i] = place[2 * k : 2 * k + 2]
            vn[k, i] = speed_now[2 * k : 2 * k + 2]

    inside(unstack)
    halo_in(2, halo)

    def last_step(i):
        node_step(i)
        unstack(i)

    around(last_step)
    stores.append(pltpu.make_async_copy(hist.at[pl.ds(0, 9), :], hist_out.at[pl.ds(0, 9), 0, :], store_sem.at[3]))
    stores[1].start()
    for n, (src, dst) in enumerate(((un, u_out), (vn, v_out))):
        copy = pltpu.make_async_copy(src, dst, store_sem.at[n])
        copy.start()
        stores.append(copy)
    for j in range(3):
        rigid_out[j : j + 1] = jnp.broadcast_to(offset[j], (1, 128))
        rigid_out[3 + j : 4 + j] = jnp.broadcast_to(speed[j], (1, 128))
    rigid_out[6:8] = jnp.zeros((2, 128), jnp.float32)
    for copy in unsent:
        copy.wait_send()
    for copy in stores:
        copy.wait()


def hand_over(u_in, v_in, hist_in, rigid_in, u_out, v_out, hist_out, x_out, xv_out, u, v, hist, sems):
    held = ((u_in, u, u_out), (v_in, v, v_out), (hist_in, hist, hist_out))
    arriving = [pltpu.make_async_copy(src, mid, sems.at[n]) for n, (src, mid, dst) in enumerate(held)]
    leaving = [pltpu.make_async_copy(mid, dst, sems.at[3 + n]) for n, (src, mid, dst) in enumerate(held)]
    for copy in arriving:
        copy.start()
    for j in range(3):
        x_out[j] = rigid_in[j, 0]
        xv_out[j] = rigid_in[3 + j, 0]
    for first, second in zip(arriving, leaving):
        first.wait()
        second.start()
    for copy in leaving:
        copy.wait()


def on_device(
    displacement, velocity, rigidity, density, history, kernel, owner_order, rigid_offset, rigid_velocity
):
    volume = (WEIGHTS[:, None, None] * WEIGHTS[:, None] * WEIGHTS).reshape(125).astype(np.float32)
    vmem = pl.BlockSpec(memory_space=pltpu.VMEM)
    smem = pl.BlockSpec(memory_space=pltpu.SMEM)
    hbm = pl.BlockSpec(memory_space=pl.ANY)
    sds = functools.partial(jax.ShapeDtypeStruct, dtype=jnp.float32)
    state = (125, 8, 128)
    sem = pltpu.SemaphoreType.DMA
    new_u, new_v, new_history, rigid = pl.pallas_call(
        on_sphere,
        out_shape=(sds((3, 125, 2, 128)), sds((3, 125, 2, 128)), sds((189, 1, 128)), sds((8, 128))),
        in_specs=[hbm] * 4 + [smem, hbm, vmem, hbm, hbm, vmem] + [smem] * 3,
        out_specs=(hbm, hbm, hbm, vmem),
        scratch_shapes=[
            pltpu.VMEM(shape, jnp.float32)
            for shape in (
                (3, 125, 2, 128), (3, 125, 2, 128), (125, 2, 128), (125, 2, 128),
                state, state, state, state, state, (25, 8, 128), (200, 128),
                (128, 40, 128), (256, 16, 128), (40, 8, 128), (32, 128), (32, 128), (3, 8, 128), (3, 8, 128),
                (3, 256, 128), (384, 256), (5, 256, 128), (320, 128), (9, 8, 128), (STEPS + 2, 3, 8, 128),
                (STEPS, 512, 128), (STEPS, 256, 128),
            )
            + ((STEPS, 25, 8, 128),) * 4
            + ((STEPS, 4, 5, 8, 128),)
        ]
        + [
            sem((7,)), sem((4,)), sem((STEPS, 2, GROUP - 1)), sem((STEPS, 2, GROUP - 1)),
            sem((STEPS, 31)), sem((STEPS, 31)), sem((7,)), sem((7,)), sem((STEPS, 16)), sem((STEPS, 16)),
        ],
        compiler_params=pltpu.CompilerParams(
            collective_id=0, has_side_effects=True, vmem_limit_bytes=VMEM_BYTES
        ),
    )(
        displacement.reshape(3, 125, 2, 128), velocity.reshape(3, 125, 2, 128),
        rigidity.reshape(125, 2, 128), density.reshape(125, 2, 128), jnp.asarray(volume),
        history.transpose(1, 2, 0, 3).reshape(189, 1, 128), kernel.transpose(1, 2, 0, 3), jnp.asarray(legendre_table()), jnp.asarray(column_tables()),
        jnp.asarray(packed_tables()), owner_order, rigid_offset, rigid_velocity,
    )
    new_u, new_v, new_history, new_offset, new_speed = pl.pallas_call(
        hand_over,
        out_shape=(sds((3, 125, 2, 128)), sds((3, 125, 2, 128)), sds((189, 1, 128)), sds((3,)), sds((3,))),
        in_specs=[hbm, hbm, hbm, smem],
        out_specs=(hbm, hbm, hbm, smem, smem),
        scratch_shapes=[pltpu.VMEM(shape, jnp.float32) for shape in ((3, 125, 2, 128), (3, 125, 2, 128), (189, 1, 128))]
        + [sem((6,))],
        compiler_params=pltpu.CompilerParams(vmem_limit_bytes=VMEM_BYTES),
    )(new_u, new_v, new_history, rigid)
    shape = displacement.shape
    new_history = new_history.reshape(63, 3, 1, 128).transpose(2, 0, 1, 3)
    return new_u.reshape(shape), new_v.reshape(shape), new_history, new_offset, new_speed


def solution(mesh):
    split = Mesh(mesh.devices.reshape(4, 8, 2, 2, 2), AXES)
    field = P(None, None, None, None, BLK, LAT, None)
    scalar_field = P(None, None, None, BLK, LAT, None)
    owned = P(AXES, None, None, None)
    return jax.shard_map(
        on_device,
        mesh=split,
        in_specs=(field, field, scalar_field, scalar_field, owned, P(), P(), P(), P()),
        out_specs=(field, field, owned, P(), P()),
        check_vma=False,
    )
```

```python
import functools
import math

import jax
import jax.numpy as jnp
import numpy as np
from jax import lax
from jax.experimental import pallas as pl
from jax.experimental.pallas import tpu as pltpu
from jax.sharding import Mesh
from jax.sharding import PartitionSpec as P

STEPS = 3
VMEM_BYTES = 60 * 1024 * 1024
AXES = ("x", "z", "ylo", "yhi", "core")
SIZES = {"x": 4, "z": 8, "ylo": 2, "yhi": 2, "core": 2}
BLK = ("x", "z", "ylo")
LAT = ("yhi", "core")
MESH_ID = pl.DeviceIdType.MESH
FIRST = ("core", "z")
SECOND = ("x", "ylo", "yhi")
GROUP = 16
PLANE = ("x", "ylo", "yhi", "core")

pole_gap = 0.1
time_step = 0.03
rigid_gain = 20.0
coupling = 1.0


def node_tables():
    points = np.array([-1.0, -math.sqrt(3.0 / 7.0), 0.0, math.sqrt(3.0 / 7.0), 1.0])
    weights = np.array([0.1, 49.0 / 90.0, 32.0 / 45.0, 49.0 / 90.0, 0.1])
    products = np.array(
        [np.prod([points[i] - points[j] for j in range(5) if j != i]) for i in range(5)]
    )
    slopes = np.zeros((5, 5))
    for i in range(5):
        for j in range(5):
            if i == j:
                slopes[i, j] = sum(1.0 / (points[i] - points[o]) for o in range(5) if o != i)
            else:
                slopes[i, j] = products[i] / products[j] / (points[i] - points[j])
    return points, weights, slopes


POINTS, WEIGHTS, SLOPES = node_tables()
THETA_STEP = (math.pi - 2.0 * pole_gap) / 8
PHI_STEP = 2.0 * math.pi / 64
THETA = pole_gap + (np.arange(8)[:, None] + 0.5 * (1.0 + POINTS)) * THETA_STEP
PHI = (np.arange(64)[:, None] + 0.5 * (1.0 + POINTS)) * PHI_STEP


def legendre_table():
    cosine, sine = np.cos(THETA).reshape(-1), np.sin(THETA).reshape(-1)
    table = np.zeros((128, 128, 40))
    diagonal = np.full(40, math.sqrt(0.5))
    for m in range(128):
        if m > 0:
            diagonal = diagonal * -math.sqrt((2 * m + 1) / (2 * m)) * sine
        table[m, m] = diagonal
        if m + 1 < 128:
            table[m, m + 1] = math.sqrt(2 * m + 3) * cosine * diagonal
        for l in range(m + 2, 128):
            up = math.sqrt((4.0 * l * l - 1) / (l * l - m * m))
            low = math.sqrt(((l - 1.0) ** 2 - m * m) / (4.0 * (l - 1.0) ** 2 - 1))
            table[m, l] = up * (cosine * table[m, l - 1] - low * table[m, l - 2])
    return table.transpose(0, 2, 1).astype(np.float32)


def circle_values():
    m = np.arange(128)
    angle = m[:, None, None] * PHI[None]
    cosines = np.cos(angle) / math.sqrt(math.pi)
    cosines[0] = 1.0 / math.sqrt(2.0 * math.pi)
    sines = np.sin(angle) / math.sqrt(math.pi)
    sines[0] = 0.0
    return np.concatenate((cosines, sines))


def rotations():
    st, ct = np.sin(THETA)[:, :, None, None], np.cos(THETA)[:, :, None, None]
    sp, cp = np.sin(PHI)[None, None], np.cos(PHI)[None, None]
    one, zero = np.ones((8, 5, 64, 5)), np.zeros((8, 5, 64, 5))
    return np.stack(
        [
            np.stack([st * cp, ct * cp, -sp * one]),
            np.stack([st * sp, ct * sp, cp * one]),
            np.stack([ct * one, -st * one, zero]),
        ]
    )


def areas():
    scale = 0.25 * THETA_STEP * PHI_STEP
    return scale * (WEIGHTS * np.sin(THETA))[:, :, None] * WEIGHTS


def pull_table():
    weighted = np.einsum("yba,jkybea,cea->cjkyb", areas(), rotations(), circle_values())
    table = np.zeros((256, 8, 4, 32))
    for k in range(3):
        for lat in range(4):
            for ey in range(2):
                at = (2 * k + ey) * 5
                table[:, :3, lat, at : at + 5] = weighted[:, :, k, 2 * lat + ey]
    return table.reshape(256, 8, 128).astype(np.float32)


def packed_tables():
    table = np.zeros((4, 3, 8, 128))
    area = areas()
    for lat in range(4):
        for r in range(6):
            for a in range(5):
                for b in range(5):
                    ey = r % 2
                    weight = area[2 * lat + ey, b, a]
                    table[lat, a // 4, r, 32 * (a % 4) + 5 * r + b] = weight
                    if r < 2:
                        copies = 2.0 if a in (0, 4) else 1.0
                        pole = (lat, ey, b) in ((0, 0, 0), (3, 1, 4))
                        copies *= 2.0 if b in (0, 4) and not pole else 1.0
                        face = coupling * WEIGHTS[a] * WEIGHTS[b] * copies
                        table[lat, 2, r, 32 + 10 * a + 5 * ey + b] = time_step**2 * weight * face
    return table.astype(np.float32)


def column_tables():
    table = np.zeros((256, 16, 128))
    e = np.arange(64)
    elem = ((e // 16) * 8 + e % 8) * 2 + e // 8 % 2
    m = np.arange(128)
    turn = m[:, None] * elem * PHI_STEP
    shift = m[:, None] * (0.5 * (1.0 + POINTS) * PHI_STEP)
    scale = np.full((128, 1), 1.0 / math.sqrt(math.pi))
    scale[0] = 1.0 / math.sqrt(2.0 * math.pi)
    real = np.ones((128, 1))
    real[0] = 0.0
    for kind in range(2):
        cols = slice(128 * kind, 128 * kind + 128)
        for pair in range(2):
            table[cols, 2 * pair, pair::2] = np.cos(turn)
            table[cols, 2 * pair + 1, pair::2] = np.sin(turn)
            for a in range(4) if pair == 0 else (4,):
                lanes = slice(32 * (a % 4), 32 * (a % 4) + 30)
                if kind == 0:
                    first, second = scale[:, 0] * np.cos(shift[:, a]), -scale[:, 0] * np.sin(shift[:, a])
                else:
                    first, second = (real * scale)[:, 0] * np.sin(shift[:, a]), (real * scale)[:, 0] * np.cos(shift[:, a])
                table[cols, 4 + 2 * pair, lanes] = first[:, None]
                table[cols, 5 + 2 * pair, lanes] = second[:, None]
    table[:, 8:11] = pull_table()[:, :3]
    circle = np.zeros((256, 384))
    circle[:, :320] = circle_values()[:, elem].transpose(0, 2, 1).reshape(256, 320)
    table[:, 11:14] = circle.reshape(256, 3, 128)
    return table.astype(np.float32)


def flat(axes, index):
    at = 0
    for axis in axes:
        at = at * SIZES[axis] + index[axis]
    return at


def unflat(axes, at):
    index = {}
    for axis in reversed(axes):
        index[axis] = at % SIZES[axis]
        at = at // SIZES[axis]
    return index


def partners(axes, me, shifts):
    count = math.prod(SIZES[axis] for axis in axes)
    mine = flat(axes, me)
    found = []
    for shift in shifts:
        other = {**me, **unflat(axes, lax.rem(mine + (shift + count), count))}
        found.append(tuple(other[axis] for axis in AXES))
    return found


def on_sphere(
    u_in, v_in, rig_in, den_in, volume, hist_in, kern, leg_in, cols_in, packing, order, x_in, xv_in,
    u_out, v_out, hist_out, rigid_out,
    un, vn, rn, dn, u, v, wr, force, inv, face_force, hist, leg, cols, lp, e32, d32, q8, gown, gtt, ga, gsb, wi, past, coefs, g1, g2,
    lon_lo, lon_hi, lat_lo, lat_hi, edges, pack_up, pack_down,
    load_sem, store_sem, send1, recv1, send2, recv2, send_p, recv_p, send_h, recv_h,
):
    me = {axis: lax.axis_index(axis) for axis in AXES}
    lat, depth = flat(LAT, me), me["z"]
    near = partners(FIRST, me, range(1, GROUP))
    far = partners(SECOND, me, range(1, GROUP))
    plane = partners(PLANE, me, range(1, 32))
    column_mates = partners(("z",), me, range(1, 8))
    lon_next, lon_prev = partners(BLK, me, (1, -1))
    lat_next, lat_prev = partners(LAT, me, (1, -1))
    corners = [lon[:3] + colat[3:] for lon in (lon_next, lon_prev) for colat in (lat_next, lat_prev)]
    everyone = near + plane + [lon_next, lon_prev, lat_next, lat_prev] + corners
    barrier = pltpu.get_barrier_semaphore()
    for other in everyone:
        pl.semaphore_signal(barrier, inc=1, device_id=other, device_id_type=MESH_ID)

    loads = []

    def load(src, dst):
        copy = pltpu.make_async_copy(src, dst, load_sem.at[len(loads)])
        copy.start()
        loads.append(copy)

    load(u_in, un)
    load(rig_in, rn)
    load(den_in, dn)
    load(v_in, vn)
    hist[0:16] = jnp.zeros((16, 128), jnp.float32)
    load(hist_in.at[:, 0, :], hist.at[pl.ds(9, 189), :])
    load(cols_in, cols)
    load(leg_in, leg)

    lanes = lax.broadcasted_iota(jnp.int32, (8, 128), 1)
    subs = lax.broadcasted_iota(jnp.int32, (8, 128), 0)
    slant = lanes - 5 * subs
    even = subs % 2 == 0
    in_field = subs < 6
    slot_near, slot_far, slot_plane = flat(FIRST, me), flat(SECOND, me), flat(PLANE, me)
    mine = slot_far * GROUP + slot_near

    def send(src, dst, ssem, rsem, other):
        copy = pltpu.make_async_remote_copy(
            src_ref=src, dst_ref=dst, send_sem=ssem, recv_sem=rsem,
            device_id=other, device_id_type=MESH_ID,
        )
        copy.start()
        return copy

    def spread(at, stage):
        if stage == 0:
            start, count, others = mine * 2, 2, near
        else:
            start, count, others = slot_far * GROUP * 2, GROUP * 2, far
        block = g1.at[at, pl.ds(start, count), :]
        return [
            send(block, block, send1.at[at, stage, d], recv1.at[at, stage, d], other)
            for d, other in enumerate(others)
        ]

    def arrived(copies):
        for copy in copies:
            copy.wait_recv()

    unsent = []

    def copies_of(a, b):
        count = 2.0 if a in (0, 4) else 1.0
        if b == 0:
            return count * jnp.where(even & (lat == 0), 1.0, 2.0)
        if b == 4:
            return count * jnp.where((~even) & (lat == 3), 1.0, 2.0)
        return count

    def pack(value, first=None):
        packed = [jnp.zeros((8, 128), jnp.float32) for row in range(2)]
        for a in range(5):
            for b in range(5):
                node = jnp.broadcast_to(value(a, b)[:, 0:1], (8, 128))
                if first is None:
                    row, at = a // 4, 32 * (a % 4) + b
                else:
                    row, at = 0, first + 10 * a + b
                packed[row] = jnp.where(slant == at, node, packed[row])
        return packed

    def post(at, value, tail=None):
        packed = pack(value)
        rows = [packed[row] * packing[lat, row] for row in range(2)]
        if tail is not None:
            rows[1] = rows[1] + tail
        g1[at, pl.ds(2 * mine, 2), :] = jnp.concatenate(
            [jnp.sum(row, axis=0, keepdims=True) for row in rows], axis=0
        )
        copies = spread(at, 0)
        unsent.extend(copies)
        return copies

    def forward(at):
        copies = spread(at, 1)
        unsent.extend(copies)
        return copies

    def gradients(base, stride):
        values = [u[base + q * stride] for q in range(5)]
        weights = [wr[base + q * stride] for q in range(5)]
        grads = []
        for p in range(5):
            total = float(SLOPES[p, 0]) * values[0]
            for q in range(1, 5):
                total = total + float(SLOPES[p, q]) * values[q]
            grads.append(total * weights[p])
        return grads, weights

    def divergence(grads, q):
        total = float(SLOPES[0, q]) * grads[0]
        for p in range(1, 5):
            total = total + float(SLOPES[p, q]) * grads[p]
        return total

    def along(stride, base_of, first):
        def line(i, carry):
            base = base_of(i)
            grads, weights = gradients(base, stride)
            for q in range(5):
                total = divergence(grads, q)
                at = base + q * stride
                if first:
                    force[at] = jnp.where(in_field, -total, weights[q])
                else:
                    force[at] = force[at] - total
            return carry

        lax.fori_loop(0, 25, line, 0)

    def stiffness():
        along(25, lambda i: i, True)
        along(5, lambda i: (i // 5) * 25 + i % 5, False)
        along(1, lambda i: i * 5, False)

    def interface_stiffness():
        def radial(i, carry):
            grads, weights = gradients(i * 5, 1)
            face_force[i] = -divergence(grads, 0)
            return carry

        def flat_lines(i, carry):
            grads, weights = gradients(i * 5, 25)
            for q in range(5):
                face_force[q * 5 + i] = face_force[q * 5 + i] - divergence(grads, q)
            grads, weights = gradients(i * 25, 5)
            for q in range(5):
                face_force[i * 5 + q] = face_force[i * 5 + q] - divergence(grads, q)
            return carry

        lax.fori_loop(0, 25, radial, 0)
        lax.fori_loop(0, 5, flat_lines, 0)

    def join_radial():
        for i in range(25):
            low, high = force[i * 5], force[i * 5 + 4]
            force[i * 5] = low + jnp.where(lanes == 0, 0.0, pltpu.roll(high, 1, 1))
            force[i * 5 + 4] = high + jnp.where(lanes == 127, 0.0, pltpu.roll(low, 127, 1))

    pairs = [(n, 2 * n, min(2 * n + 1, 24)) for n in range(13)]
    not_last, not_first = lat < 3, lat > 0

    def halo_out(step):
        lon_copies = [
            send(force.at[pl.ds(100, 25)], lon_lo.at[step], send_h.at[step, 0], recv_h.at[step, 0], lon_next),
            send(force.at[pl.ds(0, 25)], lon_hi.at[step], send_h.at[step, 1], recv_h.at[step, 1], lon_prev),
        ]
        for n, one, two in pairs:
            up = [force[25 * (x // 5) + 20 + x % 5] for x in (one, two)]
            down = [force[25 * (x // 5) + x % 5] for x in (one, two)]
            pack_up[n] = jnp.where(even, pltpu.roll(up[1], 7, 0), up[0])
            pack_down[n] = jnp.where(even, down[0], pltpu.roll(down[1], 1, 0))

        def moves(packed, face, beside, edge):
            return [
                pltpu.make_async_remote_copy(
                    src_ref=packed.at[pl.ds(start, count)], dst_ref=dst, send_sem=send_h.at[step, at],
                    recv_sem=recv_h.at[step, at], device_id=other, device_id_type=MESH_ID,
                )
                for start, count, dst, at, other in (
                    (0, 13, face.at[step], 2 + edge, beside),
                    (10, 3, edges.at[step, edge], 4 + edge, corners[edge]),
                    (0, 3, edges.at[step, 2 + edge], 6 + edge, corners[2 + edge]),
                )
            ]

        rising = moves(pack_up, lat_lo, lat_next, 0)
        falling = moves(pack_down, lat_hi, lat_prev, 1)

        @pl.when(not_last)
        def _():
            for copy in rising:
                copy.start()

        @pl.when(not_first)
        def _():
            for copy in falling:
                copy.start()

        return lon_copies, rising, falling

    def halo_in(step, copies):
        lon_copies, rising, falling = copies
        for copy in lon_copies:
            copy.wait()

        @pl.when(not_last)
        def _():
            for copy in rising:
                copy.wait_send()
            for copy in falling:
                copy.wait_recv()

        @pl.when(not_first)
        def _():
            for copy in falling:
                copy.wait_send()
            for copy in rising:
                copy.wait_recv()

        force[0:25] = force[0:25] + lon_lo[step]
        force[100:125] = force[100:125] + lon_hi[step]
        for n, one, two in pairs:
            below, above = lat_lo[step, n], lat_hi[step, n]
            if n <= 2:
                first, second = edges[step, 0, n], edges[step, 1, n]
                if n == 2:
                    first, second = jnp.where(even, 0.0, first), jnp.where(even, second, 0.0)
                below, above = below + first, above + second
            if n >= 10:
                below, above = below + edges[step, 2, n - 10], above + edges[step, 3, n - 10]
            below = jnp.where(not_first, below, 0.0)
            above = jnp.where(not_last, above, 0.0)
            for x, part_below, part_above in (
                (one, pltpu.roll(below, 7, 0), pltpu.roll(above, 1, 0)),
                (two, below, above),
            )[: 1 if one == two else 2]:
                low, high = force[25 * (x // 5) + x % 5], force[25 * (x // 5) + 20 + x % 5]
                force[25 * (x // 5) + x % 5] = low + jnp.where(even, part_below, pltpu.roll(high, 1, 0))
                force[25 * (x // 5) + 20 + x % 5] = high + jnp.where(even, pltpu.roll(low, 7, 0), part_above)

    def node_step(i):
        speed_now = jnp.where(in_field, v[i] + time_step * (force[i] * inv[i]), 0.0)
        v[i] = speed_now
        u[i] = u[i] + time_step * speed_now

    def inside(body):
        def line(t, carry):
            for c in range(5):
                body(25 * (1 + t // 3) + 5 * (1 + t % 3) + c)
            return carry

        lax.fori_loop(0, 9, line, 0)

    def around(body):
        def ends(t, carry):
            for c in range(5):
                body(5 * t + c)
                body(100 + 5 * t + c)
            return carry

        def middle(t, carry):
            for c in range(5):
                body(25 * t + c)
                body(25 * t + 20 + c)
            return carry

        lax.fori_loop(0, 5, ends, 0)
        lax.fori_loop(1, 4, middle, 0)

    def predicted(a, b):
        i = a * 5 + b
        push = (time_step**2 * copies_of(a, b)) * (inv[i * 5] * face_force[i])
        return u[i * 5] + time_step * v[i * 5] + push

    def analysed(at):
        field = g1[at].reshape(8, 4, 16, 128)
        field = jnp.concatenate([field[:, i].reshape(128, 128) for i in range(4)], axis=1)
        sums = jnp.dot(e32[...], field, precision=lax.Precision.HIGHEST, preferred_element_type=jnp.float32)
        result = jnp.zeros((8, 128), jnp.float32)
        for i in range(4):
            part = d32[0:8] * sums[0:8, 128 * i : 128 * i + 128]
            for q in range(1, 4):
                part = part + d32[8 * q : 8 * q + 8] * sums[8 * q : 8 * q + 8, 128 * i : 128 * i + 128]
            part = part + pltpu.roll(part, 64, 1)
            part = part + pltpu.roll(part, 32, 1)
            result = jnp.where(lanes // 32 == i, part, result)
        return result

    def owners(step, sums, offset):
        for j in range(3):
            sums = sums - offset[j] * q8[j]
        found = [jnp.zeros((8, 128), jnp.float32) for k in range(3)]
        for t in range(40):
            block = lp[t]
            for k in range(3):
                lane = (t // 10) * 32 + (2 * k + t // 5 % 2) * 5 + t % 5
                found[k] = found[k] + sums[:, lane : lane + 1] * block
        replies = []
        for k in range(3):
            coefs[step + 2, k] = found[k]
            row = jnp.sum(jnp.where(subs == depth, found[k], 0.0), axis=0, keepdims=True)
            hist[3 * (STEPS - 1 - step) + k : 3 * (STEPS - 1 - step) + k + 1] = row
        for k in range(3):
            reply = past[3 * step + k]
            for i in range(3):
                reply = reply + kern[k, i, 0:1] * found[i]
                for back in range(1, step + 1):
                    reply = reply + kern[k, i, back : back + 1] * coefs[step + 2 - back, i]
            replies.append(reply)
        message = jnp.zeros((8, 128), jnp.float32)
        for t in range(40):
            block = lp[t]
            for k in range(3):
                lane = (t // 10) * 32 + (2 * k + t // 5 % 2) * 5 + t % 5
                value = jnp.sum(block * replies[k], axis=1, keepdims=True)
                message = jnp.where(lanes == lane, value, message)
        pulls = [jnp.sum(message * q8[j], axis=1, keepdims=True) for j in range(3)]
        for j, lane in enumerate((30, 31, 62)):
            message = jnp.where(lanes == lane, pulls[j], message)
        block = g2.at[step, pl.ds(8 * slot_plane, 8), :]
        g2[step, pl.ds(8 * slot_plane, 8), :] = message
        copies = [send(block, block, send2.at[step, d], recv2.at[step, d], other) for d, other in enumerate(plane)]
        unsent.extend(copies)
        return copies

    def rigid_step(step, offset, speed):
        whole = jnp.sum(g2[step], axis=0, keepdims=True)
        lane_row = lax.broadcasted_iota(jnp.int32, (1, 128), 1)
        new_offset, new_speed = [], []
        for j, lane in enumerate((30, 31, 62)):
            pull = jnp.sum(jnp.where(lane_row == lane, whole, 0.0), axis=1, keepdims=True)
            new_speed.append(speed[j] + time_step * rigid_gain * pull)
            new_offset.append(offset[j] + time_step * new_speed[j])
        return new_offset, new_speed

    def add_traction(step, shared_moved=True):
        field = g2[step]
        edge = lanes == 0
        for a in range(5):
            row = jnp.sum(field * gsb[a], axis=0, keepdims=True)
            for b in range(5):
                here = (slant == 32 * lat + b) & in_field
                traction = jnp.sum(jnp.where(here, row, 0.0), axis=1, keepdims=True)
                face = float(coupling * WEIGHTS[a] * WEIGHTS[b]) * copies_of(a, b)
                i = (a * 5 + b) * 5
                gain = jnp.where(edge, time_step * (traction * face) * inv[i], 0.0)
                v[i] = v[i] - gain
                if shared_moved or (0 < a < 4 and 0 < b < 4):
                    u[i] = u[i] - time_step * gain

    def moved(step):
        total = jnp.zeros((8, 128), jnp.float32)
        for q, (start, count) in enumerate(((0, 128), (128, 128), (256, 64))):
            traction = jnp.dot(
                ga[start : start + count], g2[step], precision=lax.Precision.HIGHEST,
                preferred_element_type=jnp.float32,
            )
            total = total + jnp.dot(
                gown[q, :, 0:count], traction * wi[start : start + count], precision=lax.Precision.HIGHEST,
                preferred_element_type=jnp.float32,
            )
        return total

    none = jnp.zeros((2, 128), jnp.float32)

    def stacked(field, i):
        return jnp.concatenate([field[0, i], field[1, i], field[2, i], none], axis=0)

    def by_fives(body):
        def five(t, carry):
            for i in range(5):
                body(5 * t + i)
            return carry

        lax.fori_loop(0, 25, five, 0)

    for copy in loads[0:3]:
        copy.wait()

    def stack_state(i):
        u[i] = stacked(un, i)
        wr[i] = jnp.concatenate([rn[i], rn[i], rn[i], dn[i]], axis=0) * volume[i]

    by_fives(stack_state)
    packed_start = pack(lambda a, b: u[(a * 5 + b) * 5])
    rows = [packed_start[row] * packing[lat, row] for row in range(2)]
    g1[0, pl.ds(2 * mine, 2), :] = jnp.concatenate([jnp.sum(row, axis=0, keepdims=True) for row in rows], axis=0)
    stiffness()
    for i in range(25):
        face_force[i] = force[i * 5]
    join_radial()

    loads[4].wait()
    for step in range(STEPS):
        old = [hist[pl.ds(6 - 3 * step + i, 64, 3), :] for i in range(3)]
        for k in range(3):
            total = sum(kern[k, i] * old[i] for i in range(3))
            past[3 * step + k, pl.ds(depth, 1), :] = jnp.sum(total, axis=0, keepdims=True)

    loads[5].wait()
    base = (me["x"] * 16 + me["ylo"]) * 4 + lat
    own = [order[base + 8 * i] for i in range(8)]
    for i in range(8):
        for q in range(4):
            e32[8 * q + i : 8 * q + i + 1] = cols[own[i], q : q + 1]
            d32[8 * q + i : 8 * q + i + 1] = cols[own[i], 4 + q : 5 + q]
        for q in range(3):
            q8[q, i : i + 1] = cols[own[i], 8 + q : 9 + q]
            gown[q, i : i + 1] = cols[own[i], 11 + q : 12 + q]

    def circle_rows(t, carry):
        for i in range(8):
            column = order[((t // 8) * 16 + i * 2 + t // 4 % 2) * 4 + t % 4]
            for q in range(3):
                gtt[q, pl.ds(8 * t + i, 1), :] = cols[column, 11 + q : 12 + q]
        return carry

    lax.fori_loop(0, 32, circle_rows, 0)
    loads[6].wait()

    def take(t, carry):
        for i in range(8):
            lp[t, i : i + 1] = leg[lax.rem(own[i], 128), pl.ds(t, 1), :]
        return carry

    lax.fori_loop(0, 40, take, 0)
    many = lax.broadcasted_iota(jnp.int32, (256, 128), 1)
    elem = (me["x"] * 2 + me["ylo"]) * 8 + depth
    for a in range(5):
        picked = jnp.where(many == elem + 64 * (a % 2), gtt[a // 2], 0.0)
        gsb[a] = jnp.broadcast_to(jnp.sum(picked, axis=1, keepdims=True), (256, 128))
    for q in range(3):
        ga[128 * q : 128 * q + 128] = jnp.transpose(gtt[q])
    loads[3].wait()

    def stack_speed(i):
        v[i] = stacked(vn, i)

    by_fives(stack_speed)
    offset = [jnp.full((1, 1), x_in[j], jnp.float32) for j in range(3)]
    speed = [jnp.full((1, 1), xv_in[j], jnp.float32) for j in range(3)]

    pl.semaphore_wait(barrier, len(everyone))
    wave0 = spread(0, 0)
    halo = halo_out(0)
    own_past = past.at[:, pl.ds(depth, 1), :]
    wave_past = [
        send(own_past, own_past, send_p.at[d], recv_p.at[d], other) for d, other in enumerate(column_mates)
    ]
    unsent.extend(wave0)
    unsent.extend(wave_past)
    stores = [pltpu.make_async_copy(hist.at[pl.ds(9, 180), :], hist_out.at[pl.ds(9, 180), 0, :], store_sem.at[2])]
    stores[0].start()

    arrived(wave0)
    wave0 = forward(0)
    halo_in(0, halo)

    def invert(i):
        mass = force[i]
        inv[i] = 1.0 / jnp.where(even, mass[6:7], mass[7:8])

    def invert_column(i, carry):
        for b in range(5):
            invert(25 * i + 5 * b)
        return carry

    lax.fori_loop(0, 5, invert_column, 0)
    tail = pack(lambda a, b: inv[(a * 5 + b) * 5], 32)[0] * packing[lat, 2]
    wave1 = post(1, predicted, tail)
    arrived(wave_past)
    by_fives(invert)
    arrived(wave0)
    replies0 = owners(0, analysed(0), offset)
    arrived(wave1)
    wave1 = forward(1)
    by_fives(node_step)
    arrived(replies0)
    add_traction(0)
    offset, speed = rigid_step(0, offset, speed)

    interface_stiffness()
    wave2 = post(2, predicted)
    stiffness()
    join_radial()
    halo = halo_out(1)
    arrived(wave1)
    factors = g1[1, pl.ds(1, 256, 2), :].reshape(8, 4, 8, 128)
    wide = lax.broadcasted_iota(jnp.int32, (64, 128), 1)
    for a in range(5):
        total = jnp.zeros((64, 128), jnp.float32)
        for i in range(4):
            block = factors[:, i].reshape(64, 128)
            for k in range(3):
                start = 32 * i + 10 * k
                turned = pltpu.roll(block, (start - 32 - 10 * a) % 128, 1)
                total = jnp.where((wide >= start) & (wide < start + 10), turned, total)
        wi[64 * a : 64 * a + 64] = total
    replies1 = owners(1, analysed(1) - moved(0), offset)
    arrived(wave2)
    wave2 = forward(2)
    inside(node_step)
    halo_in(1, halo)
    around(node_step)
    arrived(replies1)
    add_traction(1)
    offset, speed = rigid_step(1, offset, speed)

    stiffness()
    join_radial()
    halo = halo_out(2)
    shift = moved(1)
    arrived(wave2)
    replies2 = owners(2, analysed(2) - shift, offset)
    inside(node_step)
    arrived(replies2)
    add_traction(2, shared_moved=False)
    offset, speed = rigid_step(2, offset, speed)

    def unstack(i):
        place, speed_now = u[i], v[i]
        for k in range(3):
            un[k, i] = place[2 * k : 2 * k + 2]
            vn[k, i] = speed_now[2 * k : 2 * k + 2]

    inside(unstack)
    halo_in(2, halo)

    def last_step(i):
        node_step(i)
        unstack(i)

    around(last_step)
    stores.append(pltpu.make_async_copy(hist.at[pl.ds(0, 9), :], hist_out.at[pl.ds(0, 9), 0, :], store_sem.at[3]))
    stores[1].start()
    for n, (src, dst) in enumerate(((un, u_out), (vn, v_out))):
        copy = pltpu.make_async_copy(src, dst, store_sem.at[n])
        copy.start()
        stores.append(copy)
    for j in range(3):
        rigid_out[j : j + 1] = jnp.broadcast_to(offset[j], (1, 128))
        rigid_out[3 + j : 4 + j] = jnp.broadcast_to(speed[j], (1, 128))
    rigid_out[6:8] = jnp.zeros((2, 128), jnp.float32)
    for copy in unsent:
        copy.wait_send()
    for copy in stores:
        copy.wait()


def hand_over(u_in, v_in, hist_in, rigid_in, u_out, v_out, hist_out, x_out, xv_out, u, v, hist, sems):
    held = ((u_in, u, u_out), (v_in, v, v_out), (hist_in, hist, hist_out))
    arriving = [pltpu.make_async_copy(src, mid, sems.at[n]) for n, (src, mid, dst) in enumerate(held)]
    leaving = [pltpu.make_async_copy(mid, dst, sems.at[3 + n]) for n, (src, mid, dst) in enumerate(held)]
    for copy in arriving:
        copy.start()
    for j in range(3):
        x_out[j] = rigid_in[j, 0]
        xv_out[j] = rigid_in[3 + j, 0]
    for first, second in zip(arriving, leaving):
        first.wait()
        second.start()
    for copy in leaving:
        copy.wait()


def on_device(
    displacement, velocity, rigidity, density, history, kernel, owner_order, rigid_offset, rigid_velocity
):
    volume = (WEIGHTS[:, None, None] * WEIGHTS[:, None] * WEIGHTS).reshape(125).astype(np.float32)
    vmem = pl.BlockSpec(memory_space=pltpu.VMEM)
    smem = pl.BlockSpec(memory_space=pltpu.SMEM)
    hbm = pl.BlockSpec(memory_space=pl.ANY)
    sds = functools.partial(jax.ShapeDtypeStruct, dtype=jnp.float32)
    state = (125, 8, 128)
    sem = pltpu.SemaphoreType.DMA
    new_u, new_v, new_history, rigid = pl.pallas_call(
        on_sphere,
        out_shape=(sds((3, 125, 2, 128)), sds((3, 125, 2, 128)), sds((189, 1, 128)), sds((8, 128))),
        in_specs=[hbm] * 4 + [smem, hbm, vmem, hbm, hbm, vmem] + [smem] * 3,
        out_specs=(hbm, hbm, hbm, vmem),
        scratch_shapes=[
            pltpu.VMEM(shape, jnp.float32)
            for shape in (
                (3, 125, 2, 128), (3, 125, 2, 128), (125, 2, 128), (125, 2, 128),
                state, state, state, state, state, (25, 8, 128), (200, 128),
                (128, 40, 128), (256, 16, 128), (40, 8, 128), (32, 128), (32, 128), (3, 8, 128), (3, 8, 128),
                (3, 256, 128), (384, 256), (5, 256, 128), (320, 128), (9, 8, 128), (STEPS + 2, 3, 8, 128),
                (STEPS, 512, 128), (STEPS, 256, 128),
            )
            + ((STEPS, 25, 8, 128),) * 2
            + ((STEPS, 13, 8, 128),) * 2
            + ((STEPS, 4, 3, 8, 128), (13, 8, 128), (13, 8, 128))
        ]
        + [
            sem((7,)), sem((4,)), sem((STEPS, 2, GROUP - 1)), sem((STEPS, 2, GROUP - 1)),
            sem((STEPS, 31)), sem((STEPS, 31)), sem((7,)), sem((7,)), sem((STEPS, 8)), sem((STEPS, 8)),
        ],
        compiler_params=pltpu.CompilerParams(
            collective_id=0, has_side_effects=True, vmem_limit_bytes=VMEM_BYTES
        ),
    )(
        displacement.reshape(3, 125, 2, 128), velocity.reshape(3, 125, 2, 128),
        rigidity.reshape(125, 2, 128), density.reshape(125, 2, 128), jnp.asarray(volume),
        history.transpose(1, 2, 0, 3).reshape(189, 1, 128), kernel.transpose(1, 2, 0, 3), jnp.asarray(legendre_table()), jnp.asarray(column_tables()),
        jnp.asarray(packed_tables()), owner_order, rigid_offset, rigid_velocity,
    )
    new_u, new_v, new_history, new_offset, new_speed = pl.pallas_call(
        hand_over,
        out_shape=(sds((3, 125, 2, 128)), sds((3, 125, 2, 128)), sds((189, 1, 128)), sds((3,)), sds((3,))),
        in_specs=[hbm, hbm, hbm, smem],
        out_specs=(hbm, hbm, hbm, smem, smem),
        scratch_shapes=[pltpu.VMEM(shape, jnp.float32) for shape in ((3, 125, 2, 128), (3, 125, 2, 128), (189, 1, 128))]
        + [sem((6,))],
        compiler_params=pltpu.CompilerParams(vmem_limit_bytes=VMEM_BYTES),
    )(new_u, new_v, new_history, rigid)
    shape = displacement.shape
    new_history = new_history.reshape(63, 3, 1, 128).transpose(2, 0, 1, 3)
    return new_u.reshape(shape), new_v.reshape(shape), new_history, new_offset, new_speed


def solution(mesh):
    split = Mesh(mesh.devices.reshape(4, 8, 2, 2, 2), AXES)
    field = P(None, None, None, None, BLK, LAT, None)
    scalar_field = P(None, None, None, BLK, LAT, None)
    owned = P(AXES, None, None, None)
    return jax.shard_map(
        on_device,
        mesh=split,
        in_specs=(field, field, scalar_field, scalar_field, owned, P(), P(), P(), P()),
        out_specs=(field, field, owned, P(), P()),
        check_vma=False,
    )
```

```python
import functools
import math

import jax
import jax.numpy as jnp
import numpy as np
from jax import lax
from jax.experimental import pallas as pl
from jax.experimental.pallas import tpu as pltpu
from jax.sharding import Mesh
from jax.sharding import PartitionSpec as P

STEPS = 3
VMEM_BYTES = 60 * 1024 * 1024
AXES = ("x", "z", "ylo", "yhi", "core")
SIZES = {"x": 4, "z": 8, "ylo": 2, "yhi": 2, "core": 2}
BLK = ("x", "z", "ylo")
LAT = ("yhi", "core")
MESH_ID = pl.DeviceIdType.MESH
FIRST = ("core", "z")
SECOND = ("x", "ylo", "yhi")
GROUP = 16
PLANE = ("x", "ylo", "yhi", "core")

pole_gap = 0.1
time_step = 0.03
rigid_gain = 20.0
coupling = 1.0


def node_tables():
    points = np.array([-1.0, -math.sqrt(3.0 / 7.0), 0.0, math.sqrt(3.0 / 7.0), 1.0])
    weights = np.array([0.1, 49.0 / 90.0, 32.0 / 45.0, 49.0 / 90.0, 0.1])
    products = np.array(
        [np.prod([points[i] - points[j] for j in range(5) if j != i]) for i in range(5)]
    )
    slopes = np.zeros((5, 5))
    for i in range(5):
        for j in range(5):
            if i == j:
                slopes[i, j] = sum(1.0 / (points[i] - points[o]) for o in range(5) if o != i)
            else:
                slopes[i, j] = products[i] / products[j] / (points[i] - points[j])
    return points, weights, slopes


POINTS, WEIGHTS, SLOPES = node_tables()
THETA_STEP = (math.pi - 2.0 * pole_gap) / 8
PHI_STEP = 2.0 * math.pi / 64
THETA = pole_gap + (np.arange(8)[:, None] + 0.5 * (1.0 + POINTS)) * THETA_STEP
PHI = (np.arange(64)[:, None] + 0.5 * (1.0 + POINTS)) * PHI_STEP


def legendre_table():
    cosine, sine = np.cos(THETA).reshape(-1), np.sin(THETA).reshape(-1)
    table = np.zeros((128, 128, 40))
    diagonal = np.full(40, math.sqrt(0.5))
    for m in range(128):
        if m > 0:
            diagonal = diagonal * -math.sqrt((2 * m + 1) / (2 * m)) * sine
        table[m, m] = diagonal
        if m + 1 < 128:
            table[m, m + 1] = math.sqrt(2 * m + 3) * cosine * diagonal
        for l in range(m + 2, 128):
            up = math.sqrt((4.0 * l * l - 1) / (l * l - m * m))
            low = math.sqrt(((l - 1.0) ** 2 - m * m) / (4.0 * (l - 1.0) ** 2 - 1))
            table[m, l] = up * (cosine * table[m, l - 1] - low * table[m, l - 2])
    return table.transpose(0, 2, 1).astype(np.float32)


def circle_values():
    m = np.arange(128)
    angle = m[:, None, None] * PHI[None]
    cosines = np.cos(angle) / math.sqrt(math.pi)
    cosines[0] = 1.0 / math.sqrt(2.0 * math.pi)
    sines = np.sin(angle) / math.sqrt(math.pi)
    sines[0] = 0.0
    return np.concatenate((cosines, sines))


def rotations():
    st, ct = np.sin(THETA)[:, :, None, None], np.cos(THETA)[:, :, None, None]
    sp, cp = np.sin(PHI)[None, None], np.cos(PHI)[None, None]
    one, zero = np.ones((8, 5, 64, 5)), np.zeros((8, 5, 64, 5))
    return np.stack(
        [
            np.stack([st * cp, ct * cp, -sp * one]),
            np.stack([st * sp, ct * sp, cp * one]),
            np.stack([ct * one, -st * one, zero]),
        ]
    )


def areas():
    scale = 0.25 * THETA_STEP * PHI_STEP
    return scale * (WEIGHTS * np.sin(THETA))[:, :, None] * WEIGHTS


def pull_table():
    weighted = np.einsum("yba,jkybea,cea->cjkyb", areas(), rotations(), circle_values())
    table = np.zeros((256, 8, 4, 32))
    for k in range(3):
        for lat in range(4):
            for ey in range(2):
                at = (2 * k + ey) * 5
                table[:, :3, lat, at : at + 5] = weighted[:, :, k, 2 * lat + ey]
    return table.reshape(256, 8, 128).astype(np.float32)


def packed_tables():
    table = np.zeros((4, 3, 8, 128))
    area = areas()
    for lat in range(4):
        for r in range(6):
            for a in range(5):
                for b in range(5):
                    ey = r % 2
                    weight = area[2 * lat + ey, b, a]
                    table[lat, a // 4, r, 32 * (a % 4) + 5 * r + b] = weight
                    if r < 2:
                        copies = 2.0 if a in (0, 4) else 1.0
                        pole = (lat, ey, b) in ((0, 0, 0), (3, 1, 4))
                        copies *= 2.0 if b in (0, 4) and not pole else 1.0
                        face = coupling * WEIGHTS[a] * WEIGHTS[b] * copies
                        table[lat, 2, r, 32 + 10 * a + 5 * ey + b] = time_step**2 * weight * face
    return table.astype(np.float32)


def column_tables():
    table = np.zeros((256, 16, 128))
    e = np.arange(64)
    elem = ((e // 16) * 8 + e % 8) * 2 + e // 8 % 2
    m = np.arange(128)
    turn = m[:, None] * elem * PHI_STEP
    shift = m[:, None] * (0.5 * (1.0 + POINTS) * PHI_STEP)
    scale = np.full((128, 1), 1.0 / math.sqrt(math.pi))
    scale[0] = 1.0 / math.sqrt(2.0 * math.pi)
    real = np.ones((128, 1))
    real[0] = 0.0
    for kind in range(2):
        cols = slice(128 * kind, 128 * kind + 128)
        for pair in range(2):
            table[cols, 2 * pair, pair::2] = np.cos(turn)
            table[cols, 2 * pair + 1, pair::2] = np.sin(turn)
            for a in range(4) if pair == 0 else (4,):
                lanes = slice(32 * (a % 4), 32 * (a % 4) + 30)
                if kind == 0:
                    first, second = scale[:, 0] * np.cos(shift[:, a]), -scale[:, 0] * np.sin(shift[:, a])
                else:
                    first, second = (real * scale)[:, 0] * np.sin(shift[:, a]), (real * scale)[:, 0] * np.cos(shift[:, a])
                table[cols, 4 + 2 * pair, lanes] = first[:, None]
                table[cols, 5 + 2 * pair, lanes] = second[:, None]
    table[:, 8:11] = pull_table()[:, :3]
    circle = np.zeros((256, 384))
    circle[:, :320] = circle_values()[:, elem].transpose(0, 2, 1).reshape(256, 320)
    table[:, 11:14] = circle.reshape(256, 3, 128)
    return table.astype(np.float32)


def flat(axes, index):
    at = 0
    for axis in axes:
        at = at * SIZES[axis] + index[axis]
    return at


def unflat(axes, at):
    index = {}
    for axis in reversed(axes):
        index[axis] = at % SIZES[axis]
        at = at // SIZES[axis]
    return index


def partners(axes, me, shifts):
    count = math.prod(SIZES[axis] for axis in axes)
    mine = flat(axes, me)
    found = []
    for shift in shifts:
        other = {**me, **unflat(axes, lax.rem(mine + (shift + count), count))}
        found.append(tuple(other[axis] for axis in AXES))
    return found


def on_sphere(
    u_in, v_in, rig_in, den_in, volume, hist_in, kern, leg_in, cols_in, packing, order, x_in, xv_in,
    u_out, v_out, hist_out, rigid_out,
    un, vn, rn, dn, u, v, wr, force, inv, face_force, hist, leg, cols, lp, e32, d32, q8, gown, gtt, ga, gsb, wi, past, coefs, g1, g2,
    lon_lo, lon_hi, lat_lo, lat_hi, edges, pack_up, pack_down, close_up, close_down,
    load_sem, store_sem, send1, recv1, send2, recv2, send_p, recv_p, send_h, recv_h,
):
    me = {axis: lax.axis_index(axis) for axis in AXES}
    lat, depth = flat(LAT, me), me["z"]
    near = partners(FIRST, me, range(1, GROUP))
    far = partners(SECOND, me, range(1, GROUP))
    plane = partners(PLANE, me, range(1, 32))
    column_mates = partners(("z",), me, range(1, 8))
    lon_next, lon_prev = partners(BLK, me, (1, -1))
    lat_next, lat_prev = partners(LAT, me, (1, -1))
    corners = [lon[:3] + colat[3:] for lon in (lon_next, lon_prev) for colat in (lat_next, lat_prev)]
    everyone = near + plane + [lon_next, lon_prev, lat_next, lat_prev] + corners
    barrier = pltpu.get_barrier_semaphore()
    for other in everyone:
        pl.semaphore_signal(barrier, inc=1, device_id=other, device_id_type=MESH_ID)

    loads = []

    def load(src, dst):
        copy = pltpu.make_async_copy(src, dst, load_sem.at[len(loads)])
        copy.start()
        loads.append(copy)

    load(u_in, un)
    load(rig_in, rn)
    load(den_in, dn)
    load(v_in, vn)
    hist[0:16] = jnp.zeros((16, 128), jnp.float32)
    load(hist_in.at[:, 0, :], hist.at[pl.ds(9, 189), :])
    load(cols_in, cols)
    load(leg_in, leg)

    lanes = lax.broadcasted_iota(jnp.int32, (8, 128), 1)
    subs = lax.broadcasted_iota(jnp.int32, (8, 128), 0)
    slant = lanes - 5 * subs
    even = subs % 2 == 0
    in_field = subs < 6
    slot_near, slot_far, slot_plane = flat(FIRST, me), flat(SECOND, me), flat(PLANE, me)
    mine = slot_far * GROUP + slot_near

    def send(src, dst, ssem, rsem, other):
        copy = pltpu.make_async_remote_copy(
            src_ref=src, dst_ref=dst, send_sem=ssem, recv_sem=rsem,
            device_id=other, device_id_type=MESH_ID,
        )
        copy.start()
        return copy

    def spread(at, stage):
        if stage == 0:
            start, count, others = mine * 2, 2, near
        else:
            start, count, others = slot_far * GROUP * 2, GROUP * 2, far
        block = g1.at[at, pl.ds(start, count), :]
        return [
            send(block, block, send1.at[at, stage, d], recv1.at[at, stage, d], other)
            for d, other in enumerate(others)
        ]

    def arrived(copies):
        for copy in copies:
            copy.wait_recv()

    unsent = []

    def copies_of(a, b):
        count = 2.0 if a in (0, 4) else 1.0
        if b == 0:
            return count * jnp.where(even & (lat == 0), 1.0, 2.0)
        if b == 4:
            return count * jnp.where((~even) & (lat == 3), 1.0, 2.0)
        return count

    def pack(value, first=None):
        packed = [jnp.zeros((8, 128), jnp.float32) for row in range(2)]
        for a in range(5):
            for b in range(5):
                node = jnp.broadcast_to(value(a, b)[:, 0:1], (8, 128))
                if first is None:
                    row, at = a // 4, 32 * (a % 4) + b
                else:
                    row, at = 0, first + 10 * a + b
                packed[row] = jnp.where(slant == at, node, packed[row])
        return packed

    def post(at, value, tail=None):
        packed = pack(value)
        rows = [packed[row] * packing[lat, row] for row in range(2)]
        if tail is not None:
            rows[1] = rows[1] + tail
        g1[at, pl.ds(2 * mine, 2), :] = jnp.concatenate(
            [jnp.sum(row, axis=0, keepdims=True) for row in rows], axis=0
        )
        copies = spread(at, 0)
        unsent.extend(copies)
        return copies

    def forward(at):
        copies = spread(at, 1)
        unsent.extend(copies)
        return copies

    def gradients(base, stride):
        values = [u[base + q * stride] for q in range(5)]
        weights = [wr[base + q * stride] for q in range(5)]
        grads = []
        for p in range(5):
            total = float(SLOPES[p, 0]) * values[0]
            for q in range(1, 5):
                total = total + float(SLOPES[p, q]) * values[q]
            grads.append(total * weights[p])
        return grads, weights

    def divergence(grads, q):
        total = float(SLOPES[0, q]) * grads[0]
        for p in range(1, 5):
            total = total + float(SLOPES[p, q]) * grads[p]
        return total

    def along(stride, base_of, first):
        def line(i, carry):
            base = base_of(i)
            grads, weights = gradients(base, stride)
            for q in range(5):
                total = divergence(grads, q)
                at = base + q * stride
                if first:
                    force[at] = jnp.where(in_field, -total, weights[q])
                else:
                    force[at] = force[at] - total
            return carry

        lax.fori_loop(0, 25, line, 0)

    def stiffness():
        along(25, lambda i: i, True)
        along(5, lambda i: (i // 5) * 25 + i % 5, False)
        along(1, lambda i: i * 5, False)

    def join_radial():
        for i in range(25):
            low, high = force[i * 5], force[i * 5 + 4]
            force[i * 5] = low + jnp.where(lanes == 0, 0.0, pltpu.roll(high, 1, 1))
            force[i * 5 + 4] = high + jnp.where(lanes == 127, 0.0, pltpu.roll(low, 127, 1))

    pairs = [(n, 2 * n, min(2 * n + 1, 24)) for n in range(13)]
    not_last, not_first = lat < 3, lat > 0

    def close_pack(base, packed):
        last = jnp.zeros((8, 128), jnp.float32)
        for b in range(5):
            third = force[base + 5 * b + 3]
            for c in range(3):
                packed[3 * b + c] = jnp.where(in_field, force[base + 5 * b + c], pltpu.roll(third, 6 - 2 * c, 0))
            last = jnp.where(lanes == b, jnp.broadcast_to(force[base + 5 * b + 4][:, 127:128], (8, 128)), last)
        packed[15] = last

    def close_add(base, packed):
        last = packed[15]
        for b in range(5):
            parts = [packed[3 * b + c] for c in range(3)]
            third = jnp.where(subs < 2, pltpu.roll(parts[0], 2, 0), pltpu.roll(parts[1], 4, 0))
            third = jnp.where(subs < 4, third, pltpu.roll(parts[2], 6, 0))
            end = jnp.where(lanes == 127, last[:, b : b + 1], pltpu.roll(parts[0], 127, 1))
            for c, part in enumerate(parts + [third, end]):
                at = base + 5 * b + c
                force[at] = force[at] + jnp.where(in_field, part, 0.0)

    def halo_out(step):
        if step == 0:
            faces = [force.at[pl.ds(100, 25)], force.at[pl.ds(0, 25)]]
            into = [lon_lo.at[0], lon_hi.at[0]]
        else:
            close_pack(100, close_up)
            close_pack(0, close_down)
            faces = [close_up, close_down]
            into = [lon_lo.at[step, pl.ds(0, 16)], lon_hi.at[step, pl.ds(0, 16)]]
        lon_copies = [
            send(faces[n], into[n], send_h.at[step, n], recv_h.at[step, n], other)
            for n, other in enumerate((lon_next, lon_prev))
        ]
        for n, one, two in pairs:
            up = [force[25 * (x // 5) + 20 + x % 5] for x in (one, two)]
            down = [force[25 * (x // 5) + x % 5] for x in (one, two)]
            pack_up[n] = jnp.where(even, pltpu.roll(up[1], 7, 0), up[0])
            pack_down[n] = jnp.where(even, down[0], pltpu.roll(down[1], 1, 0))

        def moves(packed, face, beside, edge):
            return [
                pltpu.make_async_remote_copy(
                    src_ref=packed.at[pl.ds(start, count)], dst_ref=dst, send_sem=send_h.at[step, at],
                    recv_sem=recv_h.at[step, at], device_id=other, device_id_type=MESH_ID,
                )
                for start, count, dst, at, other in (
                    (0, 13, face.at[step], 2 + edge, beside),
                    (10, 3, edges.at[step, edge], 4 + edge, corners[edge]),
                    (0, 3, edges.at[step, 2 + edge], 6 + edge, corners[2 + edge]),
                )
            ]

        rising = moves(pack_up, lat_lo, lat_next, 0)
        falling = moves(pack_down, lat_hi, lat_prev, 1)

        @pl.when(not_last)
        def _():
            for copy in rising:
                copy.start()

        @pl.when(not_first)
        def _():
            for copy in falling:
                copy.start()

        return lon_copies, rising, falling

    def halo_in(step, copies):
        lon_copies, rising, falling = copies
        for copy in lon_copies:
            copy.wait()

        @pl.when(not_last)
        def _():
            for copy in rising:
                copy.wait_send()
            for copy in falling:
                copy.wait_recv()

        @pl.when(not_first)
        def _():
            for copy in falling:
                copy.wait_send()
            for copy in rising:
                copy.wait_recv()

        if step == 0:
            force[0:25] = force[0:25] + lon_lo[0]
            force[100:125] = force[100:125] + lon_hi[0]
        else:
            close_add(0, lon_lo.at[step])
            close_add(100, lon_hi.at[step])
        for n, one, two in pairs:
            below, above = lat_lo[step, n], lat_hi[step, n]
            if n <= 2:
                first, second = edges[step, 0, n], edges[step, 1, n]
                if n == 2:
                    first, second = jnp.where(even, 0.0, first), jnp.where(even, second, 0.0)
                below, above = below + first, above + second
            if n >= 10:
                below, above = below + edges[step, 2, n - 10], above + edges[step, 3, n - 10]
            below = jnp.where(not_first, below, 0.0)
            above = jnp.where(not_last, above, 0.0)
            for x, part_below, part_above in (
                (one, pltpu.roll(below, 7, 0), pltpu.roll(above, 1, 0)),
                (two, below, above),
            )[: 1 if one == two else 2]:
                low, high = force[25 * (x // 5) + x % 5], force[25 * (x // 5) + 20 + x % 5]
                force[25 * (x // 5) + x % 5] = low + jnp.where(even, part_below, pltpu.roll(high, 1, 0))
                force[25 * (x // 5) + 20 + x % 5] = high + jnp.where(even, pltpu.roll(low, 7, 0), part_above)

    def node_step(i):
        speed_now = jnp.where(in_field, v[i] + time_step * (force[i] * inv[i]), 0.0)
        v[i] = speed_now
        u[i] = u[i] + time_step * speed_now

    def inside(body):
        def line(t, carry):
            for c in range(5):
                body(25 * (1 + t // 3) + 5 * (1 + t % 3) + c)
            return carry

        lax.fori_loop(0, 9, line, 0)

    def around(body):
        def ends(t, carry):
            for c in range(5):
                body(5 * t + c)
                body(100 + 5 * t + c)
            return carry

        def middle(t, carry):
            for c in range(5):
                body(25 * t + c)
                body(25 * t + 20 + c)
            return carry

        lax.fori_loop(0, 5, ends, 0)
        lax.fori_loop(1, 4, middle, 0)

    def predicted(a, b):
        i = a * 5 + b
        push = (time_step**2 * copies_of(a, b)) * (inv[i * 5] * face_force[i])
        return u[i * 5] + time_step * v[i * 5] + push

    def analysed(at):
        field = g1[at].reshape(8, 4, 16, 128)
        field = jnp.concatenate([field[:, i].reshape(128, 128) for i in range(4)], axis=1)
        sums = jnp.dot(e32[...], field, precision=lax.Precision.HIGHEST, preferred_element_type=jnp.float32)
        result = jnp.zeros((8, 128), jnp.float32)
        for i in range(4):
            part = d32[0:8] * sums[0:8, 128 * i : 128 * i + 128]
            for q in range(1, 4):
                part = part + d32[8 * q : 8 * q + 8] * sums[8 * q : 8 * q + 8, 128 * i : 128 * i + 128]
            part = part + pltpu.roll(part, 64, 1)
            part = part + pltpu.roll(part, 32, 1)
            result = jnp.where(lanes // 32 == i, part, result)
        return result

    def owners(step, sums, offset):
        for j in range(3):
            sums = sums - offset[j] * q8[j]
        found = [jnp.zeros((8, 128), jnp.float32) for k in range(3)]
        for t in range(40):
            block = lp[t]
            for k in range(3):
                lane = (t // 10) * 32 + (2 * k + t // 5 % 2) * 5 + t % 5
                found[k] = found[k] + sums[:, lane : lane + 1] * block
        replies = []
        for k in range(3):
            coefs[step + 2, k] = found[k]
            row = jnp.sum(jnp.where(subs == depth, found[k], 0.0), axis=0, keepdims=True)
            hist[3 * (STEPS - 1 - step) + k : 3 * (STEPS - 1 - step) + k + 1] = row
        for k in range(3):
            reply = past[3 * step + k]
            for i in range(3):
                reply = reply + kern[k, i, 0:1] * found[i]
                for back in range(1, step + 1):
                    reply = reply + kern[k, i, back : back + 1] * coefs[step + 2 - back, i]
            replies.append(reply)
        message = jnp.zeros((8, 128), jnp.float32)
        for t in range(40):
            block = lp[t]
            for k in range(3):
                lane = (t // 10) * 32 + (2 * k + t // 5 % 2) * 5 + t % 5
                value = jnp.sum(block * replies[k], axis=1, keepdims=True)
                message = jnp.where(lanes == lane, value, message)
        pulls = [jnp.sum(message * q8[j], axis=1, keepdims=True) for j in range(3)]
        for j, lane in enumerate((30, 31, 62)):
            message = jnp.where(lanes == lane, pulls[j], message)
        block = g2.at[step, pl.ds(8 * slot_plane, 8), :]
        g2[step, pl.ds(8 * slot_plane, 8), :] = message
        copies = [send(block, block, send2.at[step, d], recv2.at[step, d], other) for d, other in enumerate(plane)]
        unsent.extend(copies)
        return copies

    def rigid_step(step, offset, speed):
        whole = jnp.sum(g2[step], axis=0, keepdims=True)
        lane_row = lax.broadcasted_iota(jnp.int32, (1, 128), 1)
        new_offset, new_speed = [], []
        for j, lane in enumerate((30, 31, 62)):
            pull = jnp.sum(jnp.where(lane_row == lane, whole, 0.0), axis=1, keepdims=True)
            new_speed.append(speed[j] + time_step * rigid_gain * pull)
            new_offset.append(offset[j] + time_step * new_speed[j])
        return new_offset, new_speed

    def add_traction(step, shared_moved=True):
        field = g2[step]
        edge = lanes == 0
        for a in range(5):
            row = jnp.sum(field * gsb[a], axis=0, keepdims=True)
            for b in range(5):
                here = (slant == 32 * lat + b) & in_field
                traction = jnp.sum(jnp.where(here, row, 0.0), axis=1, keepdims=True)
                face = float(coupling * WEIGHTS[a] * WEIGHTS[b]) * copies_of(a, b)
                i = (a * 5 + b) * 5
                gain = jnp.where(edge, time_step * (traction * face) * inv[i], 0.0)
                v[i] = v[i] - gain
                if shared_moved or (0 < a < 4 and 0 < b < 4):
                    u[i] = u[i] - time_step * gain

    def moved(step):
        total = jnp.zeros((8, 128), jnp.float32)
        for q, (start, count) in enumerate(((0, 128), (128, 128), (256, 64))):
            traction = jnp.dot(
                ga[start : start + count], g2[step], precision=lax.Precision.HIGHEST,
                preferred_element_type=jnp.float32,
            )
            total = total + jnp.dot(
                gown[q, :, 0:count], traction * wi[start : start + count], precision=lax.Precision.HIGHEST,
                preferred_element_type=jnp.float32,
            )
        return total

    none = jnp.zeros((2, 128), jnp.float32)

    def stacked(field, i):
        return jnp.concatenate([field[0, i], field[1, i], field[2, i], none], axis=0)

    def by_fives(body):
        def five(t, carry):
            for i in range(5):
                body(5 * t + i)
            return carry

        lax.fori_loop(0, 25, five, 0)

    for copy in loads[0:3]:
        copy.wait()

    def stack_state(i):
        u[i] = stacked(un, i)
        wr[i] = jnp.concatenate([rn[i], rn[i], rn[i], dn[i]], axis=0) * volume[i]

    by_fives(stack_state)
    packed_start = pack(lambda a, b: u[(a * 5 + b) * 5])
    rows = [packed_start[row] * packing[lat, row] for row in range(2)]
    g1[0, pl.ds(2 * mine, 2), :] = jnp.concatenate([jnp.sum(row, axis=0, keepdims=True) for row in rows], axis=0)
    stiffness()
    for i in range(25):
        face_force[i] = force[i * 5]
    join_radial()

    loads[4].wait()
    for step in range(STEPS):
        old = [hist[pl.ds(6 - 3 * step + i, 64, 3), :] for i in range(3)]
        for k in range(3):
            total = sum(kern[k, i] * old[i] for i in range(3))
            past[3 * step + k, pl.ds(depth, 1), :] = jnp.sum(total, axis=0, keepdims=True)

    loads[5].wait()
    base = (me["x"] * 16 + me["ylo"]) * 4 + lat
    own = [order[base + 8 * i] for i in range(8)]
    for i in range(8):
        for q in range(4):
            e32[8 * q + i : 8 * q + i + 1] = cols[own[i], q : q + 1]
            d32[8 * q + i : 8 * q + i + 1] = cols[own[i], 4 + q : 5 + q]
        for q in range(3):
            q8[q, i : i + 1] = cols[own[i], 8 + q : 9 + q]
            gown[q, i : i + 1] = cols[own[i], 11 + q : 12 + q]

    def circle_rows(t, carry):
        for i in range(8):
            column = order[((t // 8) * 16 + i * 2 + t // 4 % 2) * 4 + t % 4]
            for q in range(3):
                gtt[q, pl.ds(8 * t + i, 1), :] = cols[column, 11 + q : 12 + q]
        return carry

    lax.fori_loop(0, 32, circle_rows, 0)
    loads[6].wait()

    def take(t, carry):
        for i in range(8):
            lp[t, i : i + 1] = leg[lax.rem(own[i], 128), pl.ds(t, 1), :]
        return carry

    lax.fori_loop(0, 40, take, 0)
    many = lax.broadcasted_iota(jnp.int32, (256, 128), 1)
    elem = (me["x"] * 2 + me["ylo"]) * 8 + depth
    for a in range(5):
        picked = jnp.where(many == elem + 64 * (a % 2), gtt[a // 2], 0.0)
        gsb[a] = jnp.broadcast_to(jnp.sum(picked, axis=1, keepdims=True), (256, 128))
    for q in range(3):
        ga[128 * q : 128 * q + 128] = jnp.transpose(gtt[q])
    loads[3].wait()

    def stack_speed(i):
        v[i] = stacked(vn, i)

    by_fives(stack_speed)
    offset = [jnp.full((1, 1), x_in[j], jnp.float32) for j in range(3)]
    speed = [jnp.full((1, 1), xv_in[j], jnp.float32) for j in range(3)]

    pl.semaphore_wait(barrier, len(everyone))
    wave0 = spread(0, 0)
    halo = halo_out(0)
    own_past = past.at[:, pl.ds(depth, 1), :]
    wave_past = [
        send(own_past, own_past, send_p.at[d], recv_p.at[d], other) for d, other in enumerate(column_mates)
    ]
    unsent.extend(wave0)
    unsent.extend(wave_past)
    stores = [pltpu.make_async_copy(hist.at[pl.ds(9, 180), :], hist_out.at[pl.ds(9, 180), 0, :], store_sem.at[2])]
    stores[0].start()

    arrived(wave0)
    wave0 = forward(0)
    halo_in(0, halo)

    def invert(i):
        mass = force[i]
        inv[i] = 1.0 / jnp.where(even, mass[6:7], mass[7:8])

    def invert_column(i, carry):
        for b in range(5):
            invert(25 * i + 5 * b)
        return carry

    lax.fori_loop(0, 5, invert_column, 0)
    tail = pack(lambda a, b: inv[(a * 5 + b) * 5], 32)[0] * packing[lat, 2]
    wave1 = post(1, predicted, tail)
    arrived(wave_past)
    by_fives(invert)
    arrived(wave0)
    replies0 = owners(0, analysed(0), offset)
    arrived(wave1)
    wave1 = forward(1)
    by_fives(node_step)
    arrived(replies0)
    add_traction(0)
    offset, speed = rigid_step(0, offset, speed)

    stiffness()
    for i in range(25):
        face_force[i] = force[i * 5]
    join_radial()
    halo = halo_out(1)
    wave2 = post(2, predicted)
    arrived(wave1)
    factors = g1[1, pl.ds(1, 256, 2), :].reshape(8, 4, 8, 128)
    wide = lax.broadcasted_iota(jnp.int32, (64, 128), 1)
    for a in range(5):
        total = jnp.zeros((64, 128), jnp.float32)
        for i in range(4):
            block = factors[:, i].reshape(64, 128)
            for k in range(3):
                start = 32 * i + 10 * k
                turned = pltpu.roll(block, (start - 32 - 10 * a) % 128, 1)
                total = jnp.where((wide >= start) & (wide < start + 10), turned, total)
        wi[64 * a : 64 * a + 64] = total
    replies1 = owners(1, analysed(1) - moved(0), offset)
    arrived(wave2)
    wave2 = forward(2)
    inside(node_step)
    halo_in(1, halo)
    around(node_step)
    arrived(replies1)
    add_traction(1)
    offset, speed = rigid_step(1, offset, speed)

    stiffness()
    join_radial()
    halo = halo_out(2)
    shift = moved(1)
    arrived(wave2)
    replies2 = owners(2, analysed(2) - shift, offset)
    inside(node_step)
    arrived(replies2)
    add_traction(2, shared_moved=False)
    offset, speed = rigid_step(2, offset, speed)

    def unstack(i):
        place, speed_now = u[i], v[i]
        for k in range(3):
            un[k, i] = place[2 * k : 2 * k + 2]
            vn[k, i] = speed_now[2 * k : 2 * k + 2]

    inside(unstack)
    halo_in(2, halo)

    def last_step(i):
        node_step(i)
        unstack(i)

    around(last_step)
    stores.append(pltpu.make_async_copy(hist.at[pl.ds(0, 9), :], hist_out.at[pl.ds(0, 9), 0, :], store_sem.at[3]))
    stores[1].start()
    for n, (src, dst) in enumerate(((un, u_out), (vn, v_out))):
        copy = pltpu.make_async_copy(src, dst, store_sem.at[n])
        copy.start()
        stores.append(copy)
    for j in range(3):
        rigid_out[j : j + 1] = jnp.broadcast_to(offset[j], (1, 128))
        rigid_out[3 + j : 4 + j] = jnp.broadcast_to(speed[j], (1, 128))
    rigid_out[6:8] = jnp.zeros((2, 128), jnp.float32)
    for copy in unsent:
        copy.wait_send()
    for copy in stores:
        copy.wait()


def hand_over(u_in, v_in, hist_in, rigid_in, u_out, v_out, hist_out, x_out, xv_out, u, v, hist, sems):
    held = ((u_in, u, u_out), (v_in, v, v_out), (hist_in, hist, hist_out))
    arriving = [pltpu.make_async_copy(src, mid, sems.at[n]) for n, (src, mid, dst) in enumerate(held)]
    leaving = [pltpu.make_async_copy(mid, dst, sems.at[3 + n]) for n, (src, mid, dst) in enumerate(held)]
    for copy in arriving:
        copy.start()
    for j in range(3):
        x_out[j] = rigid_in[j, 0]
        xv_out[j] = rigid_in[3 + j, 0]
    for first, second in zip(arriving, leaving):
        first.wait()
        second.start()
    for copy in leaving:
        copy.wait()


def on_device(
    displacement, velocity, rigidity, density, history, kernel, owner_order, rigid_offset, rigid_velocity
):
    volume = (WEIGHTS[:, None, None] * WEIGHTS[:, None] * WEIGHTS).reshape(125).astype(np.float32)
    vmem = pl.BlockSpec(memory_space=pltpu.VMEM)
    smem = pl.BlockSpec(memory_space=pltpu.SMEM)
    hbm = pl.BlockSpec(memory_space=pl.ANY)
    sds = functools.partial(jax.ShapeDtypeStruct, dtype=jnp.float32)
    state = (125, 8, 128)
    sem = pltpu.SemaphoreType.DMA
    new_u, new_v, new_history, rigid = pl.pallas_call(
        on_sphere,
        out_shape=(sds((3, 125, 2, 128)), sds((3, 125, 2, 128)), sds((189, 1, 128)), sds((8, 128))),
        in_specs=[hbm] * 4 + [smem, hbm, vmem, hbm, hbm, vmem] + [smem] * 3,
        out_specs=(hbm, hbm, hbm, vmem),
        scratch_shapes=[
            pltpu.VMEM(shape, jnp.float32)
            for shape in (
                (3, 125, 2, 128), (3, 125, 2, 128), (125, 2, 128), (125, 2, 128),
                state, state, state, state, state, (25, 8, 128), (200, 128),
                (128, 40, 128), (256, 16, 128), (40, 8, 128), (32, 128), (32, 128), (3, 8, 128), (3, 8, 128),
                (3, 256, 128), (384, 256), (5, 256, 128), (320, 128), (9, 8, 128), (STEPS + 2, 3, 8, 128),
                (STEPS, 512, 128), (STEPS, 256, 128),
            )
            + ((STEPS, 25, 8, 128),) * 2
            + ((STEPS, 13, 8, 128),) * 2
            + ((STEPS, 4, 3, 8, 128), (13, 8, 128), (13, 8, 128), (16, 8, 128), (16, 8, 128))
        ]
        + [
            sem((7,)), sem((4,)), sem((STEPS, 2, GROUP - 1)), sem((STEPS, 2, GROUP - 1)),
            sem((STEPS, 31)), sem((STEPS, 31)), sem((7,)), sem((7,)), sem((STEPS, 8)), sem((STEPS, 8)),
        ],
        compiler_params=pltpu.CompilerParams(
            collective_id=0, has_side_effects=True, vmem_limit_bytes=VMEM_BYTES
        ),
    )(
        displacement.reshape(3, 125, 2, 128), velocity.reshape(3, 125, 2, 128),
        rigidity.reshape(125, 2, 128), density.reshape(125, 2, 128), jnp.asarray(volume),
        history.transpose(1, 2, 0, 3).reshape(189, 1, 128), kernel.transpose(1, 2, 0, 3), jnp.asarray(legendre_table()), jnp.asarray(column_tables()),
        jnp.asarray(packed_tables()), owner_order, rigid_offset, rigid_velocity,
    )
    new_u, new_v, new_history, new_offset, new_speed = pl.pallas_call(
        hand_over,
        out_shape=(sds((3, 125, 2, 128)), sds((3, 125, 2, 128)), sds((189, 1, 128)), sds((3,)), sds((3,))),
        in_specs=[hbm, hbm, hbm, smem],
        out_specs=(hbm, hbm, hbm, smem, smem),
        scratch_shapes=[pltpu.VMEM(shape, jnp.float32) for shape in ((3, 125, 2, 128), (3, 125, 2, 128), (189, 1, 128))]
        + [sem((6,))],
        compiler_params=pltpu.CompilerParams(vmem_limit_bytes=VMEM_BYTES),
    )(new_u, new_v, new_history, rigid)
    shape = displacement.shape
    new_history = new_history.reshape(63, 3, 1, 128).transpose(2, 0, 1, 3)
    return new_u.reshape(shape), new_v.reshape(shape), new_history, new_offset, new_speed


def solution(mesh):
    split = Mesh(mesh.devices.reshape(4, 8, 2, 2, 2), AXES)
    field = P(None, None, None, None, BLK, LAT, None)
    scalar_field = P(None, None, None, BLK, LAT, None)
    owned = P(AXES, None, None, None)
    return jax.shard_map(
        on_device,
        mesh=split,
        in_specs=(field, field, scalar_field, scalar_field, owned, P(), P(), P(), P()),
        out_specs=(field, field, owned, P(), P()),
        check_vma=False,
    )
```

```python
import functools
import itertools
import math

import jax
import jax.numpy as jnp
import numpy as np
from jax import lax
from jax.experimental import pallas as pl
from jax.experimental.pallas import tpu as pltpu
from jax.sharding import Mesh
from jax.sharding import PartitionSpec as P

STEPS = 3
VMEM_BYTES = 60 * 1024 * 1024
AXES = ("x", "z", "ylo", "yhi", "core")
SIZES = {"x": 4, "z": 8, "ylo": 2, "yhi": 2, "core": 2}
BLK = ("x", "z", "ylo")
LAT = ("yhi", "core")
MESH_ID = pl.DeviceIdType.MESH
FIRST = ("core", "z")
SECOND = ("x", "ylo", "yhi")
GROUP = 16
PLANE = ("x", "ylo", "yhi", "core")

pole_gap = 0.1
time_step = 0.03
rigid_gain = 20.0
coupling = 1.0


def node_tables():
    points = np.array([-1.0, -math.sqrt(3.0 / 7.0), 0.0, math.sqrt(3.0 / 7.0), 1.0])
    weights = np.array([0.1, 49.0 / 90.0, 32.0 / 45.0, 49.0 / 90.0, 0.1])
    products = np.array(
        [np.prod([points[i] - points[j] for j in range(5) if j != i]) for i in range(5)]
    )
    slopes = np.zeros((5, 5))
    for i in range(5):
        for j in range(5):
            if i == j:
                slopes[i, j] = sum(1.0 / (points[i] - points[o]) for o in range(5) if o != i)
            else:
                slopes[i, j] = products[i] / products[j] / (points[i] - points[j])
    return points, weights, slopes


POINTS, WEIGHTS, SLOPES = node_tables()
THETA_STEP = (math.pi - 2.0 * pole_gap) / 8
PHI_STEP = 2.0 * math.pi / 64
THETA = pole_gap + (np.arange(8)[:, None] + 0.5 * (1.0 + POINTS)) * THETA_STEP
PHI = (np.arange(64)[:, None] + 0.5 * (1.0 + POINTS)) * PHI_STEP


def legendre_table():
    cosine, sine = np.cos(THETA).reshape(-1), np.sin(THETA).reshape(-1)
    table = np.zeros((128, 128, 40))
    diagonal = np.full(40, math.sqrt(0.5))
    for m in range(128):
        if m > 0:
            diagonal = diagonal * -math.sqrt((2 * m + 1) / (2 * m)) * sine
        table[m, m] = diagonal
        if m + 1 < 128:
            table[m, m + 1] = math.sqrt(2 * m + 3) * cosine * diagonal
        for l in range(m + 2, 128):
            up = math.sqrt((4.0 * l * l - 1) / (l * l - m * m))
            low = math.sqrt(((l - 1.0) ** 2 - m * m) / (4.0 * (l - 1.0) ** 2 - 1))
            table[m, l] = up * (cosine * table[m, l - 1] - low * table[m, l - 2])
    return table.transpose(0, 2, 1).astype(np.float32)


def circle_values():
    m = np.arange(128)
    angle = m[:, None, None] * PHI[None]
    cosines = np.cos(angle) / math.sqrt(math.pi)
    cosines[0] = 1.0 / math.sqrt(2.0 * math.pi)
    sines = np.sin(angle) / math.sqrt(math.pi)
    sines[0] = 0.0
    return np.concatenate((cosines, sines))


def rotations():
    st, ct = np.sin(THETA)[:, :, None, None], np.cos(THETA)[:, :, None, None]
    sp, cp = np.sin(PHI)[None, None], np.cos(PHI)[None, None]
    one, zero = np.ones((8, 5, 64, 5)), np.zeros((8, 5, 64, 5))
    return np.stack(
        [
            np.stack([st * cp, ct * cp, -sp * one]),
            np.stack([st * sp, ct * sp, cp * one]),
            np.stack([ct * one, -st * one, zero]),
        ]
    )


def areas():
    scale = 0.25 * THETA_STEP * PHI_STEP
    return scale * (WEIGHTS * np.sin(THETA))[:, :, None] * WEIGHTS


def pull_table():
    weighted = np.einsum("yba,jkybea,cea->cjkyb", areas(), rotations(), circle_values())
    table = np.zeros((256, 8, 4, 32))
    for k in range(3):
        for lat in range(4):
            for ey in range(2):
                at = (2 * k + ey) * 5
                table[:, :3, lat, at : at + 5] = weighted[:, :, k, 2 * lat + ey]
    return table.reshape(256, 8, 128).astype(np.float32)


def packed_tables():
    table = np.zeros((4, 3, 8, 128))
    area = areas()
    for lat in range(4):
        for r in range(6):
            for a in range(5):
                for b in range(5):
                    ey = r % 2
                    weight = area[2 * lat + ey, b, a]
                    table[lat, a // 4, r, 32 * (a % 4) + 5 * r + b] = weight
                    if r < 2:
                        copies = 2.0 if a in (0, 4) else 1.0
                        pole = (lat, ey, b) in ((0, 0, 0), (3, 1, 4))
                        copies *= 2.0 if b in (0, 4) and not pole else 1.0
                        face = coupling * WEIGHTS[a] * WEIGHTS[b] * copies
                        table[lat, 2, r, 32 + 10 * a + 5 * ey + b] = time_step**2 * weight * face
    return table.astype(np.float32)


def column_tables():
    table = np.zeros((256, 16, 128))
    e = np.arange(64)
    elem = ((e // 16) * 8 + e % 8) * 2 + e // 8 % 2
    m = np.arange(128)
    turn = m[:, None] * elem * PHI_STEP
    shift = m[:, None] * (0.5 * (1.0 + POINTS) * PHI_STEP)
    scale = np.full((128, 1), 1.0 / math.sqrt(math.pi))
    scale[0] = 1.0 / math.sqrt(2.0 * math.pi)
    real = np.ones((128, 1))
    real[0] = 0.0
    for kind in range(2):
        cols = slice(128 * kind, 128 * kind + 128)
        for pair in range(2):
            table[cols, 2 * pair, pair::2] = np.cos(turn)
            table[cols, 2 * pair + 1, pair::2] = np.sin(turn)
            for a in range(4) if pair == 0 else (4,):
                lanes = slice(32 * (a % 4), 32 * (a % 4) + 30)
                if kind == 0:
                    first, second = scale[:, 0] * np.cos(shift[:, a]), -scale[:, 0] * np.sin(shift[:, a])
                else:
                    first, second = (real * scale)[:, 0] * np.sin(shift[:, a]), (real * scale)[:, 0] * np.cos(shift[:, a])
                table[cols, 4 + 2 * pair, lanes] = first[:, None]
                table[cols, 5 + 2 * pair, lanes] = second[:, None]
    table[:, 8:11] = pull_table()[:, :3]
    circle = np.zeros((256, 384))
    circle[:, :320] = circle_values()[:, elem].transpose(0, 2, 1).reshape(256, 320)
    table[:, 11:14] = circle.reshape(256, 3, 128)
    return table.astype(np.float32)


def flat(axes, index):
    at = 0
    for axis in axes:
        at = at * SIZES[axis] + index[axis]
    return at


def unflat(axes, at):
    index = {}
    for axis in reversed(axes):
        index[axis] = at % SIZES[axis]
        at = at // SIZES[axis]
    return index


def partners(axes, me, shifts):
    count = math.prod(SIZES[axis] for axis in axes)
    mine = flat(axes, me)
    found = []
    for shift in shifts:
        other = {**me, **unflat(axes, lax.rem(mine + (shift + count), count))}
        found.append(tuple(other[axis] for axis in AXES))
    return found


def farthest_first(axes, me):
    shifts = []
    for shift in itertools.product(*(range(SIZES[axis]) for axis in axes)):
        by = dict(zip(axes, shift))
        hops = sum(min(by.get(axis, 0), SIZES[axis] - by.get(axis, 0)) for axis in ("x", "z"))
        hops += (0, 1, 2, 1)[2 * by.get("yhi", 0) + by.get("ylo", 0)]
        if any(shift):
            shifts.append((-hops, shift))
    found = []
    for hops, shift in sorted(shifts):
        other = {**me, **{axis: lax.rem(me[axis] + by, SIZES[axis]) for axis, by in zip(axes, shift)}}
        found.append(tuple(other[axis] for axis in AXES))
    return found


def on_sphere(
    u_in, v_in, rig_in, den_in, volume, hist_in, kern, leg_in, cols_in, packing, order, x_in, xv_in,
    u_out, v_out, hist_out, rigid_out,
    un, vn, rn, dn, u, v, wr, force, inv, face_force, hist, leg, cols, lp, e32, d32, q8, gown, gtt, ga, gsb, wi, past, coefs, g1, g2,
    lon_lo, lon_hi, lat_lo, lat_hi, edges, pack_up, pack_down, close_up, close_down,
    load_sem, store_sem, send1, recv1, send2, recv2, send_p, recv_p, send_h, recv_h,
):
    me = {axis: lax.axis_index(axis) for axis in AXES}
    lat, depth = flat(LAT, me), me["z"]
    near = farthest_first(FIRST, me)
    far = farthest_first(SECOND, me)
    plane = farthest_first(PLANE, me)
    column_mates = partners(("z",), me, range(1, 8))
    lon_next, lon_prev = partners(BLK, me, (1, -1))
    lat_next, lat_prev = partners(LAT, me, (1, -1))
    corners = [lon[:3] + colat[3:] for lon in (lon_next, lon_prev) for colat in (lat_next, lat_prev)]
    everyone = near + plane + [lon_next, lon_prev, lat_next, lat_prev] + corners
    barrier = pltpu.get_barrier_semaphore()
    for other in everyone:
        pl.semaphore_signal(barrier, inc=1, device_id=other, device_id_type=MESH_ID)

    loads = []

    def load(src, dst):
        copy = pltpu.make_async_copy(src, dst, load_sem.at[len(loads)])
        copy.start()
        loads.append(copy)

    load(u_in, un)
    load(rig_in, rn)
    load(den_in, dn)
    load(v_in, vn)
    hist[0:16] = jnp.zeros((16, 128), jnp.float32)
    load(hist_in.at[:, 0, :], hist.at[pl.ds(9, 189), :])
    load(cols_in, cols)
    load(leg_in, leg)

    lanes = lax.broadcasted_iota(jnp.int32, (8, 128), 1)
    subs = lax.broadcasted_iota(jnp.int32, (8, 128), 0)
    slant = lanes - 5 * subs
    even = subs % 2 == 0
    in_field = subs < 6
    slot_near, slot_far, slot_plane = flat(FIRST, me), flat(SECOND, me), flat(PLANE, me)
    mine = slot_far * GROUP + slot_near

    def send(src, dst, ssem, rsem, other):
        copy = pltpu.make_async_remote_copy(
            src_ref=src, dst_ref=dst, send_sem=ssem, recv_sem=rsem,
            device_id=other, device_id_type=MESH_ID,
        )
        copy.start()
        return copy

    def spread(at, stage):
        if stage == 0:
            start, count, others = mine * 2, 2, near
        else:
            start, count, others = slot_far * GROUP * 2, GROUP * 2, far
        block = g1.at[at, pl.ds(start, count), :]
        return [
            send(block, block, send1.at[at, stage, d], recv1.at[at, stage, d], other)
            for d, other in enumerate(others)
        ]

    def arrived(copies):
        for copy in copies:
            copy.wait_recv()

    unsent = []

    def copies_of(a, b):
        count = 2.0 if a in (0, 4) else 1.0
        if b == 0:
            return count * jnp.where(even & (lat == 0), 1.0, 2.0)
        if b == 4:
            return count * jnp.where((~even) & (lat == 3), 1.0, 2.0)
        return count

    def pack(value, first=None):
        packed = [jnp.zeros((8, 128), jnp.float32) for row in range(2)]
        for a in range(5):
            for b in range(5):
                node = jnp.broadcast_to(value(a, b)[:, 0:1], (8, 128))
                if first is None:
                    row, at = a // 4, 32 * (a % 4) + b
                else:
                    row, at = 0, first + 10 * a + b
                packed[row] = jnp.where(slant == at, node, packed[row])
        return packed

    def post(at, value, tail=None):
        packed = pack(value)
        rows = [packed[row] * packing[lat, row] for row in range(2)]
        if tail is not None:
            rows[1] = rows[1] + tail
        g1[at, pl.ds(2 * mine, 2), :] = jnp.concatenate(
            [jnp.sum(row, axis=0, keepdims=True) for row in rows], axis=0
        )
        copies = spread(at, 0)
        unsent.extend(copies)
        return copies

    def forward(at):
        copies = spread(at, 1)
        unsent.extend(copies)
        return copies

    def gradients(base, stride):
        values = [u[base + q * stride] for q in range(5)]
        weights = [wr[base + q * stride] for q in range(5)]
        grads = []
        for p in range(5):
            total = float(SLOPES[p, 0]) * values[0]
            for q in range(1, 5):
                total = total + float(SLOPES[p, q]) * values[q]
            grads.append(total * weights[p])
        return grads, weights

    def divergence(grads, q):
        total = float(SLOPES[0, q]) * grads[0]
        for p in range(1, 5):
            total = total + float(SLOPES[p, q]) * grads[p]
        return total

    def along(stride, base_of, first):
        def line(i, carry):
            base = base_of(i)
            grads, weights = gradients(base, stride)
            for q in range(5):
                total = divergence(grads, q)
                at = base + q * stride
                if first:
                    force[at] = jnp.where(in_field, -total, weights[q])
                else:
                    force[at] = force[at] - total
            return carry

        lax.fori_loop(0, 25, line, 0)

    def stiffness():
        along(25, lambda i: i, True)
        along(5, lambda i: (i // 5) * 25 + i % 5, False)
        along(1, lambda i: i * 5, False)

    def join_radial():
        for i in range(25):
            low, high = force[i * 5], force[i * 5 + 4]
            force[i * 5] = low + jnp.where(lanes == 0, 0.0, pltpu.roll(high, 1, 1))
            force[i * 5 + 4] = high + jnp.where(lanes == 127, 0.0, pltpu.roll(low, 127, 1))

    pairs = [(n, 2 * n, min(2 * n + 1, 24)) for n in range(13)]
    not_last, not_first = lat < 3, lat > 0

    def close_pack(base, packed):
        last = jnp.zeros((8, 128), jnp.float32)
        for b in range(5):
            third = force[base + 5 * b + 3]
            for c in range(3):
                packed[3 * b + c] = jnp.where(in_field, force[base + 5 * b + c], pltpu.roll(third, 6 - 2 * c, 0))
            last = jnp.where(lanes == b, jnp.broadcast_to(force[base + 5 * b + 4][:, 127:128], (8, 128)), last)
        packed[15] = last

    def close_add(base, packed):
        last = packed[15]
        for b in range(5):
            parts = [packed[3 * b + c] for c in range(3)]
            third = jnp.where(subs < 2, pltpu.roll(parts[0], 2, 0), pltpu.roll(parts[1], 4, 0))
            third = jnp.where(subs < 4, third, pltpu.roll(parts[2], 6, 0))
            end = jnp.where(lanes == 127, last[:, b : b + 1], pltpu.roll(parts[0], 127, 1))
            for c, part in enumerate(parts + [third, end]):
                at = base + 5 * b + c
                force[at] = force[at] + jnp.where(in_field, part, 0.0)

    def halo_out(step):
        if step == 0:
            faces = [force.at[pl.ds(100, 25)], force.at[pl.ds(0, 25)]]
            into = [lon_lo.at[0], lon_hi.at[0]]
        else:
            close_pack(100, close_up)
            close_pack(0, close_down)
            faces = [close_up, close_down]
            into = [lon_lo.at[step, pl.ds(0, 16)], lon_hi.at[step, pl.ds(0, 16)]]
        lon_copies = [
            send(faces[n], into[n], send_h.at[step, n], recv_h.at[step, n], other)
            for n, other in enumerate((lon_next, lon_prev))
        ]
        for n, one, two in pairs:
            up = [force[25 * (x // 5) + 20 + x % 5] for x in (one, two)]
            down = [force[25 * (x // 5) + x % 5] for x in (one, two)]
            pack_up[n] = jnp.where(even, pltpu.roll(up[1], 7, 0), up[0])
            pack_down[n] = jnp.where(even, down[0], pltpu.roll(down[1], 1, 0))

        def moves(packed, face, beside, edge):
            return [
                pltpu.make_async_remote_copy(
                    src_ref=packed.at[pl.ds(start, count)], dst_ref=dst, send_sem=send_h.at[step, at],
                    recv_sem=recv_h.at[step, at], device_id=other, device_id_type=MESH_ID,
                )
                for start, count, dst, at, other in (
                    (0, 13, face.at[step], 2 + edge, beside),
                    (10, 3, edges.at[step, edge], 4 + edge, corners[edge]),
                    (0, 3, edges.at[step, 2 + edge], 6 + edge, corners[2 + edge]),
                )
            ]

        rising = moves(pack_up, lat_lo, lat_next, 0)
        falling = moves(pack_down, lat_hi, lat_prev, 1)

        @pl.when(not_last)
        def _():
            for copy in rising:
                copy.start()

        @pl.when(not_first)
        def _():
            for copy in falling:
                copy.start()

        return lon_copies, rising, falling

    def halo_in(step, copies):
        lon_copies, rising, falling = copies
        for copy in lon_copies:
            copy.wait()

        @pl.when(not_last)
        def _():
            for copy in rising:
                copy.wait_send()
            for copy in falling:
                copy.wait_recv()

        @pl.when(not_first)
        def _():
            for copy in falling:
                copy.wait_send()
            for copy in rising:
                copy.wait_recv()

        if step == 0:
            force[0:25] = force[0:25] + lon_lo[0]
            force[100:125] = force[100:125] + lon_hi[0]
        else:
            close_add(0, lon_lo.at[step])
            close_add(100, lon_hi.at[step])
        for n, one, two in pairs:
            below, above = lat_lo[step, n], lat_hi[step, n]
            if n <= 2:
                first, second = edges[step, 0, n], edges[step, 1, n]
                if n == 2:
                    first, second = jnp.where(even, 0.0, first), jnp.where(even, second, 0.0)
                below, above = below + first, above + second
            if n >= 10:
                below, above = below + edges[step, 2, n - 10], above + edges[step, 3, n - 10]
            below = jnp.where(not_first, below, 0.0)
            above = jnp.where(not_last, above, 0.0)
            for x, part_below, part_above in (
                (one, pltpu.roll(below, 7, 0), pltpu.roll(above, 1, 0)),
                (two, below, above),
            )[: 1 if one == two else 2]:
                low, high = force[25 * (x // 5) + x % 5], force[25 * (x // 5) + 20 + x % 5]
                force[25 * (x // 5) + x % 5] = low + jnp.where(even, part_below, pltpu.roll(high, 1, 0))
                force[25 * (x // 5) + 20 + x % 5] = high + jnp.where(even, pltpu.roll(low, 7, 0), part_above)

    def node_step(i):
        speed_now = jnp.where(in_field, v[i] + time_step * (force[i] * inv[i]), 0.0)
        v[i] = speed_now
        u[i] = u[i] + time_step * speed_now

    def inside(body):
        def line(t, carry):
            for c in range(5):
                body(25 * (1 + t // 3) + 5 * (1 + t % 3) + c)
            return carry

        lax.fori_loop(0, 9, line, 0)

    def around(body):
        def ends(t, carry):
            for c in range(5):
                body(5 * t + c)
                body(100 + 5 * t + c)
            return carry

        def middle(t, carry):
            for c in range(5):
                body(25 * t + c)
                body(25 * t + 20 + c)
            return carry

        lax.fori_loop(0, 5, ends, 0)
        lax.fori_loop(1, 4, middle, 0)

    def predicted(a, b):
        i = a * 5 + b
        push = (time_step**2 * copies_of(a, b)) * (inv[i * 5] * face_force[i])
        return u[i * 5] + time_step * v[i * 5] + push

    def analysed(at):
        field = g1[at].reshape(8, 4, 16, 128)
        field = jnp.concatenate([field[:, i].reshape(128, 128) for i in range(4)], axis=1)
        sums = jnp.dot(e32[...], field, precision=lax.Precision.HIGHEST, preferred_element_type=jnp.float32)
        result = jnp.zeros((8, 128), jnp.float32)
        for i in range(4):
            part = d32[0:8] * sums[0:8, 128 * i : 128 * i + 128]
            for q in range(1, 4):
                part = part + d32[8 * q : 8 * q + 8] * sums[8 * q : 8 * q + 8, 128 * i : 128 * i + 128]
            part = part + pltpu.roll(part, 64, 1)
            part = part + pltpu.roll(part, 32, 1)
            result = jnp.where(lanes // 32 == i, part, result)
        return result

    def owners(step, sums, offset):
        for j in range(3):
            sums = sums - offset[j] * q8[j]
        found = [jnp.zeros((8, 128), jnp.float32) for k in range(3)]
        for t in range(40):
            block = lp[t]
            for k in range(3):
                lane = (t // 10) * 32 + (2 * k + t // 5 % 2) * 5 + t % 5
                found[k] = found[k] + sums[:, lane : lane + 1] * block
        replies = []
        for k in range(3):
            coefs[step + 2, k] = found[k]
            row = jnp.sum(jnp.where(subs == depth, found[k], 0.0), axis=0, keepdims=True)
            hist[3 * (STEPS - 1 - step) + k : 3 * (STEPS - 1 - step) + k + 1] = row
        for k in range(3):
            reply = past[3 * step + k]
            for i in range(3):
                reply = reply + kern[k, i, 0:1] * found[i]
                for back in range(1, step + 1):
                    reply = reply + kern[k, i, back : back + 1] * coefs[step + 2 - back, i]
            replies.append(reply)
        message = jnp.zeros((8, 128), jnp.float32)
        for t in range(40):
            block = lp[t]
            for k in range(3):
                lane = (t // 10) * 32 + (2 * k + t // 5 % 2) * 5 + t % 5
                value = jnp.sum(block * replies[k], axis=1, keepdims=True)
                message = jnp.where(lanes == lane, value, message)
        pulls = [jnp.sum(message * q8[j], axis=1, keepdims=True) for j in range(3)]
        for j, lane in enumerate((30, 31, 62)):
            message = jnp.where(lanes == lane, pulls[j], message)
        block = g2.at[step, pl.ds(8 * slot_plane, 8), :]
        g2[step, pl.ds(8 * slot_plane, 8), :] = message
        copies = [send(block, block, send2.at[step, d], recv2.at[step, d], other) for d, other in enumerate(plane)]
        unsent.extend(copies)
        return copies

    def rigid_step(step, offset, speed):
        whole = jnp.sum(g2[step], axis=0, keepdims=True)
        lane_row = lax.broadcasted_iota(jnp.int32, (1, 128), 1)
        new_offset, new_speed = [], []
        for j, lane in enumerate((30, 31, 62)):
            pull = jnp.sum(jnp.where(lane_row == lane, whole, 0.0), axis=1, keepdims=True)
            new_speed.append(speed[j] + time_step * rigid_gain * pull)
            new_offset.append(offset[j] + time_step * new_speed[j])
        return new_offset, new_speed

    def add_traction(step, shared_moved=True):
        field = g2[step]
        edge = lanes == 0
        for a in range(5):
            row = jnp.sum(field * gsb[a], axis=0, keepdims=True)
            for b in range(5):
                here = (slant == 32 * lat + b) & in_field
                traction = jnp.sum(jnp.where(here, row, 0.0), axis=1, keepdims=True)
                face = float(coupling * WEIGHTS[a] * WEIGHTS[b]) * copies_of(a, b)
                i = (a * 5 + b) * 5
                gain = jnp.where(edge, time_step * (traction * face) * inv[i], 0.0)
                v[i] = v[i] - gain
                if shared_moved or (0 < a < 4 and 0 < b < 4):
                    u[i] = u[i] - time_step * gain

    def moved(step):
        total = jnp.zeros((8, 128), jnp.float32)
        for q, (start, count) in enumerate(((0, 128), (128, 128), (256, 64))):
            traction = jnp.dot(
                ga[start : start + count], g2[step], precision=lax.Precision.HIGHEST,
                preferred_element_type=jnp.float32,
            )
            total = total + jnp.dot(
                gown[q, :, 0:count], traction * wi[start : start + count], precision=lax.Precision.HIGHEST,
                preferred_element_type=jnp.float32,
            )
        return total

    none = jnp.zeros((2, 128), jnp.float32)

    def stacked(field, i):
        return jnp.concatenate([field[0, i], field[1, i], field[2, i], none], axis=0)

    def by_fives(body):
        def five(t, carry):
            for i in range(5):
                body(5 * t + i)
            return carry

        lax.fori_loop(0, 25, five, 0)

    for copy in loads[0:3]:
        copy.wait()

    def stack_state(i):
        u[i] = stacked(un, i)
        wr[i] = jnp.concatenate([rn[i], rn[i], rn[i], dn[i]], axis=0) * volume[i]

    by_fives(stack_state)
    packed_start = pack(lambda a, b: u[(a * 5 + b) * 5])
    rows = [packed_start[row] * packing[lat, row] for row in range(2)]
    g1[0, pl.ds(2 * mine, 2), :] = jnp.concatenate([jnp.sum(row, axis=0, keepdims=True) for row in rows], axis=0)
    stiffness()
    for i in range(25):
        face_force[i] = force[i * 5]
    join_radial()

    loads[4].wait()
    for step in range(STEPS):
        old = [hist[pl.ds(6 - 3 * step + i, 64, 3), :] for i in range(3)]
        for k in range(3):
            total = sum(kern[k, i] * old[i] for i in range(3))
            past[3 * step + k, pl.ds(depth, 1), :] = jnp.sum(total, axis=0, keepdims=True)

    loads[5].wait()
    base = (me["x"] * 16 + me["ylo"]) * 4 + lat
    own = [order[base + 8 * i] for i in range(8)]
    for i in range(8):
        for q in range(4):
            e32[8 * q + i : 8 * q + i + 1] = cols[own[i], q : q + 1]
            d32[8 * q + i : 8 * q + i + 1] = cols[own[i], 4 + q : 5 + q]
        for q in range(3):
            q8[q, i : i + 1] = cols[own[i], 8 + q : 9 + q]
            gown[q, i : i + 1] = cols[own[i], 11 + q : 12 + q]

    def circle_rows(t, carry):
        for i in range(8):
            column = order[((t // 8) * 16 + i * 2 + t // 4 % 2) * 4 + t % 4]
            for q in range(3):
                gtt[q, pl.ds(8 * t + i, 1), :] = cols[column, 11 + q : 12 + q]
        return carry

    lax.fori_loop(0, 32, circle_rows, 0)
    loads[6].wait()

    def take(t, carry):
        for i in range(8):
            lp[t, i : i + 1] = leg[lax.rem(own[i], 128), pl.ds(t, 1), :]
        return carry

    lax.fori_loop(0, 40, take, 0)
    many = lax.broadcasted_iota(jnp.int32, (256, 128), 1)
    elem = (me["x"] * 2 + me["ylo"]) * 8 + depth
    for a in range(5):
        picked = jnp.where(many == elem + 64 * (a % 2), gtt[a // 2], 0.0)
        gsb[a] = jnp.broadcast_to(jnp.sum(picked, axis=1, keepdims=True), (256, 128))
    for q in range(3):
        ga[128 * q : 128 * q + 128] = jnp.transpose(gtt[q])
    loads[3].wait()

    def stack_speed(i):
        v[i] = stacked(vn, i)

    by_fives(stack_speed)
    offset = [jnp.full((1, 1), x_in[j], jnp.float32) for j in range(3)]
    speed = [jnp.full((1, 1), xv_in[j], jnp.float32) for j in range(3)]

    pl.semaphore_wait(barrier, len(everyone))
    wave0 = spread(0, 0)
    halo = halo_out(0)
    own_past = past.at[:, pl.ds(depth, 1), :]
    wave_past = [
        send(own_past, own_past, send_p.at[d], recv_p.at[d], other) for d, other in enumerate(column_mates)
    ]
    unsent.extend(wave0)
    unsent.extend(wave_past)
    stores = [pltpu.make_async_copy(hist.at[pl.ds(9, 180), :], hist_out.at[pl.ds(9, 180), 0, :], store_sem.at[2])]
    stores[0].start()

    arrived(wave0)
    wave0 = forward(0)
    halo_in(0, halo)

    def invert(i):
        mass = force[i]
        inv[i] = 1.0 / jnp.where(even, mass[6:7], mass[7:8])

    def invert_column(i, carry):
        for b in range(5):
            invert(25 * i + 5 * b)
        return carry

    lax.fori_loop(0, 5, invert_column, 0)
    tail = pack(lambda a, b: inv[(a * 5 + b) * 5], 32)[0] * packing[lat, 2]
    wave1 = post(1, predicted, tail)
    arrived(wave_past)
    by_fives(invert)
    arrived(wave0)
    replies0 = owners(0, analysed(0), offset)
    arrived(wave1)
    wave1 = forward(1)
    by_fives(node_step)
    arrived(replies0)
    add_traction(0)
    offset, speed = rigid_step(0, offset, speed)

    stiffness()
    for i in range(25):
        face_force[i] = force[i * 5]
    join_radial()
    halo = halo_out(1)
    wave2 = post(2, predicted)
    arrived(wave1)
    factors = g1[1, pl.ds(1, 256, 2), :].reshape(8, 4, 8, 128)
    wide = lax.broadcasted_iota(jnp.int32, (64, 128), 1)
    for a in range(5):
        total = jnp.zeros((64, 128), jnp.float32)
        for i in range(4):
            block = factors[:, i].reshape(64, 128)
            for k in range(3):
                start = 32 * i + 10 * k
                turned = pltpu.roll(block, (start - 32 - 10 * a) % 128, 1)
                total = jnp.where((wide >= start) & (wide < start + 10), turned, total)
        wi[64 * a : 64 * a + 64] = total
    replies1 = owners(1, analysed(1) - moved(0), offset)
    arrived(wave2)
    wave2 = forward(2)
    inside(node_step)
    halo_in(1, halo)
    around(node_step)
    arrived(replies1)
    add_traction(1)
    offset, speed = rigid_step(1, offset, speed)

    stiffness()
    join_radial()
    halo = halo_out(2)
    shift = moved(1)
    arrived(wave2)
    replies2 = owners(2, analysed(2) - shift, offset)
    inside(node_step)
    arrived(replies2)
    add_traction(2, shared_moved=False)
    offset, speed = rigid_step(2, offset, speed)

    def unstack(i):
        place, speed_now = u[i], v[i]
        for k in range(3):
            un[k, i] = place[2 * k : 2 * k + 2]
            vn[k, i] = speed_now[2 * k : 2 * k + 2]

    inside(unstack)
    halo_in(2, halo)

    def last_step(i):
        node_step(i)
        unstack(i)

    around(last_step)
    stores.append(pltpu.make_async_copy(hist.at[pl.ds(0, 9), :], hist_out.at[pl.ds(0, 9), 0, :], store_sem.at[3]))
    stores[1].start()
    for n, (src, dst) in enumerate(((un, u_out), (vn, v_out))):
        copy = pltpu.make_async_copy(src, dst, store_sem.at[n])
        copy.start()
        stores.append(copy)
    for j in range(3):
        rigid_out[j : j + 1] = jnp.broadcast_to(offset[j], (1, 128))
        rigid_out[3 + j : 4 + j] = jnp.broadcast_to(speed[j], (1, 128))
    rigid_out[6:8] = jnp.zeros((2, 128), jnp.float32)
    for copy in unsent:
        copy.wait_send()
    for copy in stores:
        copy.wait()


def hand_over(u_in, v_in, hist_in, rigid_in, u_out, v_out, hist_out, x_out, xv_out, u, v, hist, sems):
    held = ((u_in, u, u_out), (v_in, v, v_out), (hist_in, hist, hist_out))
    arriving = [pltpu.make_async_copy(src, mid, sems.at[n]) for n, (src, mid, dst) in enumerate(held)]
    leaving = [pltpu.make_async_copy(mid, dst, sems.at[3 + n]) for n, (src, mid, dst) in enumerate(held)]
    for copy in arriving:
        copy.start()
    for j in range(3):
        x_out[j] = rigid_in[j, 0]
        xv_out[j] = rigid_in[3 + j, 0]
    for first, second in zip(arriving, leaving):
        first.wait()
        second.start()
    for copy in leaving:
        copy.wait()


def on_device(
    displacement, velocity, rigidity, density, history, kernel, owner_order, rigid_offset, rigid_velocity
):
    volume = (WEIGHTS[:, None, None] * WEIGHTS[:, None] * WEIGHTS).reshape(125).astype(np.float32)
    vmem = pl.BlockSpec(memory_space=pltpu.VMEM)
    smem = pl.BlockSpec(memory_space=pltpu.SMEM)
    hbm = pl.BlockSpec(memory_space=pl.ANY)
    sds = functools.partial(jax.ShapeDtypeStruct, dtype=jnp.float32)
    state = (125, 8, 128)
    sem = pltpu.SemaphoreType.DMA
    new_u, new_v, new_history, rigid = pl.pallas_call(
        on_sphere,
        out_shape=(sds((3, 125, 2, 128)), sds((3, 125, 2, 128)), sds((189, 1, 128)), sds((8, 128))),
        in_specs=[hbm] * 4 + [smem, hbm, vmem, hbm, hbm, vmem] + [smem] * 3,
        out_specs=(hbm, hbm, hbm, vmem),
        scratch_shapes=[
            pltpu.VMEM(shape, jnp.float32)
            for shape in (
                (3, 125, 2, 128), (3, 125, 2, 128), (125, 2, 128), (125, 2, 128),
                state, state, state, state, state, (25, 8, 128), (200, 128),
                (128, 40, 128), (256, 16, 128), (40, 8, 128), (32, 128), (32, 128), (3, 8, 128), (3, 8, 128),
                (3, 256, 128), (384, 256), (5, 256, 128), (320, 128), (9, 8, 128), (STEPS + 2, 3, 8, 128),
                (STEPS, 512, 128), (STEPS, 256, 128),
            )
            + ((STEPS, 25, 8, 128),) * 2
            + ((STEPS, 13, 8, 128),) * 2
            + ((STEPS, 4, 3, 8, 128), (13, 8, 128), (13, 8, 128), (16, 8, 128), (16, 8, 128))
        ]
        + [
            sem((7,)), sem((4,)), sem((STEPS, 2, GROUP - 1)), sem((STEPS, 2, GROUP - 1)),
            sem((STEPS, 31)), sem((STEPS, 31)), sem((7,)), sem((7,)), sem((STEPS, 8)), sem((STEPS, 8)),
        ],
        compiler_params=pltpu.CompilerParams(
            collective_id=0, has_side_effects=True, vmem_limit_bytes=VMEM_BYTES
        ),
    )(
        displacement.reshape(3, 125, 2, 128), velocity.reshape(3, 125, 2, 128),
        rigidity.reshape(125, 2, 128), density.reshape(125, 2, 128), jnp.asarray(volume),
        history.transpose(1, 2, 0, 3).reshape(189, 1, 128), kernel.transpose(1, 2, 0, 3), jnp.asarray(legendre_table()), jnp.asarray(column_tables()),
        jnp.asarray(packed_tables()), owner_order, rigid_offset, rigid_velocity,
    )
    new_u, new_v, new_history, new_offset, new_speed = pl.pallas_call(
        hand_over,
        out_shape=(sds((3, 125, 2, 128)), sds((3, 125, 2, 128)), sds((189, 1, 128)), sds((3,)), sds((3,))),
        in_specs=[hbm, hbm, hbm, smem],
        out_specs=(hbm, hbm, hbm, smem, smem),
        scratch_shapes=[pltpu.VMEM(shape, jnp.float32) for shape in ((3, 125, 2, 128), (3, 125, 2, 128), (189, 1, 128))]
        + [sem((6,))],
        compiler_params=pltpu.CompilerParams(vmem_limit_bytes=VMEM_BYTES),
    )(new_u, new_v, new_history, rigid)
    shape = displacement.shape
    new_history = new_history.reshape(63, 3, 1, 128).transpose(2, 0, 1, 3)
    return new_u.reshape(shape), new_v.reshape(shape), new_history, new_offset, new_speed


def solution(mesh):
    split = Mesh(mesh.devices.reshape(4, 8, 2, 2, 2), AXES)
    field = P(None, None, None, None, BLK, LAT, None)
    scalar_field = P(None, None, None, BLK, LAT, None)
    owned = P(AXES, None, None, None)
    return jax.shard_map(
        on_device,
        mesh=split,
        in_specs=(field, field, scalar_field, scalar_field, owned, P(), P(), P(), P()),
        out_specs=(field, field, owned, P(), P()),
        check_vma=False,
    )
```

```python
import functools
import itertools
import math

import jax
import jax.numpy as jnp
import numpy as np
from jax import lax
from jax.experimental import pallas as pl
from jax.experimental.pallas import tpu as pltpu
from jax.sharding import Mesh
from jax.sharding import PartitionSpec as P

STEPS = 3
VMEM_BYTES = 60 * 1024 * 1024
AXES = ("x", "z", "ylo", "yhi", "core")
SIZES = {"x": 4, "z": 8, "ylo": 2, "yhi": 2, "core": 2}
BLK = ("x", "z", "ylo")
LAT = ("yhi", "core")
MESH_ID = pl.DeviceIdType.MESH
FIRST = ("core", "z")
SECOND = ("x", "ylo", "yhi")
GROUP = 16
PLANE = ("x", "ylo", "yhi", "core")

pole_gap = 0.1
time_step = 0.03
rigid_gain = 20.0
coupling = 1.0


def node_tables():
    points = np.array([-1.0, -math.sqrt(3.0 / 7.0), 0.0, math.sqrt(3.0 / 7.0), 1.0])
    weights = np.array([0.1, 49.0 / 90.0, 32.0 / 45.0, 49.0 / 90.0, 0.1])
    products = np.array(
        [np.prod([points[i] - points[j] for j in range(5) if j != i]) for i in range(5)]
    )
    slopes = np.zeros((5, 5))
    for i in range(5):
        for j in range(5):
            if i == j:
                slopes[i, j] = sum(1.0 / (points[i] - points[o]) for o in range(5) if o != i)
            else:
                slopes[i, j] = products[i] / products[j] / (points[i] - points[j])
    return points, weights, slopes


POINTS, WEIGHTS, SLOPES = node_tables()
THETA_STEP = (math.pi - 2.0 * pole_gap) / 8
PHI_STEP = 2.0 * math.pi / 64
THETA = pole_gap + (np.arange(8)[:, None] + 0.5 * (1.0 + POINTS)) * THETA_STEP
PHI = (np.arange(64)[:, None] + 0.5 * (1.0 + POINTS)) * PHI_STEP


def legendre_table():
    cosine, sine = np.cos(THETA).reshape(-1), np.sin(THETA).reshape(-1)
    table = np.zeros((128, 128, 40))
    diagonal = np.full(40, math.sqrt(0.5))
    for m in range(128):
        if m > 0:
            diagonal = diagonal * -math.sqrt((2 * m + 1) / (2 * m)) * sine
        table[m, m] = diagonal
        if m + 1 < 128:
            table[m, m + 1] = math.sqrt(2 * m + 3) * cosine * diagonal
        for l in range(m + 2, 128):
            up = math.sqrt((4.0 * l * l - 1) / (l * l - m * m))
            low = math.sqrt(((l - 1.0) ** 2 - m * m) / (4.0 * (l - 1.0) ** 2 - 1))
            table[m, l] = up * (cosine * table[m, l - 1] - low * table[m, l - 2])
    return table.transpose(0, 2, 1).astype(np.float32)


def circle_values():
    m = np.arange(128)
    angle = m[:, None, None] * PHI[None]
    cosines = np.cos(angle) / math.sqrt(math.pi)
    cosines[0] = 1.0 / math.sqrt(2.0 * math.pi)
    sines = np.sin(angle) / math.sqrt(math.pi)
    sines[0] = 0.0
    return np.concatenate((cosines, sines))


def rotations():
    st, ct = np.sin(THETA)[:, :, None, None], np.cos(THETA)[:, :, None, None]
    sp, cp = np.sin(PHI)[None, None], np.cos(PHI)[None, None]
    one, zero = np.ones((8, 5, 64, 5)), np.zeros((8, 5, 64, 5))
    return np.stack(
        [
            np.stack([st * cp, ct * cp, -sp * one]),
            np.stack([st * sp, ct * sp, cp * one]),
            np.stack([ct * one, -st * one, zero]),
        ]
    )


def areas():
    scale = 0.25 * THETA_STEP * PHI_STEP
    return scale * (WEIGHTS * np.sin(THETA))[:, :, None] * WEIGHTS


def pull_table():
    weighted = np.einsum("yba,jkybea,cea->cjkyb", areas(), rotations(), circle_values())
    table = np.zeros((256, 8, 4, 32))
    for k in range(3):
        for lat in range(4):
            for ey in range(2):
                at = (2 * k + ey) * 5
                table[:, :3, lat, at : at + 5] = weighted[:, :, k, 2 * lat + ey]
    return table.reshape(256, 8, 128).astype(np.float32)


def packed_tables():
    table = np.zeros((4, 3, 8, 128))
    area = areas()
    for lat in range(4):
        for r in range(6):
            for a in range(5):
                for b in range(5):
                    ey = r % 2
                    weight = area[2 * lat + ey, b, a]
                    table[lat, a // 4, r, 32 * (a % 4) + 5 * r + b] = weight
                    if r < 2:
                        copies = 2.0 if a in (0, 4) else 1.0
                        pole = (lat, ey, b) in ((0, 0, 0), (3, 1, 4))
                        copies *= 2.0 if b in (0, 4) and not pole else 1.0
                        face = coupling * WEIGHTS[a] * WEIGHTS[b] * copies
                        table[lat, 2, r, 32 + 10 * a + 5 * ey + b] = time_step**2 * weight * face
    return table.astype(np.float32)


def column_tables():
    table = np.zeros((256, 16, 128))
    e = np.arange(64)
    elem = ((e // 16) * 8 + e % 8) * 2 + e // 8 % 2
    m = np.arange(128)
    turn = m[:, None] * elem * PHI_STEP
    shift = m[:, None] * (0.5 * (1.0 + POINTS) * PHI_STEP)
    scale = np.full((128, 1), 1.0 / math.sqrt(math.pi))
    scale[0] = 1.0 / math.sqrt(2.0 * math.pi)
    real = np.ones((128, 1))
    real[0] = 0.0
    for kind in range(2):
        cols = slice(128 * kind, 128 * kind + 128)
        for pair in range(2):
            table[cols, 2 * pair, pair::2] = np.cos(turn)
            table[cols, 2 * pair + 1, pair::2] = np.sin(turn)
            for a in range(4) if pair == 0 else (4,):
                lanes = slice(32 * (a % 4), 32 * (a % 4) + 30)
                if kind == 0:
                    first, second = scale[:, 0] * np.cos(shift[:, a]), -scale[:, 0] * np.sin(shift[:, a])
                else:
                    first, second = (real * scale)[:, 0] * np.sin(shift[:, a]), (real * scale)[:, 0] * np.cos(shift[:, a])
                table[cols, 4 + 2 * pair, lanes] = first[:, None]
                table[cols, 5 + 2 * pair, lanes] = second[:, None]
    table[:, 8:11] = pull_table()[:, :3]
    circle = np.zeros((256, 384))
    circle[:, :320] = circle_values()[:, elem].transpose(0, 2, 1).reshape(256, 320)
    table[:, 11:14] = circle.reshape(256, 3, 128)
    return table.astype(np.float32)


def flat(axes, index):
    at = 0
    for axis in axes:
        at = at * SIZES[axis] + index[axis]
    return at


def unflat(axes, at):
    index = {}
    for axis in reversed(axes):
        index[axis] = at % SIZES[axis]
        at = at // SIZES[axis]
    return index


def partners(axes, me, shifts):
    count = math.prod(SIZES[axis] for axis in axes)
    mine = flat(axes, me)
    found = []
    for shift in shifts:
        other = {**me, **unflat(axes, lax.rem(mine + (shift + count), count))}
        found.append(tuple(other[axis] for axis in AXES))
    return found


def farthest_first(axes, me):
    shifts = []
    for shift in itertools.product(*(range(SIZES[axis]) for axis in axes)):
        by = dict(zip(axes, shift))
        hops = sum(min(by.get(axis, 0), SIZES[axis] - by.get(axis, 0)) for axis in ("x", "z"))
        hops += (0, 1, 2, 1)[2 * by.get("yhi", 0) + by.get("ylo", 0)]
        if any(shift):
            shifts.append((-hops, shift))
    found = []
    for hops, shift in sorted(shifts):
        other = {**me, **{axis: lax.rem(me[axis] + by, SIZES[axis]) for axis, by in zip(axes, shift)}}
        found.append(tuple(other[axis] for axis in AXES))
    return found


def on_sphere(
    u_in, v_in, rig_in, den_in, volume, hist_in, kern, leg_in, cols_in, packing, order, x_in, xv_in,
    u_out, v_out, hist_out, rigid_out,
    un, vn, rn, dn, u, v, wr, force, inv, face_force, hist, leg, cols, lp, e32, d32, q8, gown, gtt, ga, gsb, wi, past, coefs, g1, g2,
    lon_lo, lon_hi, lat_lo, lat_hi, edges, pack_up, pack_down, close_up, close_down,
    load_sem, store_sem, send1, recv1, send2, recv2, send_p, recv_p, send_h, recv_h,
):
    me = {axis: lax.axis_index(axis) for axis in AXES}
    lat, depth = flat(LAT, me), me["z"]
    near = farthest_first(FIRST, me)
    far = farthest_first(SECOND, me)
    plane = farthest_first(PLANE, me)
    column_mates = partners(("z",), me, range(1, 8))
    lon_next, lon_prev = partners(BLK, me, (1, -1))
    lat_next, lat_prev = partners(LAT, me, (1, -1))
    corners = [lon[:3] + colat[3:] for lon in (lon_next, lon_prev) for colat in (lat_next, lat_prev)]
    everyone = corners + [lon_next, lon_prev, lat_next, lat_prev] + plane + near
    barrier = pltpu.get_barrier_semaphore()
    for other in everyone:
        pl.semaphore_signal(barrier, inc=1, device_id=other, device_id_type=MESH_ID)

    loads = []

    def load(src, dst):
        copy = pltpu.make_async_copy(src, dst, load_sem.at[len(loads)])
        copy.start()
        loads.append(copy)

    load(u_in, un)
    load(rig_in, rn)
    load(den_in, dn)
    load(v_in, vn)
    hist[0:16] = jnp.zeros((16, 128), jnp.float32)
    load(hist_in.at[:, 0, :], hist.at[pl.ds(9, 189), :])
    load(cols_in, cols)
    load(leg_in, leg)

    lanes = lax.broadcasted_iota(jnp.int32, (8, 128), 1)
    subs = lax.broadcasted_iota(jnp.int32, (8, 128), 0)
    slant = lanes - 5 * subs
    even = subs % 2 == 0
    in_field = subs < 6
    slot_near, slot_far, slot_plane = flat(FIRST, me), flat(SECOND, me), flat(PLANE, me)
    mine = slot_far * GROUP + slot_near

    def send(src, dst, ssem, rsem, other):
        copy = pltpu.make_async_remote_copy(
            src_ref=src, dst_ref=dst, send_sem=ssem, recv_sem=rsem,
            device_id=other, device_id_type=MESH_ID,
        )
        copy.start()
        return copy

    def spread(at, stage):
        if stage == 0:
            start, count, others = mine * 2, 2, near
        else:
            start, count, others = slot_far * GROUP * 2, GROUP * 2, far
        block = g1.at[at, pl.ds(start, count), :]
        return [
            send(block, block, send1.at[at, stage, d], recv1.at[at, stage, d], other)
            for d, other in enumerate(others)
        ]

    def arrived(copies):
        for copy in copies:
            copy.wait_recv()

    unsent = []

    def copies_of(a, b):
        count = 2.0 if a in (0, 4) else 1.0
        if b == 0:
            return count * jnp.where(even & (lat == 0), 1.0, 2.0)
        if b == 4:
            return count * jnp.where((~even) & (lat == 3), 1.0, 2.0)
        return count

    def pack(value, first=None):
        packed = [jnp.zeros((8, 128), jnp.float32) for row in range(2)]
        for a in range(5):
            for b in range(5):
                node = jnp.broadcast_to(value(a, b)[:, 0:1], (8, 128))
                if first is None:
                    row, at = a // 4, 32 * (a % 4) + b
                else:
                    row, at = 0, first + 10 * a + b
                packed[row] = jnp.where(slant == at, node, packed[row])
        return packed

    def post(at, value, tail=None):
        packed = pack(value)
        rows = [packed[row] * packing[lat, row] for row in range(2)]
        if tail is not None:
            rows[1] = rows[1] + tail
        g1[at, pl.ds(2 * mine, 2), :] = jnp.concatenate(
            [jnp.sum(row, axis=0, keepdims=True) for row in rows], axis=0
        )
        copies = spread(at, 0)
        unsent.extend(copies)
        return copies

    def forward(at):
        copies = spread(at, 1)
        unsent.extend(copies)
        return copies

    def gradients(base, stride):
        values = [u[base + q * stride] for q in range(5)]
        weights = [wr[base + q * stride] for q in range(5)]
        grads = []
        for p in range(5):
            total = float(SLOPES[p, 0]) * values[0]
            for q in range(1, 5):
                total = total + float(SLOPES[p, q]) * values[q]
            grads.append(total * weights[p])
        return grads, weights

    def divergence(grads, q):
        total = float(SLOPES[0, q]) * grads[0]
        for p in range(1, 5):
            total = total + float(SLOPES[p, q]) * grads[p]
        return total

    def along(stride, base_of, first):
        def line(i, carry):
            base = base_of(i)
            grads, weights = gradients(base, stride)
            for q in range(5):
                total = divergence(grads, q)
                at = base + q * stride
                if first:
                    force[at] = jnp.where(in_field, -total, weights[q])
                else:
                    force[at] = force[at] - total
            return carry

        lax.fori_loop(0, 25, line, 0)

    def stiffness():
        along(25, lambda i: i, True)
        along(5, lambda i: (i // 5) * 25 + i % 5, False)
        along(1, lambda i: i * 5, False)

    def join_radial():
        for i in range(25):
            low, high = force[i * 5], force[i * 5 + 4]
            force[i * 5] = low + jnp.where(lanes == 0, 0.0, pltpu.roll(high, 1, 1))
            force[i * 5 + 4] = high + jnp.where(lanes == 127, 0.0, pltpu.roll(low, 127, 1))

    pairs = [(n, 2 * n, min(2 * n + 1, 24)) for n in range(13)]
    not_last, not_first = lat < 3, lat > 0

    def close_pack(base, packed):
        last = jnp.zeros((8, 128), jnp.float32)
        for b in range(5):
            third = force[base + 5 * b + 3]
            for c in range(3):
                packed[3 * b + c] = jnp.where(in_field, force[base + 5 * b + c], pltpu.roll(third, 6 - 2 * c, 0))
            last = jnp.where(lanes == b, jnp.broadcast_to(force[base + 5 * b + 4][:, 127:128], (8, 128)), last)
        packed[15] = last

    def close_add(base, packed):
        last = packed[15]
        for b in range(5):
            parts = [packed[3 * b + c] for c in range(3)]
            third = jnp.where(subs < 2, pltpu.roll(parts[0], 2, 0), pltpu.roll(parts[1], 4, 0))
            third = jnp.where(subs < 4, third, pltpu.roll(parts[2], 6, 0))
            end = jnp.where(lanes == 127, last[:, b : b + 1], pltpu.roll(parts[0], 127, 1))
            for c, part in enumerate(parts + [third, end]):
                at = base + 5 * b + c
                force[at] = force[at] + jnp.where(in_field, part, 0.0)

    def halo_out(step):
        if step == 0:
            faces = [force.at[pl.ds(100, 25)], force.at[pl.ds(0, 25)]]
            into = [lon_lo.at[0], lon_hi.at[0]]
        else:
            close_pack(100, close_up)
            close_pack(0, close_down)
            faces = [close_up, close_down]
            into = [lon_lo.at[step, pl.ds(0, 16)], lon_hi.at[step, pl.ds(0, 16)]]
        lon_copies = [
            send(faces[n], into[n], send_h.at[step, n], recv_h.at[step, n], other)
            for n, other in enumerate((lon_next, lon_prev))
        ]
        for n, one, two in pairs:
            up = [force[25 * (x // 5) + 20 + x % 5] for x in (one, two)]
            down = [force[25 * (x // 5) + x % 5] for x in (one, two)]
            pack_up[n] = jnp.where(even, pltpu.roll(up[1], 7, 0), up[0])
            pack_down[n] = jnp.where(even, down[0], pltpu.roll(down[1], 1, 0))

        def moves(packed, face, beside, edge):
            return [
                pltpu.make_async_remote_copy(
                    src_ref=packed.at[pl.ds(start, count)], dst_ref=dst, send_sem=send_h.at[step, at],
                    recv_sem=recv_h.at[step, at], device_id=other, device_id_type=MESH_ID,
                )
                for start, count, dst, at, other in (
                    (0, 13, face.at[step], 2 + edge, beside),
                    (10, 3, edges.at[step, edge], 4 + edge, corners[edge]),
                    (0, 3, edges.at[step, 2 + edge], 6 + edge, corners[2 + edge]),
                )
            ]

        rising = moves(pack_up, lat_lo, lat_next, 0)
        falling = moves(pack_down, lat_hi, lat_prev, 1)

        @pl.when(not_last)
        def _():
            for copy in rising:
                copy.start()

        @pl.when(not_first)
        def _():
            for copy in falling:
                copy.start()

        return lon_copies, rising, falling

    def halo_in(step, copies):
        lon_copies, rising, falling = copies
        for copy in lon_copies:
            copy.wait()

        @pl.when(not_last)
        def _():
            for copy in rising:
                copy.wait_send()
            for copy in falling:
                copy.wait_recv()

        @pl.when(not_first)
        def _():
            for copy in falling:
                copy.wait_send()
            for copy in rising:
                copy.wait_recv()

        if step == 0:
            force[0:25] = force[0:25] + lon_lo[0]
            force[100:125] = force[100:125] + lon_hi[0]
        else:
            close_add(0, lon_lo.at[step])
            close_add(100, lon_hi.at[step])
        for n, one, two in pairs:
            below, above = lat_lo[step, n], lat_hi[step, n]
            if n <= 2:
                first, second = edges[step, 0, n], edges[step, 1, n]
                if n == 2:
                    first, second = jnp.where(even, 0.0, first), jnp.where(even, second, 0.0)
                below, above = below + first, above + second
            if n >= 10:
                below, above = below + edges[step, 2, n - 10], above + edges[step, 3, n - 10]
            below = jnp.where(not_first, below, 0.0)
            above = jnp.where(not_last, above, 0.0)
            for x, part_below, part_above in (
                (one, pltpu.roll(below, 7, 0), pltpu.roll(above, 1, 0)),
                (two, below, above),
            )[: 1 if one == two else 2]:
                low, high = force[25 * (x // 5) + x % 5], force[25 * (x // 5) + 20 + x % 5]
                force[25 * (x // 5) + x % 5] = low + jnp.where(even, part_below, pltpu.roll(high, 1, 0))
                force[25 * (x // 5) + 20 + x % 5] = high + jnp.where(even, pltpu.roll(low, 7, 0), part_above)

    def node_step(i):
        speed_now = jnp.where(in_field, v[i] + time_step * (force[i] * inv[i]), 0.0)
        v[i] = speed_now
        u[i] = u[i] + time_step * speed_now

    def inside(body):
        def line(t, carry):
            for c in range(5):
                body(25 * (1 + t // 3) + 5 * (1 + t % 3) + c)
            return carry

        lax.fori_loop(0, 9, line, 0)

    def around(body):
        def ends(t, carry):
            for c in range(5):
                body(5 * t + c)
                body(100 + 5 * t + c)
            return carry

        def middle(t, carry):
            for c in range(5):
                body(25 * t + c)
                body(25 * t + 20 + c)
            return carry

        lax.fori_loop(0, 5, ends, 0)
        lax.fori_loop(1, 4, middle, 0)

    def predicted(a, b):
        i = a * 5 + b
        push = (time_step**2 * copies_of(a, b)) * (inv[i * 5] * face_force[i])
        return u[i * 5] + time_step * v[i * 5] + push

    def analysed(at):
        field = g1[at].reshape(8, 4, 16, 128)
        field = jnp.concatenate([field[:, i].reshape(128, 128) for i in range(4)], axis=1)
        sums = jnp.dot(e32[...], field, precision=lax.Precision.HIGHEST, preferred_element_type=jnp.float32)
        result = jnp.zeros((8, 128), jnp.float32)
        for i in range(4):
            part = d32[0:8] * sums[0:8, 128 * i : 128 * i + 128]
            for q in range(1, 4):
                part = part + d32[8 * q : 8 * q + 8] * sums[8 * q : 8 * q + 8, 128 * i : 128 * i + 128]
            part = part + pltpu.roll(part, 64, 1)
            part = part + pltpu.roll(part, 32, 1)
            result = jnp.where(lanes // 32 == i, part, result)
        return result

    def owners(step, sums, offset):
        for j in range(3):
            sums = sums - offset[j] * q8[j]
        found = [jnp.zeros((8, 128), jnp.float32) for k in range(3)]
        for t in range(40):
            block = lp[t]
            for k in range(3):
                lane = (t // 10) * 32 + (2 * k + t // 5 % 2) * 5 + t % 5
                found[k] = found[k] + sums[:, lane : lane + 1] * block
        replies = []
        for k in range(3):
            coefs[step + 2, k] = found[k]
            row = jnp.sum(jnp.where(subs == depth, found[k], 0.0), axis=0, keepdims=True)
            hist[3 * (STEPS - 1 - step) + k : 3 * (STEPS - 1 - step) + k + 1] = row
        for k in range(3):
            reply = past[3 * step + k]
            for i in range(3):
                reply = reply + kern[k, i, 0:1] * found[i]
                for back in range(1, step + 1):
                    reply = reply + kern[k, i, back : back + 1] * coefs[step + 2 - back, i]
            replies.append(reply)
        message = jnp.zeros((8, 128), jnp.float32)
        for t in range(40):
            block = lp[t]
            for k in range(3):
                lane = (t // 10) * 32 + (2 * k + t // 5 % 2) * 5 + t % 5
                value = jnp.sum(block * replies[k], axis=1, keepdims=True)
                message = jnp.where(lanes == lane, value, message)
        pulls = [jnp.sum(message * q8[j], axis=1, keepdims=True) for j in range(3)]
        for j, lane in enumerate((30, 31, 62)):
            message = jnp.where(lanes == lane, pulls[j], message)
        block = g2.at[step, pl.ds(8 * slot_plane, 8), :]
        g2[step, pl.ds(8 * slot_plane, 8), :] = message
        copies = [send(block, block, send2.at[step, d], recv2.at[step, d], other) for d, other in enumerate(plane)]
        unsent.extend(copies)
        return copies

    def rigid_step(step, offset, speed):
        whole = jnp.sum(g2[step], axis=0, keepdims=True)
        lane_row = lax.broadcasted_iota(jnp.int32, (1, 128), 1)
        new_offset, new_speed = [], []
        for j, lane in enumerate((30, 31, 62)):
            pull = jnp.sum(jnp.where(lane_row == lane, whole, 0.0), axis=1, keepdims=True)
            new_speed.append(speed[j] + time_step * rigid_gain * pull)
            new_offset.append(offset[j] + time_step * new_speed[j])
        return new_offset, new_speed

    def add_traction(step, shared_moved=True):
        field = g2[step]
        edge = lanes == 0
        for a in range(5):
            row = jnp.sum(field * gsb[a], axis=0, keepdims=True)
            for b in range(5):
                here = (slant == 32 * lat + b) & in_field
                traction = jnp.sum(jnp.where(here, row, 0.0), axis=1, keepdims=True)
                face = float(coupling * WEIGHTS[a] * WEIGHTS[b]) * copies_of(a, b)
                i = (a * 5 + b) * 5
                gain = jnp.where(edge, time_step * (traction * face) * inv[i], 0.0)
                v[i] = v[i] - gain
                if shared_moved or (0 < a < 4 and 0 < b < 4):
                    u[i] = u[i] - time_step * gain

    def moved(step):
        total = jnp.zeros((8, 128), jnp.float32)
        for q, (start, count) in enumerate(((0, 128), (128, 128), (256, 64))):
            traction = jnp.dot(
                ga[start : start + count], g2[step], precision=lax.Precision.HIGHEST,
                preferred_element_type=jnp.float32,
            )
            total = total + jnp.dot(
                gown[q, :, 0:count], traction * wi[start : start + count], precision=lax.Precision.HIGHEST,
                preferred_element_type=jnp.float32,
            )
        return total

    none = jnp.zeros((2, 128), jnp.float32)

    def stacked(field, i):
        return jnp.concatenate([field[0, i], field[1, i], field[2, i], none], axis=0)

    def by_fives(body):
        def five(t, carry):
            for i in range(5):
                body(5 * t + i)
            return carry

        lax.fori_loop(0, 25, five, 0)

    for copy in loads[0:3]:
        copy.wait()

    def stack_state(i):
        u[i] = stacked(un, i)
        wr[i] = jnp.concatenate([rn[i], rn[i], rn[i], dn[i]], axis=0) * volume[i]

    by_fives(stack_state)
    packed_start = pack(lambda a, b: u[(a * 5 + b) * 5])
    rows = [packed_start[row] * packing[lat, row] for row in range(2)]
    g1[0, pl.ds(2 * mine, 2), :] = jnp.concatenate([jnp.sum(row, axis=0, keepdims=True) for row in rows], axis=0)
    stiffness()
    for i in range(25):
        face_force[i] = force[i * 5]
    join_radial()

    loads[4].wait()
    for step in range(STEPS):
        old = [hist[pl.ds(6 - 3 * step + i, 64, 3), :] for i in range(3)]
        for k in range(3):
            total = sum(kern[k, i] * old[i] for i in range(3))
            past[3 * step + k, pl.ds(depth, 1), :] = jnp.sum(total, axis=0, keepdims=True)

    loads[5].wait()
    base = (me["x"] * 16 + me["ylo"]) * 4 + lat
    own = [order[base + 8 * i] for i in range(8)]
    for i in range(8):
        for q in range(4):
            e32[8 * q + i : 8 * q + i + 1] = cols[own[i], q : q + 1]
            d32[8 * q + i : 8 * q + i + 1] = cols[own[i], 4 + q : 5 + q]
        for q in range(3):
            q8[q, i : i + 1] = cols[own[i], 8 + q : 9 + q]
            gown[q, i : i + 1] = cols[own[i], 11 + q : 12 + q]

    def circle_rows(t, carry):
        for i in range(8):
            column = order[((t // 8) * 16 + i * 2 + t // 4 % 2) * 4 + t % 4]
            for q in range(3):
                gtt[q, pl.ds(8 * t + i, 1), :] = cols[column, 11 + q : 12 + q]
        return carry

    lax.fori_loop(0, 32, circle_rows, 0)
    loads[6].wait()

    def take(t, carry):
        for i in range(8):
            lp[t, i : i + 1] = leg[lax.rem(own[i], 128), pl.ds(t, 1), :]
        return carry

    lax.fori_loop(0, 40, take, 0)
    many = lax.broadcasted_iota(jnp.int32, (256, 128), 1)
    elem = (me["x"] * 2 + me["ylo"]) * 8 + depth
    for a in range(5):
        picked = jnp.where(many == elem + 64 * (a % 2), gtt[a // 2], 0.0)
        gsb[a] = jnp.broadcast_to(jnp.sum(picked, axis=1, keepdims=True), (256, 128))
    for q in range(3):
        ga[128 * q : 128 * q + 128] = jnp.transpose(gtt[q])
    loads[3].wait()

    def stack_speed(i):
        v[i] = stacked(vn, i)

    by_fives(stack_speed)
    offset = [jnp.full((1, 1), x_in[j], jnp.float32) for j in range(3)]
    speed = [jnp.full((1, 1), xv_in[j], jnp.float32) for j in range(3)]

    pl.semaphore_wait(barrier, len(everyone))
    wave0 = spread(0, 0)
    halo = halo_out(0)
    own_past = past.at[:, pl.ds(depth, 1), :]
    wave_past = [
        send(own_past, own_past, send_p.at[d], recv_p.at[d], other) for d, other in enumerate(column_mates)
    ]
    unsent.extend(wave0)
    unsent.extend(wave_past)
    stores = [pltpu.make_async_copy(hist.at[pl.ds(9, 180), :], hist_out.at[pl.ds(9, 180), 0, :], store_sem.at[2])]
    stores[0].start()

    arrived(wave0)
    wave0 = forward(0)
    halo_in(0, halo)

    def invert(i):
        mass = force[i]
        inv[i] = 1.0 / jnp.where(even, mass[6:7], mass[7:8])

    def invert_column(i, carry):
        for b in range(5):
            invert(25 * i + 5 * b)
        return carry

    lax.fori_loop(0, 5, invert_column, 0)
    tail = pack(lambda a, b: inv[(a * 5 + b) * 5], 32)[0] * packing[lat, 2]
    wave1 = post(1, predicted, tail)
    arrived(wave_past)
    by_fives(invert)
    arrived(wave0)
    replies0 = owners(0, analysed(0), offset)
    arrived(wave1)
    wave1 = forward(1)
    by_fives(node_step)
    arrived(replies0)
    add_traction(0)
    offset, speed = rigid_step(0, offset, speed)

    stiffness()
    for i in range(25):
        face_force[i] = force[i * 5]
    join_radial()
    halo = halo_out(1)
    wave2 = post(2, predicted)
    arrived(wave1)
    factors = g1[1, pl.ds(1, 256, 2), :].reshape(8, 4, 8, 128)
    wide = lax.broadcasted_iota(jnp.int32, (64, 128), 1)
    for a in range(5):
        total = jnp.zeros((64, 128), jnp.float32)
        for i in range(4):
            block = factors[:, i].reshape(64, 128)
            for k in range(3):
                start = 32 * i + 10 * k
                turned = pltpu.roll(block, (start - 32 - 10 * a) % 128, 1)
                total = jnp.where((wide >= start) & (wide < start + 10), turned, total)
        wi[64 * a : 64 * a + 64] = total
    replies1 = owners(1, analysed(1) - moved(0), offset)
    arrived(wave2)
    wave2 = forward(2)
    inside(node_step)
    halo_in(1, halo)
    around(node_step)
    arrived(replies1)
    add_traction(1)
    offset, speed = rigid_step(1, offset, speed)

    stiffness()
    join_radial()
    halo = halo_out(2)
    shift = moved(1)
    arrived(wave2)
    replies2 = owners(2, analysed(2) - shift, offset)
    inside(node_step)
    arrived(replies2)
    add_traction(2, shared_moved=False)
    offset, speed = rigid_step(2, offset, speed)

    def unstack(i):
        place, speed_now = u[i], v[i]
        for k in range(3):
            un[k, i] = place[2 * k : 2 * k + 2]
            vn[k, i] = speed_now[2 * k : 2 * k + 2]

    inside(unstack)
    halo_in(2, halo)

    def last_step(i):
        node_step(i)
        unstack(i)

    around(last_step)
    stores.append(pltpu.make_async_copy(hist.at[pl.ds(0, 9), :], hist_out.at[pl.ds(0, 9), 0, :], store_sem.at[3]))
    stores[1].start()
    for n, (src, dst) in enumerate(((un, u_out), (vn, v_out))):
        copy = pltpu.make_async_copy(src, dst, store_sem.at[n])
        copy.start()
        stores.append(copy)
    for j in range(3):
        rigid_out[j : j + 1] = jnp.broadcast_to(offset[j], (1, 128))
        rigid_out[3 + j : 4 + j] = jnp.broadcast_to(speed[j], (1, 128))
    rigid_out[6:8] = jnp.zeros((2, 128), jnp.float32)
    for copy in unsent:
        copy.wait_send()
    for copy in stores:
        copy.wait()


def hand_over(u_in, v_in, hist_in, rigid_in, u_out, v_out, hist_out, x_out, xv_out, u, v, hist, sems):
    held = ((u_in, u, u_out), (v_in, v, v_out), (hist_in, hist, hist_out))
    arriving = [pltpu.make_async_copy(src, mid, sems.at[n]) for n, (src, mid, dst) in enumerate(held)]
    leaving = [pltpu.make_async_copy(mid, dst, sems.at[3 + n]) for n, (src, mid, dst) in enumerate(held)]
    for copy in arriving:
        copy.start()
    for j in range(3):
        x_out[j] = rigid_in[j, 0]
        xv_out[j] = rigid_in[3 + j, 0]
    for first, second in zip(arriving, leaving):
        first.wait()
        second.start()
    for copy in leaving:
        copy.wait()


def on_device(
    displacement, velocity, rigidity, density, history, kernel, owner_order, rigid_offset, rigid_velocity
):
    volume = (WEIGHTS[:, None, None] * WEIGHTS[:, None] * WEIGHTS).reshape(125).astype(np.float32)
    vmem = pl.BlockSpec(memory_space=pltpu.VMEM)
    smem = pl.BlockSpec(memory_space=pltpu.SMEM)
    hbm = pl.BlockSpec(memory_space=pl.ANY)
    sds = functools.partial(jax.ShapeDtypeStruct, dtype=jnp.float32)
    state = (125, 8, 128)
    sem = pltpu.SemaphoreType.DMA
    new_u, new_v, new_history, rigid = pl.pallas_call(
        on_sphere,
        out_shape=(sds((3, 125, 2, 128)), sds((3, 125, 2, 128)), sds((189, 1, 128)), sds((8, 128))),
        in_specs=[hbm] * 4 + [smem, hbm, vmem, hbm, hbm, vmem] + [smem] * 3,
        out_specs=(hbm, hbm, hbm, vmem),
        scratch_shapes=[
            pltpu.VMEM(shape, jnp.float32)
            for shape in (
                (3, 125, 2, 128), (3, 125, 2, 128), (125, 2, 128), (125, 2, 128),
                state, state, state, state, state, (25, 8, 128), (200, 128),
                (128, 40, 128), (256, 16, 128), (40, 8, 128), (32, 128), (32, 128), (3, 8, 128), (3, 8, 128),
                (3, 256, 128), (384, 256), (5, 256, 128), (320, 128), (9, 8, 128), (STEPS + 2, 3, 8, 128),
                (STEPS, 512, 128), (STEPS, 256, 128),
            )
            + ((STEPS, 25, 8, 128),) * 2
            + ((STEPS, 13, 8, 128),) * 2
            + ((STEPS, 4, 3, 8, 128), (13, 8, 128), (13, 8, 128), (16, 8, 128), (16, 8, 128))
        ]
        + [
            sem((7,)), sem((4,)), sem((STEPS, 2, GROUP - 1)), sem((STEPS, 2, GROUP - 1)),
            sem((STEPS, 31)), sem((STEPS, 31)), sem((7,)), sem((7,)), sem((STEPS, 8)), sem((STEPS, 8)),
        ],
        compiler_params=pltpu.CompilerParams(
            collective_id=0, has_side_effects=True, vmem_limit_bytes=VMEM_BYTES
        ),
    )(
        displacement.reshape(3, 125, 2, 128), velocity.reshape(3, 125, 2, 128),
        rigidity.reshape(125, 2, 128), density.reshape(125, 2, 128), jnp.asarray(volume),
        history.transpose(1, 2, 0, 3).reshape(189, 1, 128), kernel.transpose(1, 2, 0, 3), jnp.asarray(legendre_table()), jnp.asarray(column_tables()),
        jnp.asarray(packed_tables()), owner_order, rigid_offset, rigid_velocity,
    )
    new_u, new_v, new_history, new_offset, new_speed = pl.pallas_call(
        hand_over,
        out_shape=(sds((3, 125, 2, 128)), sds((3, 125, 2, 128)), sds((189, 1, 128)), sds((3,)), sds((3,))),
        in_specs=[hbm, hbm, hbm, smem],
        out_specs=(hbm, hbm, hbm, smem, smem),
        scratch_shapes=[pltpu.VMEM(shape, jnp.float32) for shape in ((3, 125, 2, 128), (3, 125, 2, 128), (189, 1, 128))]
        + [sem((6,))],
        compiler_params=pltpu.CompilerParams(vmem_limit_bytes=VMEM_BYTES),
    )(new_u, new_v, new_history, rigid)
    shape = displacement.shape
    new_history = new_history.reshape(63, 3, 1, 128).transpose(2, 0, 1, 3)
    return new_u.reshape(shape), new_v.reshape(shape), new_history, new_offset, new_speed


def solution(mesh):
    split = Mesh(mesh.devices.reshape(4, 8, 2, 2, 2), AXES)
    field = P(None, None, None, None, BLK, LAT, None)
    scalar_field = P(None, None, None, BLK, LAT, None)
    owned = P(AXES, None, None, None)
    return jax.shard_map(
        on_device,
        mesh=split,
        in_specs=(field, field, scalar_field, scalar_field, owned, P(), P(), P(), P()),
        out_specs=(field, field, owned, P(), P()),
        check_vma=False,
    )
```
